32 devices in a mesh: dp: 2 (over x), row: 4 (over z), col: 4 (over y, core).
Axes of the slice: x: 2, y: 2, z: 4, core: 2. Of those that a mesh axis runs over, the one named last changes fastest.
Arguments:
- layer_input: bfloat16 [6144, 2048], P(('dp', 'col'), 'row'), may hold values from -16 to 16
- gains: bfloat16 [4, 2048], replicated, may hold values from 0.25 to 1.75
- qkv_weight: bfloat16 [2048, 3, 2048], P('row', None, 'col'), may hold values from -0.125 to 0.125
- output_weight: bfloat16 [2048, 2048], P('col', 'row'), may hold values from -2 to 2
- router_weight: bfloat16 [2048, 32], replicated, may hold values from -0.0625 to 0.0625
- expand_weight: bfloat16 [32, 2048, 2048], P(('row', 'col')), may hold values from -0.125 to 0.125
- reduce_weight: bfloat16 [32, 1024, 2048], P(('row', 'col')), may hold values from -3 to 3
- routes: int32 [6144, 8], P(('dp', 'col')), may hold values from 0 to 31, all different within a row
- drop_order: int32 [6144], P(('dp', 'col')), may hold values from 0 to 3071
- prefix_len: int32 [2], P('dp'), may hold values from 307 to 1536
- cotangent: bfloat16 [6144, 2048], P(('dp', 'col'), 'row'), may hold values from -6 to 6
Outputs:
- layer_output: bfloat16 [6144, 2048], P(('dp', 'col'), 'row')
- input_grad: bfloat16 [6144, 2048], P(('dp', 'col'), 'row')
- gains_grad: float32 [4, 2048], replicated
- qkv_grad: float32 [4, 512, 3, 2048], P('row', 'dp', None, 'col')
- output_grad: float32 [4, 512, 2048], P('col', 'dp', 'row')
- router_grad: float32 [2048, 32], replicated
- expand_grad: float32 [32, 2048, 2048], P(('row', 'col'), 'dp')
- reduce_grad: float32 [32, 1024, 2048], P(('row', 'col'), 'dp')
The draws below stay inside these ranges and needn't reach their ends.
Inputs may be any that keep to these rules, and one draw needn't show every extreme that they name: `routes`: each row names 8 different experts.
All inputs are finite; a program needn't handle non-finite values.
Results may differ from the reference program's by a relative error of at most 0.02.
The reference program's roundings to bfloat16 on the way count: a program that leaves them out, or rounds other values in their place, can miss the bound.
Values may be sent and summed in bfloat16 or wider, within the bound.
No kernel may reach another device: no remote copies, remote signals or barrier semaphores. Data moves between devices by JAX's collectives and lax.ppermute only.
A program may use at most 320 MiB of HBM per device.

```python
import jax
import jax.numpy as jnp
from jax import lax

D = 2048
HEADS = 16
HD = 128
F = 1024
TOP = 8
TOK_DEV = 192
QBLK = 768
EXPERTS = 32
SEQ = 3072
SEQS = 2
TOKENS = 6144
N_ROW = 4
N_COL = 4


def draw_layer_input(key, part):
    key = jax.random.fold_in(key, 11)
    row_key, col_key, value_key = jax.random.split(key, 3)
    row_scale = jnp.exp(jax.random.uniform(row_key, (TOKENS, 1), minval=-0.8, maxval=0.8))
    col_scale = 2.0 ** (jnp.arange(D, dtype=jnp.float32)[None, :] / D) * jnp.exp(jax.random.uniform(col_key, (1, D), minval=-0.4, maxval=0.4))
    values = jnp.clip(jax.random.normal(value_key, (TOKENS, D)), -4.0, 4.0)
    return (values * row_scale * col_scale * 0.45).astype(jnp.bfloat16)


def touch_ends(result, rng, low, high):
    index_at = [jax.random.randint(jax.random.fold_in(rng, axis), (), 0, length) for axis, length in enumerate(result.shape)]
    widest = result.shape.index(max(result.shape))
    next_to = index_at[:widest] + [(index_at[widest] + 1) % result.shape[widest]] + index_at[widest + 1:]
    return result.at[tuple(index_at)].set(low).at[tuple(next_to)].set(high)


def shard_levels(own_key, extent, cuts, smallest, high):
    loudness = 1.0
    for axis_at, blocks in cuts:
        heights = jax.random.uniform(jax.random.fold_in(jax.random.fold_in(own_key, 6), axis_at), (blocks,), jnp.float32, smallest / len(cuts), high / len(cuts))
        loudness = loudness * jnp.repeat(jnp.exp(heights), extent[axis_at] // blocks).reshape((-1,) + (1,) * (len(extent) - 1 - axis_at))
    return loudness


def distinct(stream_key, rows, count, top, lift):
    ranking = jax.random.permutation(jax.random.fold_in(stream_key, 1), count)
    favour = ranking
    for power in range(3):
        favour = favour * favour // count
    favour = favour * lift // count
    chance = jax.random.randint(jax.random.fold_in(stream_key, 2), (rows, count), 0, 4096) + favour
    fixed_rows = jax.random.permutation(jax.random.fold_in(stream_key, 3), rows)[jnp.arange(count) % rows]
    chance = jnp.where(jnp.arange(rows)[:, None] == fixed_rows[None, :], 1 << 14, chance)
    merit = chance * count + jnp.arange(count)
    return lax.top_k(merit.astype(jnp.int32), top)[1].astype(jnp.int32)


def noise(stream_key, extent, spread, most, cuts=(), kind=jnp.bfloat16):
    result = spread * jax.random.normal(stream_key, extent, jnp.float32)
    if cuts:
        result = result * shard_levels(stream_key, extent, cuts, -0.22, 0.18)
    return jnp.clip(result, -most, most).astype(kind)


def setup_inputs(seed: int = 0) -> dict:
    splits = jax.random.split(jax.random.key(seed), 12)
    layer_input = draw_layer_input(jax.random.fold_in(splits[11], 71), 0)
    gains = jnp.clip(1.0 + 0.15 * jax.random.normal(splits[1], (4, D), jnp.float32), 0.25, 1.75).astype(jnp.bfloat16)
    qkv_weight = noise(splits[2], (D, 3, D), D ** -0.5, 0.125, ((0, 4), (2, 4)))
    output_weight = noise(splits[3], (D, D), (max(D // 256, 2)) ** -0.5, 2.0, ((0, 4), (1, 4)))
    router_weight = noise(splits[4], (D, EXPERTS), (4 * D) ** -0.5, 0.0625)
    expand_weight = noise(splits[5], (EXPERTS, D, 2 * F), D ** -0.5, 0.125, ((0, 16),))
    reduce_weight = noise(splits[6], (EXPERTS, F, D), (max(F // 256, 2)) ** -0.5, 3.0, ((0, 16),))
    routes = distinct(splits[7], TOKENS, EXPERTS, TOP, 2048)
    drop_order = touch_ends(jax.random.randint(splits[8], (TOKENS,), 0, TOK_DEV * 16), jax.random.fold_in(splits[8], 1), 0, (TOK_DEV * 16) - 1).astype(jnp.int32)
    prefix_len = jax.random.randint(splits[9], (SEQS,), SEQ // 10, SEQ // 2 + 1).astype(jnp.int32)
    cotangent = noise(splits[10], (TOKENS, D), 1.0, 6.0, ((0, 8), (1, 4)))
    return {"layer_input": layer_input, "gains": gains, "qkv_weight": qkv_weight, "output_weight": output_weight, "router_weight": router_weight, "expand_weight": expand_weight, "reduce_weight": reduce_weight, "routes": routes, "drop_order": drop_order, "prefix_len": prefix_len, "cotangent": cotangent}


norm_epsilon = 1e-05
rope_base = 10000.0
highest = lax.Precision.HIGHEST

@jax.custom_vjp
def low(v):
    return lax.optimization_barrier(v.astype(jnp.bfloat16)).astype(jnp.float32)

@jax.custom_vjp
def low_back(v):
    return v

def low_keep(v):
    return (low(v), None)

def low_pass(kept, grad):
    return (grad,)

def back_keep(v):
    return (v, None)

def back_low(kept, grad):
    return (low(grad),)
low.defvjp(low_keep, low_pass)
low_back.defvjp(back_keep, back_low)

def root_norm(values, gain_row):
    return values * lax.rsqrt(lax.optimization_barrier(jnp.mean(values * values, axis=-1, keepdims=True)) + norm_epsilon) * gain_row

def rope_tables(positions):
    half_width = HD // 2
    frequency = rope_base ** (-2.0 * jnp.arange(half_width, dtype=jnp.float32) / HD)
    angles = positions.astype(jnp.float32)[:, None] * frequency[None, :]
    return (jnp.cos(angles)[:, None, :], jnp.sin(angles)[:, None, :])

def rotate(values, cosine, sine_part):
    half_width = values.shape[-1] // 2
    first_half = values[..., :half_width]
    second_half = values[..., half_width:]
    return jnp.concatenate([first_half * cosine - second_half * sine_part, second_half * cosine + first_half * sine_part], axis=-1)

def attention(query_rot, key_rot, value_heads, prefix_len):
    seq_count = query_rot.shape[0] // SEQ
    score_scale = HD ** (-0.5)
    key_pos = jnp.arange(SEQ)

    def one_sequence(packed):
        query_seq, key_seq, value_seq, prefix = packed

        def one_block(block_start):
            query_block = lax.dynamic_slice_in_dim(query_seq, block_start, QBLK, 0)
            scores = low_back(jnp.einsum('qhd,khd->hqk', query_block, key_seq, precision=highest) * score_scale)
            query_pos = block_start + jnp.arange(QBLK)
            allowed = (key_pos[None, :] <= query_pos[:, None]) | (key_pos[None, :] < prefix)
            scores = jnp.where(allowed[None], scores, -1e+30)
            peak = lax.optimization_barrier(jnp.max(scores, axis=-1, keepdims=True))
            log_total = peak + jnp.log(lax.optimization_barrier(jnp.sum(jnp.exp(scores - peak), axis=-1, keepdims=True)))
            weights = low(jnp.exp(scores - log_total))
            return jnp.einsum('hqk,khd->qhd', weights, value_seq, precision=highest)
        block_starts = jnp.arange(SEQ // QBLK) * QBLK
        mixed_heads = lax.map(jax.checkpoint(one_block), block_starts)
        return mixed_heads.reshape(SEQ, HEADS, HD)
    shaped = (query_rot.reshape(seq_count, SEQ, HEADS, HD), key_rot.reshape(seq_count, SEQ, HEADS, HD), value_heads.reshape(seq_count, SEQ, HEADS, HD), prefix_len)
    return lax.map(one_sequence, shaped).reshape(seq_count * SEQ, HEADS, HD)

def experts_layer(features, router_weight, expand_weight, reduce_weight, routes, drop_order):
    token_count = features.shape[0]
    block_count = token_count // TOK_DEV
    capacity = TOK_DEV * TOP // EXPERTS
    slot_count = EXPERTS * capacity
    logits = low_back(jnp.dot(features, router_weight, precision=highest))
    router_probs = jax.nn.softmax(logits, axis=-1).reshape(block_count, TOK_DEV, EXPERTS)
    own_routes = routes.reshape(block_count, TOK_DEV, TOP)
    drop_rank = drop_order.reshape(block_count, TOK_DEV)
    chosen = (own_routes[..., None] == jnp.arange(EXPERTS)).astype(jnp.float32)
    gate_vals = lax.optimization_barrier(jnp.sum(chosen * router_probs[:, :, None, :], axis=-1))
    token_index = jnp.arange(TOK_DEV)
    earlier = (drop_rank[:, None, :] < drop_rank[:, :, None]) | (drop_rank[:, None, :] == drop_rank[:, :, None]) & (token_index[None, None, :] < token_index[None, :, None])
    counts = jnp.einsum('bts,bse->bte', earlier.astype(jnp.float32), lax.optimization_barrier(jnp.sum(chosen, axis=2)), precision=highest)
    position = lax.optimization_barrier(jnp.sum(chosen * counts[:, :, None, :], axis=-1)).astype(jnp.int32)
    kept_mask = position < capacity
    slot_index = own_routes * capacity + position
    slot_ids = jnp.arange(slot_count)
    dispatch = jnp.zeros((block_count, TOK_DEV, slot_count), jnp.float32)
    combine = jnp.zeros((block_count, TOK_DEV, slot_count), jnp.float32)
    for pick_index in range(TOP):
        hit_mask = (slot_index[:, :, pick_index, None] == slot_ids) & kept_mask[:, :, pick_index, None]
        dispatch = dispatch + hit_mask.astype(jnp.float32)
        combine = combine + jnp.where(hit_mask, gate_vals[:, :, pick_index, None], 0.0)
    feature_blocks = features.reshape(block_count, TOK_DEV, D)
    slots = low_back(jnp.einsum('bts,btd->bsd', dispatch, feature_blocks, precision=highest))
    expert_slots = jnp.swapaxes(slots.reshape(block_count, EXPERTS, capacity, D), 0, 1)

    def one_expert(packed):
        slot_rows, weight_in, weight_down = packed
        gate_up = jnp.einsum('bcd,df->bcf', slot_rows, weight_in, precision=highest)
        gate_pre = low_back(gate_up[..., :F])
        up_pre = low_back(gate_up[..., F:])
        hidden = low(jax.nn.silu(gate_pre) * up_pre)
        return low_back(low(jnp.einsum('bcf,fd->bcd', hidden, weight_down, precision=highest)))
    expert_out = lax.map(one_expert, (expert_slots, expand_weight, reduce_weight))
    expert_out = jnp.swapaxes(expert_out, 0, 1).reshape(block_count, slot_count, D)
    return jnp.einsum('bts,bsd->btd', combine, expert_out, precision=highest).reshape(token_count, D)

def forward(inputs, gain_rows, qkv_weight, output_weight, router_weight, expand_weight, reduce_weight, routes, drop_order, prefix_len):
    token_count = inputs.shape[0]
    normed_first = low(root_norm(inputs, gain_rows[0]))
    projected = jnp.einsum('td,djc->jtc', normed_first, qkv_weight, precision=highest)
    query_raw = low_back(projected[0])
    key_raw = low_back(projected[1])
    value_low = low(low_back(projected[2]))
    positions = jnp.tile(jnp.arange(SEQ), token_count // SEQ)
    cosine, sine_part = rope_tables(positions)
    head_shape = (token_count, HEADS, HD)
    query_rot = low(rotate(root_norm(query_raw, gain_rows[1]).reshape(head_shape), cosine, sine_part))
    key_rot = low(rotate(root_norm(key_raw, gain_rows[2]).reshape(head_shape), cosine, sine_part))
    mixed_heads = attention(query_rot, key_rot, value_low.reshape(head_shape), prefix_len)
    attn_low = low_back(low(mixed_heads.reshape(token_count, D)))
    branch = low_back(jnp.dot(attn_low, output_weight, precision=highest))
    residual = inputs + branch
    normed_second = low(root_norm(residual, gain_rows[3]))
    experts_sum = experts_layer(normed_second, router_weight, expand_weight, reduce_weight, routes, drop_order)
    return residual + low_back(experts_sum)

def reference(layer_input, gains, qkv_weight, output_weight, router_weight, expand_weight, reduce_weight, routes, drop_order, prefix_len, cotangent):

    def layer(inputs, gain_rows, weight_qkv, weight_output, weight_router, weight_expand, weight_reduce):
        return forward(inputs, gain_rows, weight_qkv, weight_output, weight_router, weight_expand, weight_reduce, routes, drop_order, prefix_len)
    layer_out, pullback = jax.vjp(layer, layer_input.astype(jnp.float32), gains.astype(jnp.float32), qkv_weight.astype(jnp.float32), output_weight.astype(jnp.float32), router_weight.astype(jnp.float32), expand_weight.astype(jnp.float32), reduce_weight.astype(jnp.float32))
    gradients = pullback(cotangent.astype(jnp.float32))
    return (layer_out.astype(jnp.bfloat16), gradients[0].astype(jnp.bfloat16), gradients[1], gradients[2].reshape(N_ROW, D // N_ROW, 3, D), gradients[3].reshape(N_COL, D // N_COL, D), gradients[4], gradients[5], gradients[6])
```

```python
import functools
import math

import jax
import jax.numpy as jnp
from jax import lax
from jax.experimental import pallas as pl
from jax.experimental.pallas import tpu as pltpu
from jax.sharding import PartitionSpec as P

D = 2048
HD = 128
F = 1024
TOP = 8
CORES = 2
PLANE = ("row", "col")
BLOCKS = ("col", "row")
LOG2E = math.log2(math.e)
MASKED = -1e30

norm_epsilon = 1e-05
rope_base = 10000.0
bf16 = jnp.bfloat16
f32 = jnp.float32


def dot_nt(a, b):
    return lax.dot_general(a, b, (((1,), (1,)), ((), ())), preferred_element_type=f32)


def dot_nn(a, b):
    return lax.dot_general(a, b, (((1,), (0,)), ((), ())), preferred_element_type=f32)


def key_limits(first_query, query_rows, key_rows, prefix):
    open_blocks = jnp.maximum((first_query + 1) // key_rows, prefix // key_rows)
    all_blocks = pl.cdiv(jnp.maximum(first_query + query_rows, prefix), key_rows)
    return open_blocks, all_blocks


def mask_scores(scores, first_key, first_query, prefix):
    keys = first_key + lax.broadcasted_iota(jnp.int32, scores.shape, 0)
    queries = first_query + lax.broadcasted_iota(jnp.int32, scores.shape, 1)
    return jnp.where((keys <= queries) | (keys < prefix), scores, MASKED)


def attention_kernel(scale, prefix_ref, q_ref, k_ref, v_flip_ref, out_ref, lse_ref, scores_ref):
    query_rows = q_ref.shape[0]
    key_rows = min(512, k_ref.shape[0])
    first_query = pl.program_id(0) * query_rows
    prefix = prefix_ref[0]
    q = q_ref[...]
    open_blocks, all_blocks = key_limits(first_query, query_rows, key_rows, prefix)

    def score(j, top, masked):
        start = pl.multiple_of(j * key_rows, key_rows)
        scores = dot_nt(k_ref[pl.ds(start, key_rows), :], q) * (scale * LOG2E)
        if masked:
            scores = mask_scores(scores, start, first_query, prefix)
        scores_ref[pl.ds(start, key_rows), :] = scores
        return jnp.maximum(top, jnp.max(scores.reshape(key_rows // 8, 8, query_rows), axis=0))

    top = jnp.full((8, query_rows), MASKED, f32)
    top = lax.fori_loop(0, open_blocks, lambda j, t: score(j, t, False), top)
    top = lax.fori_loop(open_blocks, all_blocks, lambda j, t: score(j, t, True), top)
    peak = jnp.max(top, axis=0, keepdims=True)

    def mix(j, carry):
        total, mixed = carry
        start = pl.multiple_of(j * key_rows, key_rows)
        weights = jnp.exp2(scores_ref[pl.ds(start, key_rows), :] - peak)
        total = total + jnp.sum(weights.reshape(key_rows // 8, 8, query_rows), axis=0)
        mixed = mixed + dot_nn(v_flip_ref[:, pl.ds(start, key_rows)], weights.astype(bf16))
        return total, mixed

    total, mixed = lax.fori_loop(
        0,
        all_blocks,
        mix,
        (jnp.zeros((8, query_rows), f32), jnp.zeros((q.shape[1], query_rows), f32)),
    )
    total = jnp.sum(total, axis=0, keepdims=True)
    out_ref[...] = (mixed / total).T.astype(out_ref.dtype)
    lse_ref[...] = peak + jnp.log2(total)


def attention(q, k, v, prefix_len, query_rows):
    length, width = q.shape
    query_block = pl.BlockSpec((query_rows, width), lambda i, p: (i, 0))
    return pl.pallas_call(
        functools.partial(attention_kernel, width**-0.5),
        grid_spec=pltpu.PrefetchScalarGridSpec(
            num_scalar_prefetch=1,
            grid=(length // query_rows,),
            in_specs=[
                query_block,
                pl.BlockSpec((length, width), lambda i, p: (0, 0)),
                pl.BlockSpec((width, length), lambda i, p: (0, 0)),
            ],
            out_specs=[query_block, pl.BlockSpec((1, query_rows), lambda i, p: (0, i))],
            scratch_shapes=[pltpu.VMEM((length, query_rows), f32)],
        ),
        out_shape=[
            jax.ShapeDtypeStruct((length, width), bf16),
            jax.ShapeDtypeStruct((1, length), f32),
        ],
        compiler_params=pltpu.CompilerParams(vmem_limit_bytes=40 * 2**20),
        cost_estimate=pl.CostEstimate(
            flops=2 * length * length * width, bytes_accessed=10 * length * width,
            transcendentals=length * length // 2,
        ),
        name="attention_forward",
    )(prefix_len, q, k, v.T)


def attention_back_kernel(
    scale, prefix_ref, q_ref, grad_ref, lse_ref, centre_ref, k_ref, k_flip_ref, v_ref,
    grad_q_ref, grad_k_ref, grad_v_ref,
):
    query_rows = q_ref.shape[0]
    key_rows = min(512, k_ref.shape[0])
    step = pl.program_id(0)
    first_query = step * query_rows
    prefix = prefix_ref[0]

    @pl.when(step == 0)
    def _():
        grad_k_ref[...] = jnp.zeros_like(grad_k_ref)
        grad_v_ref[...] = jnp.zeros_like(grad_v_ref)

    q = q_ref[...]
    grad = grad_ref[...]
    lse = lse_ref[...]
    centre = centre_ref[...]
    open_blocks, all_blocks = key_limits(first_query, query_rows, key_rows, prefix)

    def block(j, total, masked):
        start = pl.multiple_of(j * key_rows, key_rows)
        rows = pl.ds(start, key_rows)
        scores = dot_nt(k_ref[rows, :], q) * (scale * LOG2E) - lse
        if masked:
            scores = mask_scores(scores, start, first_query, prefix)
        weights = jnp.exp2(scores)
        grad_weights = dot_nt(v_ref[rows, :], grad)
        grad_scores = (weights * (grad_weights - centre)).astype(bf16)
        grad_v_ref[rows, :] += dot_nn(weights.astype(bf16), grad)
        grad_k_ref[rows, :] += dot_nn(grad_scores, q)
        return total + dot_nn(k_flip_ref[:, rows], grad_scores)

    total = jnp.zeros((q.shape[1], query_rows), f32)
    total = lax.fori_loop(0, open_blocks, lambda j, a: block(j, a, False), total)
    total = lax.fori_loop(open_blocks, all_blocks, lambda j, a: block(j, a, True), total)
    grad_q_ref[...] = total.T * scale

    @pl.when(step == pl.num_programs(0) - 1)
    def _():
        grad_k_ref[...] = grad_k_ref[...] * scale


def attention_back(q, k, v, grad, lse, centre, prefix_len, query_rows):
    length, width = q.shape
    whole = pl.BlockSpec((length, width), lambda i, p: (0, 0))
    flipped = pl.BlockSpec((width, length), lambda i, p: (0, 0))
    query_block = pl.BlockSpec((query_rows, width), lambda i, p: (i, 0))
    query_row = pl.BlockSpec((1, query_rows), lambda i, p: (0, i))
    result = jax.ShapeDtypeStruct((length, width), f32)
    return pl.pallas_call(
        functools.partial(attention_back_kernel, width**-0.5),
        grid_spec=pltpu.PrefetchScalarGridSpec(
            num_scalar_prefetch=1,
            grid=(length // query_rows,),
            in_specs=[query_block, query_block, query_row, query_row, whole, flipped, whole],
            out_specs=[query_block, whole, whole],
        ),
        out_shape=[result, result, result],
        compiler_params=pltpu.CompilerParams(vmem_limit_bytes=40 * 2**20),
        cost_estimate=pl.CostEstimate(
            flops=5 * length * length * width, bytes_accessed=22 * length * width,
            transcendentals=length * length // 2,
        ),
        name="attention_backward",
    )(prefix_len, q, grad, lse, centre, k, k.T, v)


class Ring:
    def __init__(self, rows, cols):
        self.rows, self.cols = rows, cols
        self.cores = CORES if cols % CORES == 0 else 1
        self.groups = cols // self.cores
        self.order = [
            (row, group)
            for group in range(self.groups)
            for row in (range(rows) if group % 2 == 0 else range(rows - 1, -1, -1))
        ]
        self.size = len(self.order)
        self.clockwise = self.shift(1)
        self.counter = self.shift(-1)
        self.sibling = [
            (row * cols + col, row * cols + col - col % self.cores + (col + 1) % self.cores)
            for row in range(rows)
            for col in range(cols)
        ]
        row, col = lax.axis_index("row"), lax.axis_index("col")
        group = col // self.cores
        self.core = col % self.cores
        self.place = group * rows + jnp.where(group % 2 == 0, row, rows - 1 - row)

    def shift(self, step):
        pairs = []
        for at, (row, group) in enumerate(self.order):
            to_row, to_group = self.order[(at + step) % self.size]
            for core in range(self.cores):
                pairs.append(
                    (
                        row * self.cols + group * self.cores + core,
                        to_row * self.cols + to_group * self.cores + core,
                    )
                )
        return pairs

    def chip(self, distance):
        at = (self.place + distance + self.size) % self.size
        group = at // self.rows
        along = at % self.rows
        return jnp.where(group % 2 == 0, along, self.rows - 1 - along), group

    def owners(self, distance):
        row, group = self.chip(distance)
        return [(row, group * self.cores + (self.core + k) % self.cores) for k in range(self.cores)]

    def gather(self, block, put):
        def arrived(piece, distance):
            for k, (row, col) in enumerate(self.owners(distance)):
                put(lax.ppermute(piece, PLANE, self.sibling) if k else piece, row, col)

        forth = back = block
        arrived(block, 0)
        for step in range(1, (self.size + 1) // 2):
            forth = lax.ppermute(forth, PLANE, self.clockwise)
            back = lax.ppermute(back, PLANE, self.counter)
            arrived(forth, -step)
            arrived(back, step)
        if self.size % 2 == 0:
            half = block.shape[0] // 2
            forth = lax.ppermute(forth[:half], PLANE, self.clockwise)
            back = lax.ppermute(back[half:], PLANE, self.counter)
            arrived(jnp.concatenate([forth, back], axis=0), self.size // 2)

    def scatter_sum(self, get):
        def add(one, two):
            return (one.astype(f32) + two.astype(f32)).astype(bf16)

        def chip_sum(distance):
            mine, *others = [get(row, col) for row, col in self.owners(distance)]
            for other in others:
                mine = add(mine, lax.ppermute(other, PLANE, self.sibling))
            return mine

        forth = back = None
        half = 0
        if self.size % 2 == 0:
            far = chip_sum(self.size // 2)
            half = far.shape[0] // 2
            forth = lax.ppermute(far[:half], PLANE, self.clockwise)
            back = lax.ppermute(far[half:], PLANE, self.counter)
        for step in range((self.size - 1) // 2, 0, -1):
            ahead, behind = chip_sum(step), chip_sum(-step)
            if forth is None:
                forth, back = ahead, behind
            elif forth.shape[0] == half:
                forth = jnp.concatenate([add(ahead[:half], forth), ahead[half:]], axis=0)
                back = jnp.concatenate([behind[:half], add(behind[half:], back)], axis=0)
            else:
                forth, back = add(ahead, forth), add(behind, back)
            forth = lax.ppermute(forth, PLANE, self.clockwise)
            back = lax.ppermute(back, PLANE, self.counter)
        return chip_sum(0).astype(f32) + forth.astype(f32) + back.astype(f32)

    def small_sum(self, values):
        rows, cols = self.rows, self.cols
        if rows & (rows - 1) or cols & (cols - 1):
            return lax.psum(values, PLANE)
        swaps = []
        bit = 1
        while bit < cols:
            swaps.append(lambda row, col, bit=bit: (row, col ^ bit))
            bit *= 2
        bit = 1
        while bit < rows:
            swaps.append(lambda row, col, bit=bit: (row ^ bit, col))
            bit *= 2
        for swap in swaps:
            pairs = []
            for row in range(rows):
                for col in range(cols):
                    to_row, to_col = swap(row, col)
                    pairs.append((row * cols + col, to_row * cols + to_col))
            values = values + lax.ppermute(values, PLANE, pairs)
        return values


def dp_sum(part):
    count = lax.axis_size("dp")
    rank = lax.axis_index("dp")
    if count == 1:
        return part(rank)
    onward = [(d, (d + 1) % count) for d in range(count)]
    total = part((rank + count - 1) % count)
    for step in range(1, count):
        arrived = lax.ppermute(total.astype(bf16), "dp", onward)
        total = part((rank + 2 * count - 1 - step) % count) + arrived.astype(f32)
    return total


def exchange(pieces, axes):
    return lax.all_to_all(pieces, axes, split_axis=0, concat_axis=0, tiled=True)


def rope_tables(positions):
    half_width = HD // 2
    frequency = rope_base ** (-2.0 * jnp.arange(half_width, dtype=f32) / HD)
    angles = positions.astype(f32)[:, None] * frequency[None, :]
    return jnp.cos(angles), jnp.sin(angles)


def rotate(values, cosine, sine_part):
    half_width = values.shape[-1] // 2
    first_half, second_half = values[..., :half_width], values[..., half_width:]
    return jnp.concatenate(
        [
            first_half * cosine - second_half * sine_part,
            second_half * cosine + first_half * sine_part,
        ],
        axis=-1,
    )


def unrotate(gradient, cosine, sine_part):
    return rotate(gradient, cosine, -sine_part)


def norm_back(values, inverse, gain_row, upstream, dot_total):
    scaled = upstream * gain_row
    return inverse[:, None] * scaled - values * (inverse**3 * dot_total / D)[:, None]


def dot(a, b):
    return jnp.dot(a, b, preferred_element_type=f32)


def einsum(spec, a, b):
    return jnp.einsum(spec, a, b, preferred_element_type=f32)


def on_device(
    layer_input,
    gains,
    qkv_weight,
    output_weight,
    router_weight,
    expand_weight,
    reduce_weight,
    routes,
    drop_order,
    prefix_len,
    cotangent,
):
    row_rank, col_rank = lax.axis_index("row"), lax.axis_index("col")
    rows, cols = lax.axis_size("row"), lax.axis_size("col")
    dp_count = lax.axis_size("dp")
    group = rows * cols
    res_rows, row_width = layer_input.shape
    col_width = qkv_weight.shape[2]
    seq_len = res_rows * cols
    tok_rows = res_rows // rows
    block_rank = col_rank * rows + row_rank
    expert_rank = row_rank * cols + col_rank
    expert_count = router_weight.shape[1]
    local_experts = expand_weight.shape[0]
    capacity = tok_rows * TOP // expert_count
    slots = group * capacity
    ring = Ring(rows, cols)
    gain_rows = gains.astype(f32)

    head_weight = exchange(
        qkv_weight.reshape(row_width, 3, rows, HD).transpose(2, 0, 1, 3), "row"
    ).reshape(D, 3 * HD)
    cosine, sine_part = rope_tables(jnp.arange(seq_len))
    route_rows = lax.all_gather(
        jnp.concatenate([routes, drop_order[:, None]], axis=1), "col", axis=0, tiled=True
    )
    all_routes = route_rows[:, :TOP]
    drop_rank = route_rows[:, TOP].reshape(group, tok_rows)
    own_experts = expert_rank * local_experts + jnp.arange(local_experts)
    member = jnp.any(all_routes[:, :, None] == own_experts[None, None, :], axis=1)
    member = member.reshape(group, tok_rows, local_experts).transpose(0, 2, 1)
    token_index = jnp.arange(tok_rows)
    earlier = (drop_rank[:, None, :] < drop_rank[:, :, None]) | (
        drop_rank[:, None, :] == drop_rank[:, :, None]
    ) & (token_index[None, None, :] < token_index[None, :, None])
    position = jnp.sum(
        jnp.where(earlier[:, None] & member[:, :, None, :], 1, 0), axis=-1
    )
    kept = member & (position < capacity)
    hits = kept[:, :, None, :] & (
        position[:, :, None, :] == jnp.arange(capacity)[None, None, :, None]
    )
    dispatch = hits.astype(bf16)

    x_box = [jnp.zeros((seq_len, D), bf16)]

    def put_input(block, row, col):
        x_box[0] = lax.dynamic_update_slice(x_box[0], block, (col * res_rows, row * row_width))

    ring.gather(layer_input, put_input)
    x_all = x_box[0]
    x_wide = x_all.astype(f32)
    inv_first = lax.rsqrt(jnp.sum(x_wide * x_wide, axis=1) / D + norm_epsilon)
    first_low = (x_wide * inv_first[:, None] * gain_rows[0]).astype(bf16)
    projected = dot(first_low, head_weight)
    query_raw = projected[:, :HD]
    key_raw = projected[:, HD : 2 * HD]
    value_raw = projected[:, 2 * HD :]
    squares = ring.small_sum(
        jnp.stack([jnp.sum(query_raw * query_raw, axis=1), jnp.sum(key_raw * key_raw, axis=1)])
    )
    inv_query, inv_key = lax.rsqrt(squares / D + norm_epsilon)
    head_first = block_rank * HD
    gain_query = lax.dynamic_slice_in_dim(gain_rows[1], head_first, HD)
    gain_key = lax.dynamic_slice_in_dim(gain_rows[2], head_first, HD)
    query_low = rotate(query_raw * inv_query[:, None] * gain_query, cosine, sine_part).astype(bf16)
    key_low = rotate(key_raw * inv_key[:, None] * gain_key, cosine, sine_part).astype(bf16)
    value_low = value_raw.astype(bf16)

    query_rows = max(seq_len // 6, 128)
    attn_head, lse = attention(query_low, key_low, value_low, prefix_len, query_rows)
    attn_tokens = exchange(attn_head.reshape(group, tok_rows, HD), BLOCKS)
    attn_tokens = attn_tokens.transpose(1, 0, 2).reshape(tok_rows, D)
    output_full = lax.all_gather(output_weight, BLOCKS, axis=0)
    output_full = output_full.reshape(cols, rows, col_width, row_width)
    output_full = output_full.transpose(0, 2, 1, 3).reshape(D, D)
    first_token = block_rank * tok_rows
    x_tokens = lax.dynamic_slice_in_dim(x_all, first_token, tok_rows, 0).astype(f32)
    residual = x_tokens + dot(attn_tokens, output_full)
    inv_second = lax.rsqrt(jnp.sum(residual * residual, axis=1) / D + norm_epsilon)
    second_low = (residual * inv_second[:, None] * gain_rows[3]).astype(bf16)

    upstream_all = lax.all_gather(cotangent, BLOCKS, axis=0)
    upstream_all = upstream_all.reshape(cols, rows, res_rows, row_width)
    upstream_all = upstream_all.transpose(0, 2, 1, 3).reshape(seq_len, D)
    upstream = lax.dynamic_slice_in_dim(upstream_all, first_token, tok_rows, 0).astype(f32)

    def to_slots(token_rows):
        filled = einsum("best,btd->ebsd", dispatch, token_rows.reshape(group, tok_rows, D))
        return filled.astype(bf16).reshape(local_experts, slots, D)

    def from_slots(slot_rows):
        shaped = slot_rows.reshape(local_experts, group, capacity, D)
        return einsum("best,ebsd->btd", dispatch, shaped).astype(bf16)

    upstream_slots = to_slots(upstream_all)
    grad_hidden_raw = einsum("end,efd->enf", upstream_slots, reduce_weight)

    h_box = [jnp.zeros((group, tok_rows, D), bf16)]

    def put_rows(block, row, col):
        h_box[0] = lax.dynamic_update_slice(h_box[0], block[None], (col * rows + row, 0, 0))

    ring.gather(second_low, put_rows)
    feats_all = h_box[0].reshape(seq_len, D)
    slot_rows = to_slots(feats_all)
    logits = dot(feats_all, router_weight)
    router_probs = jax.nn.softmax(logits, axis=-1)
    own_probs = lax.dynamic_slice_in_dim(
        router_probs, expert_rank * local_experts, local_experts, 1
    ).reshape(group, tok_rows, local_experts)
    slot_gate = jnp.sum(
        jnp.where(hits, own_probs.transpose(0, 2, 1)[:, :, None, :], 0.0), axis=-1
    )
    slot_gate = slot_gate.transpose(1, 0, 2).reshape(local_experts, slots)[:, :, None]
    gate_up = einsum("end,edf->enf", slot_rows, expand_weight)
    gate_pre, up_pre = gate_up[..., :F], gate_up[..., F:]
    sigmoid_gate = jax.nn.sigmoid(gate_pre)
    silu_gate = gate_pre * sigmoid_gate
    hidden = (silu_gate * up_pre).astype(bf16)
    grad_hidden = grad_hidden_raw * slot_gate
    grad_gate_pre = (
        grad_hidden * up_pre * sigmoid_gate * (1.0 + gate_pre * (1.0 - sigmoid_gate))
    ).astype(bf16)
    grad_up_pre = (grad_hidden * silu_gate).astype(bf16)
    grad_gate_up = jnp.concatenate([grad_gate_pre, grad_up_pre], axis=-1)
    grad_slot_in = einsum("enf,edf->end", grad_gate_up, expand_weight).astype(bf16)
    grad_feats_part = from_slots(grad_slot_in)

    def rows_of(parts):
        return lambda row, col: lax.dynamic_index_in_dim(parts, col * rows + row, 0, False)

    grad_feats = ring.scatter_sum(rows_of(grad_feats_part))

    expert_out = einsum("enf,efd->end", hidden, reduce_weight).astype(bf16)
    grad_gate = jnp.sum(expert_out.astype(f32) * upstream_slots.astype(f32), axis=-1)
    grad_gate = grad_gate.reshape(local_experts, group, capacity).transpose(1, 0, 2)
    gate_tokens = jnp.sum(jnp.where(hits, grad_gate[..., None], 0.0), axis=2)
    grad_probs = exchange(gate_tokens, BLOCKS).reshape(cols, rows, local_experts, tok_rows)
    grad_probs = grad_probs.transpose(3, 1, 0, 2).reshape(tok_rows, expert_count)
    probs = lax.dynamic_slice_in_dim(router_probs, first_token, tok_rows, 0)
    grad_logits = (
        probs * (grad_probs - jnp.sum(probs * grad_probs, axis=-1, keepdims=True))
    ).astype(bf16)
    router_term = einsum("td,te->de", second_low, grad_logits)

    moe_part = from_slots((expert_out.astype(f32) * slot_gate).astype(bf16))
    moe_tokens = ring.scatter_sum(rows_of(moe_part))
    layer_tokens = (residual + moe_tokens).astype(bf16)
    layer_output = lax.all_to_all(layer_tokens, "row", split_axis=1, concat_axis=0, tiled=True)

    grad_out_slots = (upstream_slots.astype(f32) * slot_gate).astype(bf16)
    reduce_rows = F // dp_count
    expand_rows = D // dp_count

    def reduce_part(rank):
        block = lax.dynamic_slice_in_dim(hidden, rank * reduce_rows, reduce_rows, 2)
        return einsum("enf,end->efd", block, grad_out_slots)

    def expand_part(rank):
        block = lax.dynamic_slice_in_dim(slot_rows, rank * expand_rows, expand_rows, 2)
        return einsum("end,enf->edf", block, grad_gate_up)

    reduce_grad = dp_sum(reduce_part)
    expand_grad = dp_sum(expand_part)

    grad_feats = grad_feats + dot(grad_logits, router_weight.T)
    dot_second = jnp.sum(grad_feats * gain_rows[3] * residual, axis=1)
    grad_resid = upstream + norm_back(residual, inv_second, gain_rows[3], grad_feats, dot_second)
    gain_second_term = jnp.sum(grad_feats * residual * inv_second[:, None], axis=0)
    grad_branch = grad_resid.astype(bf16)
    grad_attn = einsum("tr,cr->tc", grad_branch, output_full).astype(bf16)
    grad_attn = grad_attn.reshape(tok_rows, group, HD).transpose(1, 0, 2)
    grad_attn = exchange(grad_attn, BLOCKS).reshape(seq_len, HD)
    grad_block = lax.all_to_all(grad_branch, "row", split_axis=1, concat_axis=0, tiled=True)
    output_term = einsum("tc,tr->cr", attn_tokens, grad_branch).astype(bf16)
    output_term = output_term.reshape(cols, col_width, rows, row_width).transpose(0, 2, 1, 3)
    output_sum = lax.psum_scatter(
        output_term.reshape(group, col_width, row_width), BLOCKS, scatter_dimension=0, tiled=False
    )
    output_rows = col_width // dp_count
    output_grad = dp_sum(
        lambda rank: lax.dynamic_slice_in_dim(
            output_sum, rank * output_rows, output_rows, 0
        ).astype(f32)
    )

    centre = jnp.sum(attn_head.astype(f32) * grad_attn.astype(f32), axis=1)[None]
    grad_query, grad_key, grad_value = attention_back(
        query_low, key_low, value_low, grad_attn, lse, centre, prefix_len, query_rows
    )
    grad_qnorm = unrotate(grad_query, cosine, sine_part)
    grad_knorm = unrotate(grad_key, cosine, sine_part)
    dots = ring.small_sum(
        jnp.stack(
            [
                jnp.sum(grad_qnorm * gain_query * query_raw, axis=1),
                jnp.sum(grad_knorm * gain_key * key_raw, axis=1),
            ]
        )
    )
    grad_qraw = norm_back(query_raw, inv_query, gain_query, grad_qnorm, dots[0])
    grad_kraw = norm_back(key_raw, inv_key, gain_key, grad_knorm, dots[1])
    gain_query_term = jnp.sum(grad_qnorm * query_raw * inv_query[:, None], axis=0)
    gain_key_term = jnp.sum(grad_knorm * key_raw * inv_key[:, None], axis=0)
    grad_qkv = jnp.concatenate([grad_qraw, grad_kraw, grad_value], axis=1).astype(bf16)

    grad_first_part = einsum("tc,fc->tf", grad_qkv, head_weight).astype(bf16)
    grad_first = ring.scatter_sum(
        lambda row, col: lax.dynamic_slice(
            grad_first_part, (col * res_rows, row * row_width), (res_rows, row_width)
        )
    )
    dot_first = ring.small_sum(jnp.sum(grad_qkv.astype(f32) * projected, axis=1) / inv_first)
    own_first = col_rank * res_rows
    dot_first = lax.dynamic_slice_in_dim(dot_first, own_first, res_rows)
    inv_block = lax.dynamic_slice_in_dim(inv_first, own_first, res_rows)
    gain_block = lax.dynamic_slice_in_dim(gain_rows[0], row_rank * row_width, row_width)
    input_grad = grad_block.astype(f32) + norm_back(
        layer_input.astype(f32), inv_block, gain_block, grad_first, dot_first
    )

    qkv_term = einsum("tf,tc->fc", first_low, grad_qkv)
    gain_first_term = jnp.sum(qkv_term * head_weight.astype(f32), axis=1) / gain_rows[0]
    qkv_rows = row_width // dp_count
    qkv_shaped = qkv_term.reshape(rows, row_width, 3 * HD)
    qkv_sum = dp_sum(
        lambda rank: lax.dynamic_slice_in_dim(qkv_shaped, rank * qkv_rows, qkv_rows, 1)
    )
    qkv_grad = exchange(qkv_sum.astype(bf16), "row").reshape(rows, qkv_rows, 3, HD)
    qkv_grad = qkv_grad.transpose(1, 2, 0, 3).reshape(1, qkv_rows, 3, col_width).astype(f32)

    def placed(term):
        return lax.dynamic_update_slice(jnp.zeros((D,), f32), term, (head_first,))

    gain_terms = jnp.stack(
        [gain_first_term, placed(gain_query_term), placed(gain_key_term), gain_second_term]
    )
    gain_total, router_total = lax.psum((gain_terms, router_term), ("dp", "row", "col"))
    return (
        layer_output,
        input_grad.astype(bf16),
        gain_total,
        qkv_grad,
        output_grad[None],
        router_total,
        expand_grad,
        reduce_grad,
    )


def solution(mesh):
    return jax.shard_map(
        on_device,
        mesh=mesh,
        in_specs=(
            P(("dp", "col"), "row"),
            P(),
            P("row", None, "col"),
            P("col", "row"),
            P(),
            P(("row", "col"), None, None),
            P(("row", "col"), None, None),
            P(("dp", "col"), None),
            P(("dp", "col")),
            P("dp"),
            P(("dp", "col"), "row"),
        ),
        out_specs=(
            P(("dp", "col"), "row"),
            P(("dp", "col"), "row"),
            P(),
            P("row", "dp", None, "col"),
            P("col", "dp", "row"),
            P(),
            P(("row", "col"), "dp", None),
            P(("row", "col"), "dp", None),
        ),
        check_vma=False,
    )
```

```python
import functools
import math

import jax
import jax.numpy as jnp
from jax import lax
from jax.experimental import pallas as pl
from jax.experimental.pallas import tpu as pltpu
from jax.sharding import PartitionSpec as P

D = 2048
HD = 128
F = 1024
TOP = 8
CORES = 2
PLANE = ("row", "col")
BLOCKS = ("col", "row")
LOG2E = math.log2(math.e)
MASKED = -1e30

norm_epsilon = 1e-05
rope_base = 10000.0
bf16 = jnp.bfloat16
f32 = jnp.float32


def dot_nt(a, b):
    return lax.dot_general(a, b, (((1,), (1,)), ((), ())), preferred_element_type=f32)


def dot_nn(a, b):
    return lax.dot_general(a, b, (((1,), (0,)), ((), ())), preferred_element_type=f32)


def cost(microseconds):
    return pl.CostEstimate(flops=int(microseconds * 1.1e9), bytes_accessed=0, transcendentals=0)


def as_row(column):
    return jnp.broadcast_to(column, (column.shape[0], 128)).T[:1]


def as_column(row):
    return jnp.broadcast_to(row, (8, row.shape[1])).T[:, :1]


def key_limits(first_query, query_rows, key_rows, prefix):
    open_blocks = jnp.maximum((first_query + 1) // key_rows, prefix // key_rows)
    all_blocks = pl.cdiv(jnp.maximum(first_query + query_rows, prefix), key_rows)
    return open_blocks, all_blocks


def mask_scores(scores, first_key, first_query, prefix):
    keys = first_key + lax.broadcasted_iota(jnp.int32, scores.shape, 0)
    queries = first_query + lax.broadcasted_iota(jnp.int32, scores.shape, 1)
    return jnp.where((keys <= queries) | (keys < prefix), scores, MASKED)


def attention_kernel(scale, prefix_ref, q_ref, k_ref, v_flip_ref, out_ref, lse_ref, scores_ref):
    query_rows = q_ref.shape[0]
    key_rows = min(512, k_ref.shape[0])
    first_query = pl.program_id(0) * query_rows
    prefix = prefix_ref[0]
    q = q_ref[...]
    open_blocks, all_blocks = key_limits(first_query, query_rows, key_rows, prefix)

    def score(j, top, masked):
        start = pl.multiple_of(j * key_rows, key_rows)
        scores = dot_nt(k_ref[pl.ds(start, key_rows), :], q) * (scale * LOG2E)
        if masked:
            scores = mask_scores(scores, start, first_query, prefix)
        scores_ref[pl.ds(start, key_rows), :] = scores
        return jnp.maximum(top, jnp.max(scores.reshape(key_rows // 8, 8, query_rows), axis=0))

    top = jnp.full((8, query_rows), MASKED, f32)
    top = lax.fori_loop(0, open_blocks, lambda j, t: score(j, t, False), top)
    top = lax.fori_loop(open_blocks, all_blocks, lambda j, t: score(j, t, True), top)
    peak = jnp.max(top, axis=0, keepdims=True)

    def mix(j, carry):
        total, mixed = carry
        start = pl.multiple_of(j * key_rows, key_rows)
        weights = jnp.exp2(scores_ref[pl.ds(start, key_rows), :] - peak)
        total = total + jnp.sum(weights.reshape(key_rows // 8, 8, query_rows), axis=0)
        mixed = mixed + dot_nn(v_flip_ref[:, pl.ds(start, key_rows)], weights.astype(bf16))
        return total, mixed

    total, mixed = lax.fori_loop(
        0,
        all_blocks,
        mix,
        (jnp.zeros((8, query_rows), f32), jnp.zeros((q.shape[1], query_rows), f32)),
    )
    total = jnp.sum(total, axis=0, keepdims=True)
    out_ref[...] = (mixed / total).T.astype(out_ref.dtype)
    lse_ref[...] = peak + jnp.log2(total)


def attention(q, k, v_flip, prefix_len, query_rows):
    length, width = q.shape
    query_block = pl.BlockSpec((query_rows, width), lambda i, p: (i, 0))
    return pl.pallas_call(
        functools.partial(attention_kernel, width**-0.5),
        grid_spec=pltpu.PrefetchScalarGridSpec(
            num_scalar_prefetch=1,
            grid=(length // query_rows,),
            in_specs=[
                query_block,
                pl.BlockSpec((length, width), lambda i, p: (0, 0)),
                pl.BlockSpec((width, length), lambda i, p: (0, 0)),
            ],
            out_specs=[query_block, pl.BlockSpec((1, query_rows), lambda i, p: (0, i))],
            scratch_shapes=[pltpu.VMEM((length, query_rows), f32)],
        ),
        out_shape=[
            jax.ShapeDtypeStruct((length, width), bf16),
            jax.ShapeDtypeStruct((1, length), f32),
        ],
        compiler_params=pltpu.CompilerParams(vmem_limit_bytes=40 * 2**20),
        cost_estimate=cost(17),
        name="attention_forward",
    )(prefix_len, q, k, v_flip)


def attention_back_kernel(
    scale, prefix_ref, q_ref, grad_ref, lse_ref, centre_ref, k_ref, k_flip_ref, v_ref,
    grad_q_ref, grad_k_ref, grad_v_ref, dot_q_ref, dot_k_ref, dot_v_ref,
):
    query_rows = q_ref.shape[0]
    key_rows = min(512, k_ref.shape[0])
    step = pl.program_id(0)
    first_query = step * query_rows
    prefix = prefix_ref[0]

    @pl.when(step == 0)
    def _():
        grad_k_ref[...] = jnp.zeros_like(grad_k_ref)
        grad_v_ref[...] = jnp.zeros_like(grad_v_ref)

    q = q_ref[...]
    grad = grad_ref[...]
    lse = lse_ref[...]
    centre = centre_ref[...]
    open_blocks, all_blocks = key_limits(first_query, query_rows, key_rows, prefix)

    def block(j, total, masked):
        start = pl.multiple_of(j * key_rows, key_rows)
        rows = pl.ds(start, key_rows)
        scores = dot_nt(k_ref[rows, :], q) * (scale * LOG2E) - lse
        if masked:
            scores = mask_scores(scores, start, first_query, prefix)
        weights = jnp.exp2(scores)
        grad_weights = dot_nt(v_ref[rows, :], grad)
        grad_scores = (weights * (grad_weights - centre)).astype(bf16)
        grad_v_ref[rows, :] += dot_nn(weights.astype(bf16), grad)
        grad_k_ref[rows, :] += dot_nn(grad_scores, q)
        return total + dot_nn(k_flip_ref[:, rows], grad_scores)

    total = jnp.zeros((q.shape[1], query_rows), f32)
    total = lax.fori_loop(0, open_blocks, lambda j, a: block(j, a, False), total)
    total = lax.fori_loop(open_blocks, all_blocks, lambda j, a: block(j, a, True), total)
    grad_q = total.T * scale
    grad_q_ref[...] = grad_q
    dot_q_ref[...] = as_row(jnp.sum(grad_q * q.astype(f32), axis=1, keepdims=True))

    @pl.when(step == pl.num_programs(0) - 1)
    def _():
        for start in range(0, k_ref.shape[0], key_rows):
            rows = pl.ds(start, key_rows)
            grad_k = grad_k_ref[rows, :] * scale
            grad_k_ref[rows, :] = grad_k
            dot_k_ref[:, rows] = as_row(
                jnp.sum(grad_k * k_ref[rows, :].astype(f32), axis=1, keepdims=True)
            )
            dot_v_ref[:, rows] = as_row(
                jnp.sum(grad_v_ref[rows, :] * v_ref[rows, :].astype(f32), axis=1, keepdims=True)
            )


def attention_back(q, k, k_flip, v, grad, lse, centre, prefix_len, query_rows):
    length, width = q.shape
    whole = pl.BlockSpec((length, width), lambda i, p: (0, 0))
    flipped = pl.BlockSpec((width, length), lambda i, p: (0, 0))
    query_block = pl.BlockSpec((query_rows, width), lambda i, p: (i, 0))
    query_row = pl.BlockSpec((1, query_rows), lambda i, p: (0, i))
    result = jax.ShapeDtypeStruct((length, width), f32)
    return pl.pallas_call(
        functools.partial(attention_back_kernel, width**-0.5),
        grid_spec=pltpu.PrefetchScalarGridSpec(
            num_scalar_prefetch=1,
            grid=(length // query_rows,),
            in_specs=[query_block, query_block, query_row, query_row, whole, flipped, whole],
            out_specs=[query_block, whole, whole, query_row] + [pl.BlockSpec((1, length), lambda i, p: (0, 0))] * 2,
        ),
        out_shape=[result, result, result] + [jax.ShapeDtypeStruct((1, length), f32)] * 3,
        compiler_params=pltpu.CompilerParams(vmem_limit_bytes=40 * 2**20),
        cost_estimate=cost(24),
        name="attention_backward",
    )(prefix_len, q, grad, lse, centre, k, k_flip, v)


def unwritten(shape, dtype):
    return pl.pallas_call(
        lambda out_ref: None,
        out_specs=pl.BlockSpec(memory_space=pl.ANY),
        out_shape=jax.ShapeDtypeStruct(shape, dtype),
        name="buffer",
    )()


def add_low(one, two):
    return (one.astype(f32) + two.astype(f32)).astype(bf16)


def after(value, earlier):
    return lax.optimization_barrier((value, earlier))[0]


def together(*values):
    return lax.optimization_barrier(values)


class Ring:
    def __init__(self, rows, cols):
        self.rows, self.cols = rows, cols
        self.cores = CORES if cols % CORES == 0 else 1
        self.groups = cols // self.cores
        self.order = [
            (row, group)
            for group in range(self.groups)
            for row in (range(rows) if group % 2 == 0 else range(rows - 1, -1, -1))
        ]
        self.size = len(self.order)
        self.clockwise = self.shift(1)
        self.counter = self.shift(-1)
        self.sibling = [
            (row * cols + col, row * cols + col - col % self.cores + (col + 1) % self.cores)
            for row in range(rows)
            for col in range(cols)
        ]
        row, col = lax.axis_index("row"), lax.axis_index("col")
        group = col // self.cores
        self.core = col % self.cores
        self.place = group * rows + jnp.where(group % 2 == 0, row, rows - 1 - row)

    def shift(self, step):
        pairs = []
        for at, (row, group) in enumerate(self.order):
            to_row, to_group = self.order[(at + step) % self.size]
            for core in range(self.cores):
                pairs.append(
                    (
                        row * self.cols + group * self.cores + core,
                        to_row * self.cols + to_group * self.cores + core,
                    )
                )
        return pairs

    def chip(self, distance):
        at = (self.place + distance + self.size) % self.size
        group = at // self.rows
        along = at % self.rows
        return jnp.where(group % 2 == 0, along, self.rows - 1 - along), group

    def owners(self, distance):
        row, group = self.chip(distance)
        return [(row, group * self.cores + (self.core + k) % self.cores) for k in range(self.cores)]

    def block_ids(self, distance):
        return [col * self.rows + row for row, col in self.owners(distance)]

    def from_siblings(self, block):
        return [block] + [lax.ppermute(block, PLANE, self.sibling)] * (self.cores - 1)

    def gather_steps(self, block):
        forth = back = block
        yield [(block, 0)]
        for step in range(1, (self.size + 1) // 2):
            forth = lax.ppermute(forth, PLANE, self.clockwise)
            back = lax.ppermute(back, PLANE, self.counter)
            sent = yield [(forth, -step), (back, step)]
            if sent is not None:
                forth, back = sent
        if self.size % 2 == 0:
            half = block.shape[0] // 2
            forth = lax.ppermute(forth[:half], PLANE, self.clockwise)
            back = lax.ppermute(back[half:], PLANE, self.counter)
            yield [(jnp.concatenate([forth, back], axis=0), self.size // 2)]

    def with_siblings(self, arrival):
        return [
            pair
            for piece, distance in arrival
            for pair in zip(self.from_siblings(piece), self.block_ids(distance))
        ]

    def place_blocks(self, box, pairs):
        for piece, ident in pairs:
            start = (ident,) + (0,) * piece.ndim
            box = lax.dynamic_update_slice(box, piece[None], start)
        return box

    def gather_array(self, block):
        box = unwritten((self.rows * self.cols,) + block.shape, block.dtype)
        for arrival in self.gather_steps(block):
            box = self.place_blocks(box, self.with_siblings(arrival))
        return box

    def chip_sum(self, mine, *others):
        for other in others:
            mine = add_low(mine, lax.ppermute(other, PLANE, self.sibling))
        return mine

    def scatter_steps(self, parts):
        forth = back = None
        half = 0
        if self.size % 2 == 0:
            far = parts(self.size // 2)
            half = far.shape[0] // 2
            forth = lax.ppermute(far[:half], PLANE, self.clockwise)
            back = lax.ppermute(far[half:], PLANE, self.counter)
            forth, back = yield forth, back
        for step in range((self.size - 1) // 2, 0, -1):
            ahead, behind = parts(step), parts(-step)
            if forth is None:
                forth, back = ahead, behind
            elif forth.shape[0] == half:
                forth = jnp.concatenate([add_low(ahead[:half], forth), ahead[half:]], axis=0)
                back = jnp.concatenate([behind[:half], add_low(behind[half:], back)], axis=0)
            else:
                forth, back = add_low(ahead, forth), add_low(behind, back)
            forth = lax.ppermute(forth, PLANE, self.clockwise)
            back = lax.ppermute(back, PLANE, self.counter)
            forth, back = yield forth, back
        yield parts(0), forth, back

    def scatter_parts(self, parts):
        steps = self.scatter_steps(parts)
        terms = next(steps)
        while len(terms) == 2:
            terms = steps.send(terms)
        return terms

    def distances(self):
        half = (self.size - 1) // 2
        far = [self.size // 2] if self.size % 2 == 0 else []
        return [0] + [d for step in range(1, half + 1) for d in (-step, step)] + far

    def sum_steps(self, values):
        rows, cols = self.rows, self.cols
        if rows & (rows - 1) or cols & (cols - 1):
            yield lax.psum(values, PLANE)
            return
        swaps = []
        bit = 1
        while bit < cols:
            swaps.append(lambda row, col, bit=bit: (row, col ^ bit))
            bit *= 2
        bit = 1
        while bit < rows:
            swaps.append(lambda row, col, bit=bit: (row ^ bit, col))
            bit *= 2
        for swap in swaps:
            pairs = []
            for row in range(rows):
                for col in range(cols):
                    to_row, to_col = swap(row, col)
                    pairs.append((row * cols + col, to_row * cols + to_col))
            values = values + lax.ppermute(values, PLANE, pairs)
            sent = yield values
            values = values if sent is None else sent

    def small_sum(self, values):
        *_, last = self.sum_steps(values)
        return last


def dp_sum(part):
    count = lax.axis_size("dp")
    rank = lax.axis_index("dp")
    if count == 1:
        return part(rank)
    onward = [(d, (d + 1) % count) for d in range(count)]
    total = part((rank + count - 1) % count)
    for step in range(1, count):
        arrived = lax.ppermute(total.astype(bf16), "dp", onward)
        total = part((rank + 2 * count - 1 - step) % count) + arrived.astype(f32)
    return total


def dp_all_sum(values):
    count = lax.axis_size("dp")
    if count & (count - 1):
        return lax.psum(values, "dp")
    bit = 1
    while bit < count:
        values = values + lax.ppermute(values, "dp", [(d, d ^ bit) for d in range(count)])
        bit *= 2
    return values


def exchange_rows(pieces):
    rows = pieces.shape[0]
    row = lax.axis_index("row")
    start = lambda at: (at,) + (0,) * (pieces.ndim - 1)
    taken = unwritten(pieces.shape, pieces.dtype)
    own = lax.dynamic_index_in_dim(pieces, row, 0, True)
    taken = lax.dynamic_update_slice(taken, own, start(row))
    for step in range(1, rows):
        sent = lax.dynamic_index_in_dim(pieces, (row + step) % rows, 0, True)
        sent = lax.ppermute(sent, "row", [(r, (r + step) % rows) for r in range(rows)])
        taken = lax.dynamic_update_slice(taken, sent, start((row + rows - step) % rows))
    return taken


def exchange(pieces, axes):
    return lax.all_to_all(pieces, axes, split_axis=0, concat_axis=0, tiled=True)


def project_kernel(x_ref, gain_ref, weight_ref, out_ref, inverse_ref, squares_ref, low_ref):
    blocks, _, width = x_ref.shape
    total = 0.0
    for block in range(blocks):
        part = x_ref[block].astype(f32)
        total = total + jnp.sum(part * part, axis=1, keepdims=True)
    inverse = lax.rsqrt(total / D + norm_epsilon)
    for block in range(blocks):
        at = pl.ds(block * width, width)
        low_ref[:, at] = (x_ref[block].astype(f32) * inverse * gain_ref[:, at]).astype(bf16)
    out = dot_nn(low_ref[...], weight_ref[...])
    out_ref[...] = out
    inverse_ref[...] = as_row(inverse)
    for j in range(2):
        part = out[:, j * HD : (j + 1) * HD]
        squares_ref[pl.ds(j, 1), :] = as_row(jnp.sum(part * part, axis=1, keepdims=True))


def project(x_blocks, gain_row, weight, rows):
    count, block_rows, width = x_blocks.shape
    cols = count // rows
    tile = block_rows
    per = block_rows // tile
    length = cols * block_rows
    return pl.pallas_call(
        project_kernel,
        grid=(cols * per,),
        in_specs=[
            pl.BlockSpec((rows, tile, width), lambda i: (i // per, i % per, 0)),
            pl.BlockSpec((1, D), lambda i: (0, 0)),
            pl.BlockSpec(weight.shape, lambda i: (0, 0)),
        ],
        out_specs=[
            pl.BlockSpec((tile, 3 * HD), lambda i: (i, 0)),
            pl.BlockSpec((1, tile), lambda i: (0, i)),
            pl.BlockSpec((2, tile), lambda i: (0, i)),
        ],
        scratch_shapes=[pltpu.VMEM((tile, D), bf16)],
        out_shape=[
            jax.ShapeDtypeStruct((length, 3 * HD), f32),
            jax.ShapeDtypeStruct((1, length), f32),
            jax.ShapeDtypeStruct((2, length), f32),
        ],
        compiler_params=pltpu.CompilerParams(vmem_limit_bytes=52 * 2**20),
        cost_estimate=cost(14),
        name="norm_and_project",
    )(x_blocks, gain_row, weight)


def project_weight_kernel(x_ref, gain_ref, inverse_ref, grad_ref, out_ref, low_ref):
    blocks, _, width = x_ref.shape
    inverse = as_column(inverse_ref[...])

    @pl.when(pl.program_id(0) == 0)
    def _():
        out_ref[...] = jnp.zeros_like(out_ref)

    for block in range(blocks):
        at = pl.ds(block * width, width)
        low_ref[:, at] = (x_ref[block].astype(f32) * inverse * gain_ref[:, at]).astype(bf16)
    for block in range(blocks):
        at = pl.ds(block * width, width)
        out_ref[at, :] += dot_nn(low_ref[:, at].T, grad_ref[...])


def project_weight(x_blocks, gain_row, inverse, grads, rows):
    count, block_rows, width = x_blocks.shape
    cols = count // rows
    tile = block_rows // 3 if block_rows % 384 == 0 else block_rows
    per = block_rows // tile
    return pl.pallas_call(
        project_weight_kernel,
        grid=(cols * per,),
        in_specs=[
            pl.BlockSpec((rows, tile, width), lambda i: (i // per, i % per, 0)),
            pl.BlockSpec((1, D), lambda i: (0, 0)),
            pl.BlockSpec((1, tile), lambda i: (0, i)),
            pl.BlockSpec((tile, 3 * HD), lambda i: (i, 0)),
        ],
        out_specs=pl.BlockSpec((D, 3 * HD), lambda i: (0, 0)),
        scratch_shapes=[pltpu.VMEM((tile, D), bf16)],
        out_shape=jax.ShapeDtypeStruct((D, 3 * HD), f32),
        compiler_params=pltpu.CompilerParams(vmem_limit_bytes=40 * 2**20),
        cost_estimate=cost(15),
        name="projection_weight_gradient",
    )(x_blocks, gain_row, inverse, grads)


def turn_kernel(raw_ref, squares_ref, gain_ref, cosine_ref, sine_ref, q_ref, k_ref, v_ref, k_flip_ref, v_flip_ref):
    inverse = lax.rsqrt(squares_ref[...] / D + norm_epsilon)
    for j, out_ref in ((0, q_ref), (1, k_ref)):
        normed = raw_ref[:, j * HD : (j + 1) * HD] * as_column(inverse[j : j + 1]) * gain_ref[j : j + 1, :]
        turned = normed * cosine_ref[...] + jnp.roll(normed, HD // 2, axis=1) * sine_ref[...]
        out_ref[...] = turned.astype(bf16)
        if j == 1:
            k_flip_ref[...] = turned.T.astype(bf16)
    v = raw_ref[:, 2 * HD :]
    v_ref[...] = v.astype(bf16)
    v_flip_ref[...] = v.T.astype(bf16)


def turn(raw, squares, gain_pair, cosine, sine_part):
    length = raw.shape[0]
    tile = min(1024, length)
    tall = pl.BlockSpec((tile, HD), lambda i: (i, 0))
    wide = pl.BlockSpec((HD, tile), lambda i: (0, i))
    tall_shape = jax.ShapeDtypeStruct((length, HD), bf16)
    wide_shape = jax.ShapeDtypeStruct((HD, length), bf16)
    return pl.pallas_call(
        turn_kernel,
        grid=(length // tile,),
        in_specs=[
            pl.BlockSpec((tile, 3 * HD), lambda i: (i, 0)),
            pl.BlockSpec((2, tile), lambda i: (0, i)),
            pl.BlockSpec((2, HD), lambda i: (0, 0)),
            tall,
            tall,
        ],
        out_specs=[tall, tall, tall, wide, wide],
        out_shape=[tall_shape, tall_shape, tall_shape, wide_shape, wide_shape],
        cost_estimate=cost(7.4),
        name="query_key_value",
    )(raw, squares, gain_pair, cosine, sine_part)


def branch_kernel(
    groups, sets, at_ref, heads_ref, x_ref, gain_ref, *refs
):
    weights, (residual_ref, low_ref) = refs[: groups * sets], refs[groups * sets :]
    step = pl.program_id(0)
    rows, width = x_ref.shape[0], x_ref.shape[2]
    height = weights[0].shape[1]
    per = height // HD
    branch = x_ref[pl.ds(step, 1)][0].astype(f32)
    for group in range(groups):
        for k in range(sets):
            first = at_ref[2 + group * sets + k]
            heads = jnp.concatenate([heads_ref[first + j] for j in range(per)], axis=1)
            branch = branch + dot_nn(heads, weights[group * sets + k][0])
    residual_ref[:, pl.ds(pl.multiple_of(step * width, width), width)] = branch

    @pl.when(step == rows - 1)
    def _():
        total = residual_ref[...]
        inverse = lax.rsqrt(jnp.sum(total * total, axis=1, keepdims=True) / D + norm_epsilon)
        low_ref[...] = (total * inverse * gain_ref[...]).astype(bf16)


def output_branch(at, table, heads, weight_sets, x_blocks, gain_row, rows, groups):
    tok_rows = heads.shape[1]
    sets = len(weight_sets)
    _, height, width = weight_sets[0].shape
    fixed = lambda shape: pl.BlockSpec(shape, lambda i, a, t: (0,) * len(shape))
    return pl.pallas_call(
        lambda at_ref, table_ref, *refs: branch_kernel(groups, sets, at_ref, *refs),
        grid_spec=pltpu.PrefetchScalarGridSpec(
            num_scalar_prefetch=2,
            grid=(rows,),
            in_specs=[
                fixed(heads.shape),
                pl.BlockSpec((rows, tok_rows, width), lambda i, a, t: (a[0], a[1], 0)),
                fixed((1, D)),
            ]
            + [
                pl.BlockSpec(
                    (1, height, width), lambda i, a, t, g=g, k=k: (t[(k * groups + g) * rows + i], 0, 0)
                )
                for g in range(groups)
                for k in range(sets)
            ],
            out_specs=[fixed((tok_rows, D)), fixed((tok_rows, D))],
        ),
        out_shape=[
            jax.ShapeDtypeStruct((tok_rows, D), f32),
            jax.ShapeDtypeStruct((tok_rows, D), bf16),
        ],
        compiler_params=pltpu.CompilerParams(vmem_limit_bytes=40 * 2**20),
        cost_estimate=cost(6),
        name="output_projection",
    )(at, table, heads, x_blocks, gain_row, *[w for _ in range(groups) for w in weight_sets])


def resid_kernel(
    at_ref, own_ref, forth_ref, back_ref, logit_ref, router_ref, residual_ref, up_ref, gain_ref,
    grad_low_ref, gain_term_ref,
):
    rows, width = up_ref.shape[0], up_ref.shape[2]
    grad = own_ref[...].astype(f32) + forth_ref[...].astype(f32) + back_ref[...].astype(f32)
    grad = grad + dot_nn(logit_ref[...], router_ref[...])
    residual = residual_ref[...]
    inverse = lax.rsqrt(jnp.sum(residual * residual, axis=1, keepdims=True) / D + norm_epsilon)
    scaled = grad * gain_ref[...]
    total = jnp.sum(scaled * residual, axis=1, keepdims=True)
    gain_term_ref[...] = jnp.sum(grad * residual * inverse, axis=0, keepdims=True)
    back = inverse * scaled - residual * (inverse * inverse * inverse * total / D)
    for row in range(rows):
        at = pl.ds(row * width, width)
        grad_low_ref[:, at] = (
            up_ref[row].astype(f32) + back[:, row * width : (row + 1) * width]
        ).astype(bf16)


def residual_back(at, terms, grad_logits, router_flip, residual, up_blocks, gain_row, rows):
    tok_rows = residual.shape[0]
    width = up_blocks.shape[2]
    fixed = lambda shape: pl.BlockSpec(shape, lambda i, a: (0,) * len(shape))
    whole, line = fixed((tok_rows, D)), fixed((1, D))
    return pl.pallas_call(
        resid_kernel,
        grid_spec=pltpu.PrefetchScalarGridSpec(
            num_scalar_prefetch=1,
            grid=(1,),
            in_specs=[
                whole,
                whole,
                whole,
                fixed(grad_logits.shape),
                fixed(router_flip.shape),
                whole,
                pl.BlockSpec((rows, tok_rows, width), lambda i, a: (a[0], a[1], 0)),
                line,
            ],
            out_specs=[whole, line],
        ),
        out_shape=[
            jax.ShapeDtypeStruct((tok_rows, D), bf16),
            jax.ShapeDtypeStruct((1, D), f32),
        ],
        compiler_params=pltpu.CompilerParams(vmem_limit_bytes=40 * 2**20),
        cost_estimate=cost(3),
        name="residual_backward",
    )(at, *terms, grad_logits, router_flip, residual, up_blocks, gain_row)


def dispatch_kernel(hits_ref, x_ref, out_ref):
    experts, _, capacity, _ = out_ref.shape
    width = x_ref.shape[2]
    for block in range(x_ref.shape[0]):
        picked = dot_nn(hits_ref[0], x_ref[block]).astype(bf16)
        for e in range(experts):
            out_ref[e, 0, :, pl.ds(block * width, width)] = picked[e * capacity : (e + 1) * capacity]


def dispatch_blocks(hits, x_blocks, rows, experts):
    group, slot_rows, tok_rows = hits.shape
    width = x_blocks.shape[2]
    capacity = slot_rows // experts
    return pl.pallas_call(
        dispatch_kernel,
        grid=(group,),
        in_specs=[
            pl.BlockSpec((1, slot_rows, tok_rows), lambda b: (b, 0, 0)),
            pl.BlockSpec((rows, tok_rows, width), lambda b: (b // rows, b % rows, 0)),
        ],
        out_specs=pl.BlockSpec((experts, 1, capacity, D), lambda b: (0, b, 0, 0)),
        out_shape=jax.ShapeDtypeStruct((experts, group, capacity, D), bf16),
        cost_estimate=cost(14),
        name="cotangent_to_slots",
    )(hits, x_blocks)


def experts_kernel(count, first, ids_ref, *refs):
    feats = refs[:count]
    raws = refs[count : 2 * count]
    hits_ref, flip_ref, router_ref, gate_w_ref, up_w_ref = refs[2 * count : 2 * count + 5]
    rest = refs[2 * count + 5 :]
    if not first:
        rest = rest[5:]
    slot_ref, hidden_ref, grad_gate_ref, grad_up_ref, scale_ref = rest[:5]
    feat_sums = rest[5 : 5 + count]
    probs_ref, in_acc, in_all = rest[5 + count :]
    e, f = pl.program_id(0), pl.program_id(1)
    last_expert = e == pl.num_programs(0) - 1
    last_tile = f == pl.num_programs(1) - 1
    capacity = raws[0].shape[2]
    chosen = ids_ref[count] + e
    own_slots = pl.ds(pl.multiple_of(e * capacity, 16), capacity)

    @pl.when((e == 0) & (f == 0))
    def _():
        for k in range(count):
            logits = dot_nt(router_ref[...], feats[k][...])
            raised = jnp.exp(logits - jnp.max(logits, axis=0, keepdims=True))
            probs_ref[k] = raised / jnp.sum(raised, axis=0, keepdims=True)

    @pl.when(f == 0)
    def _():
        for k in range(count):
            at = pl.ds(k * capacity, capacity)
            hits = hits_ref[ids_ref[k], own_slots, :]
            slot_ref[0, at, :] = dot_nn(hits, feats[k][...]).astype(bf16)
            probs = probs_ref[k]
            rank = lax.broadcasted_iota(jnp.int32, probs.shape, 0)
            gate = jnp.sum(jnp.where(rank == chosen, probs, 0.0), axis=0, keepdims=True)
            scale_ref[0, at, :] = jnp.sum(hits.astype(f32) * gate, axis=1, keepdims=True)

    slots = slot_ref[0]
    gate_w, up_w = gate_w_ref[0], up_w_ref[0]
    gate_pre = dot_nn(slots, gate_w)
    up_pre = dot_nn(slots, up_w)
    sigmoid = 1.0 / (1.0 + jnp.exp(-gate_pre))
    silu = gate_pre * sigmoid
    hidden_ref[0] = (silu * up_pre).astype(bf16)
    grad_hidden = jnp.concatenate([raw[0, 0] for raw in raws], axis=0) * scale_ref[0]
    grad_gate = (grad_hidden * up_pre * sigmoid * (1.0 + gate_pre * (1.0 - sigmoid))).astype(bf16)
    grad_up = (grad_hidden * silu).astype(bf16)
    grad_gate_ref[0] = grad_gate
    grad_up_ref[0] = grad_up
    in_term = dot_nt(grad_gate, gate_w) + dot_nt(grad_up, up_w)

    @pl.when(f == 0)
    def _():
        in_acc[...] = in_term

    @pl.when(f > 0)
    def _():
        in_acc[...] += in_term

    @pl.when(last_tile)
    def _():
        for k in range(count):
            in_all[k, own_slots, :] = in_acc[pl.ds(k * capacity, capacity), :].astype(bf16)

    @pl.when(last_tile & last_expert)
    def _():
        for k in range(count):
            feat_sums[k][...] = dot_nn(flip_ref[ids_ref[k]], in_all[k]).astype(bf16)


def run_experts(feats, ids, first_expert, grad_raw, hits, flip, router_flip, expand_weight, carried, place):
    count = len(feats)
    experts, group, capacity, _ = grad_raw.shape
    tok_rows = feats[0].shape[0]
    rows = count * capacity
    tile = F // 2
    tiles = F // tile
    first = carried is None
    whole = lambda shape: pl.BlockSpec(shape, lambda e, f, ids: (0,) * len(shape))
    in_specs = [whole((tok_rows, D))] * count
    in_specs += [
        pl.BlockSpec((1, 1, capacity, tile), lambda e, f, ids, k=k: (e, ids[k], 0, f))
        for k in range(count)
    ]
    in_specs += [
        whole(hits.shape),
        whole(flip.shape),
        whole(router_flip.shape),
        pl.BlockSpec((1, D, tile), lambda e, f, ids: (e, 0, f)),
        pl.BlockSpec((1, D, tile), lambda e, f, ids: (e, 0, f + tiles)),
    ]
    operands = [*feats, *[grad_raw] * count, hits, flip, router_flip, expand_weight, expand_weight]
    aliases = {}
    if not first:
        in_specs += [pl.BlockSpec(memory_space=pl.ANY)] * 5
        operands += carried
        aliases = {1 + len(operands) - 5 + k: k for k in range(5)}
    wide = pl.BlockSpec((1, rows, D), lambda e, f, ids: (e, place, 0))
    narrow = pl.BlockSpec((1, rows, tile), lambda e, f, ids: (e, place, f))
    thin = pl.BlockSpec((1, rows, 1), lambda e, f, ids: (e, place, 0))
    narrow_shape = jax.ShapeDtypeStruct((experts, group * capacity, F), bf16)
    out = pl.pallas_call(
        functools.partial(experts_kernel, count, first),
        grid_spec=pltpu.PrefetchScalarGridSpec(
            num_scalar_prefetch=1,
            grid=(experts, tiles),
            in_specs=in_specs,
            out_specs=[wide, narrow, narrow, narrow, thin] + [whole((tok_rows, D))] * count,
            scratch_shapes=[
                pltpu.VMEM((count, router_flip.shape[0], tok_rows), f32),
                pltpu.VMEM((rows, D), f32),
                pltpu.VMEM((count, experts * capacity, D), bf16),
            ],
        ),
        out_shape=[jax.ShapeDtypeStruct((experts, group * capacity, D), bf16)]
        + [narrow_shape] * 3
        + [jax.ShapeDtypeStruct((experts, group * capacity, 1), f32)]
        + [jax.ShapeDtypeStruct((tok_rows, D), bf16)] * count,
        input_output_aliases=aliases,
        compiler_params=pltpu.CompilerParams(vmem_limit_bytes=56 * 2**20),
        cost_estimate=cost(13 + 2 * count),
        name="experts",
    )(jnp.stack([*ids, first_expert]).astype(jnp.int32), *operands)
    return out[:5], out[5:]


def combine_kernel(ids_ref, out_ref, up_ref, hits_ref, flip_ref, scale_ref, gates_ref, grad_out_ref, moe_ref):
    experts, _, capacity, _ = out_ref.shape
    scaled = []
    for e in range(experts):
        expert_out = out_ref[e, 0].astype(f32)
        upstream = up_ref[e, 0].astype(f32)
        scale = scale_ref[e, 0]
        dots = jnp.sum(expert_out * upstream, axis=1, keepdims=True)
        hits = hits_ref[0, e * capacity : (e + 1) * capacity, :].astype(f32)
        gates_ref[0, pl.ds(e, 1), :] = jnp.sum(hits * dots, axis=0, keepdims=True)
        grad_out_ref[e, 0] = (upstream * scale).astype(bf16)
        scaled.append((expert_out * scale).astype(bf16))
    moe_ref[0] = dot_nn(flip_ref[0], jnp.concatenate(scaled, axis=0)).astype(bf16)


def combine_experts(ids, expert_out, upstream_slots, hits, flip, scale):
    experts, group, capacity, _ = upstream_slots.shape
    tok_rows = hits.shape[2]
    by_place = pl.BlockSpec((experts, 1, capacity, D), lambda j, ids: (0, j, 0, 0))
    by_id = lambda shape: pl.BlockSpec((1,) + shape, lambda j, ids: (ids[j], 0, 0))
    return pl.pallas_call(
        combine_kernel,
        grid_spec=pltpu.PrefetchScalarGridSpec(
            num_scalar_prefetch=1,
            grid=(group,),
            in_specs=[
                by_place,
                pl.BlockSpec((experts, 1, capacity, D), lambda j, ids: (0, ids[j], 0, 0)),
                by_id(hits.shape[1:]),
                by_id(flip.shape[1:]),
                pl.BlockSpec((experts, 1, capacity, 1), lambda j, ids: (0, j, 0, 0)),
            ],
            out_specs=[by_id((experts, tok_rows)), by_place, by_id((tok_rows, D))],
        ),
        out_shape=[
            jax.ShapeDtypeStruct((group, experts, tok_rows), f32),
            jax.ShapeDtypeStruct((experts, group, capacity, D), bf16),
            jax.ShapeDtypeStruct((group, tok_rows, D), bf16),
        ],
        compiler_params=pltpu.CompilerParams(vmem_limit_bytes=40 * 2**20),
        cost_estimate=cost(18),
        name="experts_combine",
    )(
        ids,
        expert_out.reshape(experts, group, capacity, D),
        upstream_slots,
        hits,
        flip,
        scale.reshape(experts, group, capacity, 1),
    )


def weight_grad_kernel(sides, added, pieces, rank_ref, left_ref, *refs):
    rights, refs = refs[:sides], refs[sides:]
    more, refs = refs[:added], refs[added:]
    outs, flip_ref = refs[:-1], refs[-1]
    e, m, n = pl.program_id(0), pl.program_id(1), pl.program_id(2)

    @pl.when(n == 0)
    def _():
        flip_ref[...] = left_ref[0].T

    for side in range(sides):

        @pl.when(n == side)
        def _():
            total = dot_nn(flip_ref[...], rights[side][0])
            if not added and not pieces:
                outs[0][0] = total
            for k in range(side, max(added, len(outs) if pieces else 0), sides):

                @pl.when(e * pl.num_programs(1) + m == k // sides)
                def _():
                    grown = total + more[k][...].astype(f32) if added else total
                    if pieces:
                        outs[k][...] = grown.astype(bf16)
                    else:
                        outs[0][0] = grown


def weight_grad(left, rights, rank, rows, first=0, experts=None, more=(), pieces=False):
    experts = left.shape[0] if experts is None else experts
    slots = left.shape[1]
    tile = min(512, rows)
    per = rows // tile
    width = F
    shares = [(right, j) for right in rights for j in range(right.shape[2] // width)]
    sides = len(shares)
    piece = pl.BlockSpec((tile, width), lambda e, m, n, p: (0, 0))
    if pieces:
        out_specs = [piece] * (experts * per * sides)
        out_shape = [jax.ShapeDtypeStruct((tile, width), bf16)] * (experts * per * sides)
    else:
        out_specs = [pl.BlockSpec((1, tile, width), lambda e, m, n, p: (e, m, n))]
        out_shape = [jax.ShapeDtypeStruct((experts, rows, sides * width), f32)]
    out = pl.pallas_call(
        functools.partial(weight_grad_kernel, sides, len(more), pieces),
        grid_spec=pltpu.PrefetchScalarGridSpec(
            num_scalar_prefetch=1,
            grid=(experts, per, sides),
            in_specs=[
                pl.BlockSpec((1, slots, tile), lambda e, m, n, p: (e + first, 0, p[0] * per + m))
            ]
            + [
                pl.BlockSpec((1, slots, width), lambda e, m, n, p, j=j: (e + first, 0, j))
                for _, j in shares
            ]
            + [piece] * len(more),
            out_specs=out_specs,
            scratch_shapes=[pltpu.VMEM((tile, slots), bf16)],
        ),
        out_shape=out_shape,
        compiler_params=pltpu.CompilerParams(vmem_limit_bytes=48 * 2**20),
        cost_estimate=cost(experts * rows * sides / 560 * (2 if more else 1.7)),
        name="weight_gradient",
    )(rank.reshape(1).astype(jnp.int32), left, *[right for right, _ in shares], *more)
    return out if pieces else out[0]


def weight_grad_sends(left, rights, rows):
    count = lax.axis_size("dp")
    rank = lax.axis_index("dp")
    onward = [(d, (d + 1) % count) for d in range(count)]
    sent, arrived = [], []
    for e in range(left.shape[0]):
        more = []
        for step in range(1, count):
            parts = weight_grad(left, rights, (rank + count - step) % count, rows, e, 1, more, True)
            more = [lax.ppermute(part, "dp", onward) for part in parts]
        sent += parts if more else []
        arrived += more
    return sent, arrived


def unturn(grad, cosine, sine_part):
    return grad * cosine - jnp.roll(grad, HD // 2, axis=1) * sine_part


def unproject_kernel(
    grad_q_ref, grad_k_ref, grad_v_ref, raw_ref, squares_ref, dots_ref, gain_ref, cosine_ref, sine_ref,
    weight_ref, grad_ref, gain_terms_ref, out_ref,
):
    rows, _, width = out_ref.shape
    inverse = lax.rsqrt(squares_ref[...] / D + norm_epsilon)
    inner = inverse * inverse * dots_ref[:2] / D

    @pl.when(pl.program_id(0) == 0)
    def _():
        gain_terms_ref[...] = jnp.zeros_like(gain_terms_ref)

    for j, part_ref in ((0, grad_q_ref), (1, grad_k_ref)):
        grad = unturn(part_ref[...], cosine_ref[...], sine_ref[...])
        column = as_column(inverse[j : j + 1])
        raw = raw_ref[:, j * HD : (j + 1) * HD]
        gain_terms_ref[pl.ds(j, 1), :] += jnp.sum(grad * raw * column, axis=0, keepdims=True)
        back = column * grad * gain_ref[j : j + 1, :] - raw * as_column(inner[j : j + 1])
        grad_ref[:, pl.ds(j * HD, HD)] = back.astype(bf16)
    grad_ref[:, pl.ds(2 * HD, HD)] = grad_v_ref[...].astype(bf16)
    for row in range(rows):
        at = pl.ds(row * width, width)
        out_ref[row] = dot_nn(grad_ref[...], weight_ref[:, at]).astype(bf16)


def unproject(grads, raw, squares, dots, gain_pair, cosine, sine_part, weight_flip, rows, cols):
    length = raw.shape[0]
    block_rows, width = length // cols, D // rows
    tile = block_rows
    tall = pl.BlockSpec((tile, HD), lambda i: (i, 0))
    three = pl.BlockSpec((tile, 3 * HD), lambda i: (i, 0))
    pair = pl.BlockSpec((2, tile), lambda i: (0, i))
    trio = pl.BlockSpec((3, tile), lambda i: (0, i))
    fixed = pl.BlockSpec((2, HD), lambda i: (0, 0))
    return pl.pallas_call(
        unproject_kernel,
        grid=(length // tile,),
        in_specs=[
            tall, tall, tall, three, pair, trio, fixed, tall, tall,
            pl.BlockSpec(weight_flip.shape, lambda i: (0, 0)),
        ],
        out_specs=[
            three, fixed, pl.BlockSpec((rows, tile, width), lambda i: (i, 0, 0)),
        ],
        out_shape=[
            jax.ShapeDtypeStruct((length, 3 * HD), bf16),
            jax.ShapeDtypeStruct((2, HD), f32),
            jax.ShapeDtypeStruct((rows * cols, block_rows, width), bf16),
        ],
        compiler_params=pltpu.CompilerParams(vmem_limit_bytes=52 * 2**20),
        cost_estimate=cost(15.5),
        name="projection_backward",
    )(*grads, raw, squares, dots, gain_pair, cosine, sine_part, weight_flip)


def norm_back(values, inverse, gain_row, upstream, dot_total):
    scaled = upstream * gain_row
    return inverse[:, None] * scaled - values * (inverse**3 * dot_total / D)[:, None]


def dot(a, b):
    return jnp.dot(a, b, preferred_element_type=f32)


def einsum(spec, a, b):
    return jnp.einsum(spec, a, b, preferred_element_type=f32)


def on_device(
    layer_input,
    gains,
    qkv_weight,
    output_weight,
    router_weight,
    expand_weight,
    reduce_weight,
    routes,
    drop_order,
    prefix_len,
    cotangent,
):
    row_rank, col_rank = lax.axis_index("row"), lax.axis_index("col")
    rows, cols = lax.axis_size("row"), lax.axis_size("col")
    dp_count = lax.axis_size("dp")
    group = rows * cols
    res_rows, row_width = layer_input.shape
    col_width = qkv_weight.shape[2]
    seq_len = res_rows * cols
    tok_rows = res_rows // rows
    block_rank = col_rank * rows + row_rank
    expert_rank = row_rank * cols + col_rank
    expert_count = router_weight.shape[1]
    local_experts = expand_weight.shape[0]
    capacity = tok_rows * TOP // expert_count
    ring = Ring(rows, cols)
    gain_rows = gains.astype(f32)
    router_flip = router_weight.T

    paired = dp_count % 2 == 0
    half_rank = lax.axis_index("dp") % 2 if paired else 0
    partner = [(d, d ^ 1) for d in range(dp_count)]
    halves = 2 if paired else 1
    half_rows = row_width // halves
    head_half = lax.dynamic_slice_in_dim(qkv_weight, half_rank * half_rows, half_rows, 0)
    head_half = head_half.reshape(half_rows, 3, rows, HD).transpose(2, 0, 1, 3)
    head_half = exchange_rows(head_half.reshape(rows, half_rows, 3 * HD))
    half_width = HD // 2
    frequency = rope_base ** (-2.0 * jnp.arange(half_width, dtype=f32) / HD)
    angles = jnp.arange(seq_len).astype(f32)[:, None] * frequency[None, :]
    cosine, sine_part = jnp.cos(angles), jnp.sin(angles)
    cosine = jnp.concatenate([cosine, cosine], axis=1)
    sine_part = jnp.concatenate([-sine_part, sine_part], axis=1)
    own_lines = jnp.concatenate([routes.T, drop_order[None, :]], axis=0)
    lines = jnp.zeros((cols,) + own_lines.shape, jnp.int32)
    lines = lax.dynamic_update_slice(lines, own_lines[None], (col_rank, 0, 0))
    for step in range(1, cols):
        arrived = lax.ppermute(own_lines, "col", [(c, (c + step) % cols) for c in range(cols)])
        lines = lax.dynamic_update_slice(
            lines, arrived[None], ((col_rank + cols - step) % cols, 0, 0)
        )
    first_expert = expert_rank * local_experts
    own_experts = first_expert + jnp.arange(local_experts)
    member = jnp.any(lines[None, :, :TOP] == own_experts[:, None, None, None], axis=2)
    member = member.reshape(local_experts, group, tok_rows).transpose(1, 0, 2)
    drop_rank = lines[:, TOP].reshape(group, tok_rows)
    token_index = jnp.arange(tok_rows)
    earlier = (drop_rank[:, None, :] < drop_rank[:, :, None]) | (
        drop_rank[:, None, :] == drop_rank[:, :, None]
    ) & (token_index[None, None, :] < token_index[None, :, None])
    position = jnp.sum(jnp.where(earlier[:, None] & member[:, :, None, :], 1, 0), axis=-1)
    kept = member & (position < capacity)
    hits = kept[:, :, None, :] & (
        position[:, :, None, :] == jnp.arange(capacity)[None, None, :, None]
    )
    hits = hits.reshape(group, local_experts * capacity, tok_rows)
    dispatch = hits.astype(bf16)
    combine = hits.transpose(0, 2, 1).astype(bf16)

    weight_half = lax.dynamic_slice_in_dim(
        output_weight, half_rank * (col_width // 2), col_width // halves, 0
    )
    weight_mine = lax.all_gather(weight_half, BLOCKS, axis=0)
    by_core = weight_mine.reshape(
        ring.groups, ring.cores, rows, weight_half.shape[0], row_width
    )
    if paired:
        own_core = lax.dynamic_index_in_dim(by_core, ring.core, 1, False)
        own_core = own_core.reshape(ring.size, weight_half.shape[0], row_width)
        weight_theirs = ring.from_siblings(lax.ppermute(own_core, "dp", partner))
        weight_sets = [weight_mine] * ring.cores + weight_theirs
    else:
        weight_sets = [weight_mine[:, : col_width // 2]] * ring.cores
        weight_sets += [weight_mine[:, col_width // 2 :]] * ring.cores
    head_out = exchange_rows(output_weight.reshape(rows, col_width // rows, row_width))
    head_out = head_out.transpose(0, 2, 1).reshape(D, HD)
    at = [col_rank, row_rank]
    table = []
    for half in range(2):
        for k in range(ring.cores):
            for chip_group in range(ring.groups):
                col = chip_group * ring.cores + (ring.core + k) % ring.cores
                for row in range(rows):
                    whole_plane = half == 0 or not paired
                    table.append(col * rows + row if whole_plane else chip_group * rows + row)
    for chip_group in range(ring.groups):
        for half in range(2):
            for k in range(ring.cores):
                col = chip_group * ring.cores + (ring.core + k) % ring.cores
                at.append((col * 2 + (half_rank + half) % 2) * (rows // 2))
    at = jnp.stack([jnp.asarray(value, jnp.int32) for value in at])
    table = jnp.stack([jnp.asarray(value, jnp.int32) for value in table])

    x_steps = ring.gather_steps(layer_input)
    x_arrivals = [next(x_steps), next(x_steps)]
    pieces, head_half = together([piece for piece, _ in x_arrivals[-1]], head_half)
    x_arrivals[-1] = list(zip(pieces, [distance for _, distance in x_arrivals[-1]]))
    x_arrivals.append(x_steps.send(pieces))
    if paired:
        other_half = lax.ppermute(head_half, "dp", partner)
        pieces, other_half, head_out = together(
            [piece for piece, _ in x_arrivals[-1]], other_half, head_out
        )
        x_arrivals[-1] = list(zip(pieces, [distance for _, distance in x_arrivals[-1]]))
        head_weight = jnp.where(
            half_rank == 0,
            jnp.stack([head_half, other_half], axis=1),
            jnp.stack([other_half, head_half], axis=1),
        )
    else:
        head_weight = head_half
    x_arrivals += [x_steps.send(pieces), *x_steps]
    head_weight = head_weight.reshape(D, 3 * HD)
    weight_flip = head_weight.T
    x_blocks = unwritten((group,) + layer_input.shape, bf16)
    for arrival in x_arrivals:
        x_blocks = ring.place_blocks(x_blocks, ring.with_siblings(arrival))
    x_blocks, cosine, sine_part, dispatch, combine = together(
        x_blocks, cosine, sine_part, dispatch, combine
    )
    projected, inv_first, square_terms = project(x_blocks, gain_rows[0:1], head_weight, rows)
    squares = ring.small_sum(square_terms)

    head_first = block_rank * HD
    gain_pair = lax.dynamic_slice(gain_rows, (1, head_first), (2, HD))
    query_low, key_low, value_low, key_flip, value_flip = turn(
        projected, squares, gain_pair, cosine, sine_part
    )

    upstream_blocks = lax.all_gather(after(cotangent, x_blocks), BLOCKS, axis=0)
    query_rows = max(seq_len // 6, 128)
    attn_head, lse = attention(query_low, key_low, value_flip, prefix_len, query_rows)
    attn_tokens = exchange(attn_head.reshape(group, tok_rows, HD), BLOCKS)
    upstream_slots = dispatch_blocks(dispatch, upstream_blocks, rows, local_experts)
    residual, second_low = output_branch(
        at, table, attn_tokens, weight_sets, x_blocks, gain_rows[3:4], rows, ring.groups
    )
    feat_steps = ring.gather_steps(second_low)
    arrivals = [next(feat_steps), next(feat_steps)]
    grad_raw = einsum(
        "end,efd->enf", upstream_slots.reshape(local_experts, group * capacity, D), reduce_weight
    ).reshape(local_experts, group, capacity, F)
    pieces, upstream_slots = together([piece for piece, _ in arrivals[-1]], upstream_slots)
    arrivals[-1] = list(zip(pieces, [distance for _, distance in arrivals[-1]]))
    arrivals.append(feat_steps.send(pieces))
    pieces, grad_raw = together([piece for piece, _ in arrivals[-1]], grad_raw)
    arrivals[-1] = list(zip(pieces, [distance for _, distance in arrivals[-1]]))
    arrivals.append(feat_steps.send(pieces))

    carried = None
    waiting, feat_parts, places = [], {}, {}
    calls = {1: 0, ring.size // 2 - 2: 3, ring.size // 2: 1}
    start = {0: 0, 3: group - 2 * ring.cores, 1: 3 * ring.cores}
    for step in range(ring.size // 2 + 1):
        if step == len(arrivals):
            pieces, *carried = together([piece for piece, _ in arrivals[-1]], *carried)
            arrivals.append(feat_steps.send(pieces))
        arrival = arrivals[step]
        pairs = ring.with_siblings(arrival)
        for k, (_, distance) in enumerate(arrival):
            waiting.append((distance, pairs[k * ring.cores : (k + 1) * ring.cores]))
        if step not in calls:
            continue
        taken = [pair for _, chip in waiting for pair in chip]
        carried, feat_sums = run_experts(
            [block for block, _ in taken],
            [ident for _, ident in taken],
            first_expert,
            grad_raw,
            dispatch,
            combine,
            router_flip,
            expand_weight,
            carried,
            calls[step],
        )
        for k, (distance, chip) in enumerate(waiting):
            feat_parts[distance] = ring.chip_sum(*feat_sums[k * ring.cores : (k + 1) * ring.cores])
            for j, (_, ident) in enumerate(chip):
                places[start[calls[step]] + k * ring.cores + j] = (distance, ident)
        waiting.clear()
    slot_rows, hidden, grad_gate_pre, grad_up_pre, slot_gate = carried

    far = ring.size // 2
    feat_parts[far], slot_rows = together(feat_parts[far], slot_rows)
    grad_steps = ring.scatter_steps(lambda distance: feat_parts[distance])
    grad_terms = next(grad_steps)
    expand_sides = [grad_gate_pre, grad_up_pre]
    expand_sent, expand_arrived = weight_grad_sends(slot_rows, expand_sides, D // dp_count)
    grad_terms, expand_sent, hidden = together(grad_terms, expand_sent, hidden)
    grad_terms = grad_steps.send(grad_terms)
    expert_out = einsum("enf,efd->end", hidden, reduce_weight).astype(bf16)
    arriving, arrived = list(expand_arrived), []

    def taking(count, *values):
        taken, arriving[:count] = arriving[:count], []
        *values, taken = together(*values, taken)
        arrived.extend(taken)
        return values

    grad_terms, expert_out = taking(1, grad_terms, expert_out)
    grad_terms = grad_steps.send(grad_terms)
    ids = jnp.stack([places[k][1] for k in range(group)]).astype(jnp.int32)
    gate_tokens, grad_out_slots, moe_sums = combine_experts(
        ids, expert_out, upstream_slots, dispatch, combine, slot_gate
    )
    grad_out_slots = grad_out_slots.reshape(local_experts, group * capacity, D)
    grad_probs = exchange(gate_tokens, BLOCKS)
    grad_terms, grad_out_slots, moe_sums = taking(1, grad_terms, grad_out_slots, moe_sums)
    grad_terms = grad_steps.send(grad_terms)
    reduce_sent, reduce_arrived = weight_grad_sends(hidden, [grad_out_slots], F // dp_count)
    arriving += reduce_arrived
    grad_probs = grad_probs.reshape(cols, rows, local_experts, tok_rows)
    grad_probs = grad_probs.transpose(1, 0, 2, 3).reshape(expert_count, tok_rows)
    logits = dot_nt(router_flip, second_low)
    probs = jax.nn.softmax(logits, axis=0)
    grad_logits = probs * (grad_probs - jnp.sum(probs * grad_probs, axis=0, keepdims=True))
    grad_logits = grad_logits.T.astype(bf16)
    router_term = einsum("te,td->ed", grad_logits, second_low)
    while len(grad_terms) == 2:
        grad_terms = grad_steps.send(grad_terms)

    grad_branch, gain_second_term = residual_back(
        at[:2], grad_terms, grad_logits, router_flip, residual, upstream_blocks, gain_rows[3:4], rows
    )
    grad_branch, reduce_sent, router_term = taking(1, grad_branch, reduce_sent, router_term)
    branch_steps = ring.gather_steps(grad_branch)
    branch_arrivals = [next(branch_steps)]
    router_total = lax.psum(router_term, ("dp", "row", "col"))
    pieces = None
    for arrival in iter(lambda: branch_steps.send(pieces), None):
        pieces, = taking(1, [piece for piece, _ in arrival])
        branch_arrivals.append(list(zip(pieces, [distance for _, distance in arrival])))
        if len(branch_arrivals) == ring.size // 2 + 1:
            break
    branch_all = unwritten((group, tok_rows, D), bf16)
    for arrival in branch_arrivals:
        branch_all = ring.place_blocks(branch_all, ring.with_siblings(arrival))

    moe_tokens = lax.psum_scatter(
        after(moe_sums, branch_all), BLOCKS, scatter_dimension=0, tiled=False
    )
    grad_attn = dot(branch_all.reshape(seq_len, D), head_out).astype(bf16)
    centre = jnp.sum(attn_head.astype(f32) * grad_attn.astype(f32), axis=1)[None]
    *head_grads, dot_query, dot_key, dot_value = attention_back(
        query_low, key_low, key_flip, value_low, grad_attn, lse, centre, prefix_len, query_rows
    )
    dots = jnp.concatenate([dot_query, dot_key, dot_value], axis=0)
    dots, = taking(1, dots)
    dots = ring.small_sum(dots)

    grad_qkv, gain_pair_terms, grad_first_blocks = unproject(
        head_grads, projected, squares, dots, gain_pair, cosine, sine_part, weight_flip, rows, cols
    )
    grad_first_blocks, = taking(2, grad_first_blocks)

    def blocks_sum(blocks, distance):
        return ring.chip_sum(
            *[lax.dynamic_index_in_dim(blocks, ident, 0, False) for ident in ring.block_ids(distance)]
        )

    first_far = blocks_sum(grad_first_blocks, ring.size // 2)
    first_far, grad_first_blocks = together(first_far, grad_first_blocks)

    def first_part(distance):
        return first_far if distance == ring.size // 2 else blocks_sum(grad_first_blocks, distance)

    first_steps = ring.scatter_steps(first_part)
    grad_first = next(first_steps)
    grad_first, grad_qkv = together(grad_first, grad_qkv)
    grad_first = first_steps.send(grad_first)
    qkv_term = project_weight(x_blocks, gain_rows[0:1], inv_first, grad_qkv, rows)
    grad_first, qkv_term = taking(1, grad_first, qkv_term)
    grad_first = first_steps.send(grad_first)
    rank = lax.axis_index("dp")
    expand_grad = weight_grad(
        slot_rows, expand_sides, rank, D // dp_count, more=arrived[: len(expand_arrived)]
    )
    layer_tokens = (residual + moe_tokens.astype(f32)).astype(bf16)
    layer_output = lax.all_to_all(layer_tokens, "row", split_axis=1, concat_axis=0, tiled=True)
    grad_first, expand_grad, layer_output = taking(
        len(arriving), grad_first, expand_grad, layer_output
    )
    grad_first = first_steps.send(grad_first)
    output_term = dot(attn_head.T, branch_all.reshape(seq_len, D))
    output_term = output_term.astype(bf16).reshape(HD, rows, row_width).transpose(1, 0, 2)
    output_sum = exchange_rows(output_term).reshape(col_width, row_width)
    reduce_grad = weight_grad(
        hidden, [grad_out_slots], rank, F // dp_count, more=arrived[len(expand_arrived) :]
    )
    grad_first, output_sum, reduce_grad = together(grad_first, output_sum, reduce_grad)
    grad_first = first_steps.send(grad_first)
    grad_first = sum(term.astype(f32) for term in grad_first)
    grad_block = lax.dynamic_slice(
        branch_all, (col_rank * rows, 0, row_rank * row_width), (rows, tok_rows, row_width)
    ).reshape(res_rows, row_width)
    inverse = lax.rsqrt(squares / D + norm_epsilon)
    dot_first = dots[2] + norm_epsilon * jnp.sum(dots[:2] * inverse, axis=0)
    dot_first = dot_first / inv_first[0]
    own_first = col_rank * res_rows
    dot_first = lax.dynamic_slice_in_dim(dot_first, own_first, res_rows)
    inv_block = lax.dynamic_slice_in_dim(inv_first[0], own_first, res_rows)
    gain_block = lax.dynamic_slice_in_dim(gain_rows[0], row_rank * row_width, row_width)
    input_grad = grad_block.astype(f32) + norm_back(
        layer_input.astype(f32), inv_block, gain_block, grad_first, dot_first
    )

    output_rows = col_width // dp_count
    output_grad = dp_sum(
        lambda rank: lax.dynamic_slice_in_dim(
            output_sum, rank * output_rows, output_rows, 0
        ).astype(f32)
    )
    gain_first_term = jnp.sum(qkv_term * head_weight.astype(f32), axis=1) / gain_rows[0]
    qkv_rows = row_width // dp_count
    qkv_shaped = qkv_term.reshape(rows, row_width, 3 * HD)
    qkv_sum = dp_sum(
        lambda rank: lax.dynamic_slice_in_dim(qkv_shaped, rank * qkv_rows, qkv_rows, 1)
    )
    qkv_grad = exchange_rows(qkv_sum.astype(bf16)).reshape(rows, qkv_rows, 3, HD)
    qkv_grad = qkv_grad.transpose(1, 2, 0, 3).reshape(1, qkv_rows, 3, col_width).astype(f32)

    def placed(term):
        return lax.dynamic_update_slice(jnp.zeros((D,), f32), term, (head_first,))

    gain_total = dp_all_sum(
        ring.small_sum(
            jnp.concatenate(
                [
                    jnp.stack(
                        [gain_first_term, placed(gain_pair_terms[0]), placed(gain_pair_terms[1])]
                    ),
                    gain_second_term,
                ],
                axis=0,
            )
        )
    )
    router_total = router_total.T
    return (
        layer_output,
        input_grad.astype(bf16),
        gain_total,
        qkv_grad,
        output_grad[None],
        router_total,
        expand_grad,
        reduce_grad,
    )


def solution(mesh):
    return jax.shard_map(
        on_device,
        mesh=mesh,
        in_specs=(
            P(("dp", "col"), "row"),
            P(),
            P("row", None, "col"),
            P("col", "row"),
            P(),
            P(("row", "col"), None, None),
            P(("row", "col"), None, None),
            P(("dp", "col"), None),
            P(("dp", "col")),
            P("dp"),
            P(("dp", "col"), "row"),
        ),
        out_specs=(
            P(("dp", "col"), "row"),
            P(("dp", "col"), "row"),
            P(),
            P("row", "dp", None, "col"),
            P("col", "dp", "row"),
            P(),
            P(("row", "col"), "dp", None),
            P(("row", "col"), "dp", None),
        ),
        check_vma=False,
    )
```

```python
import functools
import math

import jax
import jax.numpy as jnp
from jax import lax
from jax.experimental import pallas as pl
from jax.experimental.pallas import tpu as pltpu
from jax.sharding import PartitionSpec as P

D = 2048
HD = 128
F = 1024
TOP = 8
CORES = 2
PLANE = ("row", "col")
BLOCKS = ("col", "row")
LOG2E = math.log2(math.e)
MASKED = -1e30
COST_SHARE = 0.2

norm_epsilon = 1e-05
rope_base = 10000.0
bf16 = jnp.bfloat16
f32 = jnp.float32


def dot_nt(a, b):
    return lax.dot_general(a, b, (((1,), (1,)), ((), ())), preferred_element_type=f32)


def dot_nn(a, b):
    return lax.dot_general(a, b, (((1,), (0,)), ((), ())), preferred_element_type=f32)


def cost(microseconds):
    return pl.CostEstimate(
        flops=int(microseconds * 1.1e9 * COST_SHARE), bytes_accessed=0, transcendentals=0
    )


def as_row(column):
    return jnp.broadcast_to(column, (column.shape[0], 128)).T[:1]


def as_column(row):
    return jnp.broadcast_to(row, (8, row.shape[1])).T[:, :1]


def key_limits(first_query, query_rows, key_rows, prefix):
    open_blocks = jnp.maximum((first_query + 1) // key_rows, prefix // key_rows)
    all_blocks = pl.cdiv(jnp.maximum(first_query + query_rows, prefix), key_rows)
    return open_blocks, all_blocks


def mask_scores(scores, first_key, first_query, prefix):
    keys = first_key + lax.broadcasted_iota(jnp.int32, scores.shape, 0)
    queries = first_query + lax.broadcasted_iota(jnp.int32, scores.shape, 1)
    return jnp.where((keys <= queries) | (keys < prefix), scores, MASKED)


def attention_kernel(scale, prefix_ref, q_ref, k_ref, v_flip_ref, out_ref, lse_ref, scores_ref):
    query_rows = q_ref.shape[0]
    key_rows = min(512, k_ref.shape[0])
    first_query = pl.program_id(0) * query_rows
    prefix = prefix_ref[0]
    q = q_ref[...]
    open_blocks, all_blocks = key_limits(first_query, query_rows, key_rows, prefix)

    def score(j, top, masked):
        start = pl.multiple_of(j * key_rows, key_rows)
        scores = dot_nt(k_ref[pl.ds(start, key_rows), :], q) * (scale * LOG2E)
        if masked:
            scores = mask_scores(scores, start, first_query, prefix)
        scores_ref[pl.ds(start, key_rows), :] = scores
        return jnp.maximum(top, jnp.max(scores.reshape(key_rows // 8, 8, query_rows), axis=0))

    top = jnp.full((8, query_rows), MASKED, f32)
    top = lax.fori_loop(0, open_blocks, lambda j, t: score(j, t, False), top)
    top = lax.fori_loop(open_blocks, all_blocks, lambda j, t: score(j, t, True), top)
    peak = jnp.max(top, axis=0, keepdims=True)

    def mix(j, carry):
        total, mixed = carry
        start = pl.multiple_of(j * key_rows, key_rows)
        weights = jnp.exp2(scores_ref[pl.ds(start, key_rows), :] - peak)
        total = total + jnp.sum(weights.reshape(key_rows // 8, 8, query_rows), axis=0)
        mixed = mixed + dot_nn(v_flip_ref[:, pl.ds(start, key_rows)], weights.astype(bf16))
        return total, mixed

    total, mixed = lax.fori_loop(
        0,
        all_blocks,
        mix,
        (jnp.zeros((8, query_rows), f32), jnp.zeros((q.shape[1], query_rows), f32)),
    )
    total = jnp.sum(total, axis=0, keepdims=True)
    out_ref[...] = (mixed / total).T.astype(out_ref.dtype)
    lse_ref[...] = peak + jnp.log2(total)


def attention(q, k, v_flip, prefix_len, query_rows):
    length, width = q.shape
    query_block = pl.BlockSpec((query_rows, width), lambda i, p: (i, 0))
    return pl.pallas_call(
        functools.partial(attention_kernel, width**-0.5),
        grid_spec=pltpu.PrefetchScalarGridSpec(
            num_scalar_prefetch=1,
            grid=(length // query_rows,),
            in_specs=[
                query_block,
                pl.BlockSpec((length, width), lambda i, p: (0, 0)),
                pl.BlockSpec((width, length), lambda i, p: (0, 0)),
            ],
            out_specs=[query_block, pl.BlockSpec((1, query_rows), lambda i, p: (0, i))],
            scratch_shapes=[pltpu.VMEM((length, query_rows), f32)],
        ),
        out_shape=[
            jax.ShapeDtypeStruct((length, width), bf16),
            jax.ShapeDtypeStruct((1, length), f32),
        ],
        compiler_params=pltpu.CompilerParams(vmem_limit_bytes=40 * 2**20),
        cost_estimate=cost(17),
        name="attention_forward",
    )(prefix_len, q, k, v_flip)


def attention_back_kernel(
    scale, prefix_ref, q_ref, grad_ref, lse_ref, centre_ref, k_ref, k_flip_ref, v_ref,
    grad_q_ref, dot_q_ref, grad_k_ref, grad_v_ref, dot_k_ref, dot_v_ref,
):
    query_rows = q_ref.shape[0]
    key_rows = min(512, k_ref.shape[0])
    step = pl.program_id(0)
    first_query = step * query_rows
    prefix = prefix_ref[0]

    @pl.when(step == 0)
    def _():
        grad_k_ref[...] = jnp.zeros_like(grad_k_ref)
        grad_v_ref[...] = jnp.zeros_like(grad_v_ref)

    q = q_ref[...]
    grad = grad_ref[...]
    lse = lse_ref[...]
    centre = centre_ref[...]
    open_blocks, all_blocks = key_limits(first_query, query_rows, key_rows, prefix)

    def block(j, total, masked):
        start = pl.multiple_of(j * key_rows, key_rows)
        rows = pl.ds(start, key_rows)
        scores = dot_nt(k_ref[rows, :], q) * (scale * LOG2E) - lse
        if masked:
            scores = mask_scores(scores, start, first_query, prefix)
        weights = jnp.exp2(scores)
        grad_weights = dot_nt(v_ref[rows, :], grad)
        grad_scores = (weights * (grad_weights - centre)).astype(bf16)
        grad_v_ref[rows, :] += dot_nn(weights.astype(bf16), grad)
        grad_k_ref[rows, :] += dot_nn(grad_scores, q)
        return total + dot_nn(k_flip_ref[:, rows], grad_scores)

    total = jnp.zeros((q.shape[1], query_rows), f32)
    total = lax.fori_loop(0, open_blocks, lambda j, a: block(j, a, False), total)
    total = lax.fori_loop(open_blocks, all_blocks, lambda j, a: block(j, a, True), total)
    grad_q = total.T * scale
    grad_q_ref[...] = grad_q
    dot_q_ref[...] = as_row(jnp.sum(grad_q * q.astype(f32), axis=1, keepdims=True))

    @pl.when(step == pl.num_programs(0) - 1)
    def _():
        for start in range(0, k_ref.shape[0], key_rows):
            rows = pl.ds(start, key_rows)
            grad_k = grad_k_ref[rows, :] * scale
            grad_k_ref[rows, :] = grad_k
            dot_k_ref[:, rows] = as_row(
                jnp.sum(grad_k * k_ref[rows, :].astype(f32), axis=1, keepdims=True)
            )
            dot_v_ref[:, rows] = as_row(
                jnp.sum(grad_v_ref[rows, :] * v_ref[rows, :].astype(f32), axis=1, keepdims=True)
            )


def attention_back(q, k, k_flip, v, grad, lse, centre, prefix_len, query_rows):
    length, width = q.shape
    whole = pl.BlockSpec((length, width), lambda i, p: (0, 0))
    flipped = pl.BlockSpec((width, length), lambda i, p: (0, 0))
    query_block = pl.BlockSpec((query_rows, width), lambda i, p: (i, 0))
    query_row = pl.BlockSpec((1, query_rows), lambda i, p: (0, i))
    key_row = pl.BlockSpec((1, length), lambda i, p: (0, 0))
    result = jax.ShapeDtypeStruct((length, width), f32)
    line = jax.ShapeDtypeStruct((1, length), f32)
    return pl.pallas_call(
        functools.partial(attention_back_kernel, width**-0.5),
        grid_spec=pltpu.PrefetchScalarGridSpec(
            num_scalar_prefetch=1,
            grid=(length // query_rows,),
            in_specs=[query_block, query_block, query_row, query_row, whole, flipped, whole],
            out_specs=[query_block, query_row, whole, whole] + [key_row] * 2,
        ),
        out_shape=[result, line, result, result] + [line] * 2,
        compiler_params=pltpu.CompilerParams(vmem_limit_bytes=40 * 2**20),
        cost_estimate=cost(24),
        name="attention_backward",
    )(prefix_len, q, grad, lse, centre, k, k_flip, v)


def unwritten(shape, dtype):
    return pl.pallas_call(
        lambda out_ref: None,
        out_specs=pl.BlockSpec(memory_space=pl.ANY),
        out_shape=jax.ShapeDtypeStruct(shape, dtype),
        name="buffer",
    )()


def add_low(one, two):
    return (one.astype(f32) + two.astype(f32)).astype(bf16)


def step_sum_kernel(counts, halved, ids_ref, *refs):
    half = pl.program_id(0)
    parts, (forth_ref, back_ref, ahead_ref, behind_ref) = refs[:-4], refs[-4:]
    for start, came_ref, out_ref, at in (
        (0, forth_ref, ahead_ref, 0),
        (counts[0], back_ref, behind_ref, 1),
    ):
        count = counts[at]
        total = sum(ref[0].astype(f32) for ref in parts[start : start + count])
        if not halved:
            out_ref[...] = (total + came_ref[...].astype(f32)).astype(bf16)
            continue

        @pl.when(half == at)
        def _():
            out_ref[...] = (total + came_ref[...].astype(f32)).astype(bf16)

        @pl.when(half != at)
        def _():
            out_ref[...] = total.astype(bf16)


def step_sum(ahead, behind, forth, back):
    parts = [(array if array.ndim == 3 else array[None], place) for array, place in ahead + behind]
    ids = jnp.stack([jnp.asarray(place, jnp.int32) for _, place in parts])
    _, rows, width = parts[0][0].shape
    tile = rows // 2
    halved = forth.shape[0] != rows
    came = pl.BlockSpec((tile, width), (lambda i, ids: (0, 0)) if halved else (lambda i, ids: (i, 0)))
    whole = pl.BlockSpec((tile, width), lambda i, ids: (i, 0))
    return pl.pallas_call(
        functools.partial(step_sum_kernel, (len(ahead), len(behind)), halved),
        grid_spec=pltpu.PrefetchScalarGridSpec(
            num_scalar_prefetch=1,
            grid=(2,),
            in_specs=[
                pl.BlockSpec((1, tile, width), lambda i, ids, k=k: (ids[k], i, 0))
                for k in range(len(parts))
            ]
            + [came, came],
            out_specs=[whole, whole],
        ),
        out_shape=[jax.ShapeDtypeStruct((rows, width), bf16)] * 2,
        cost_estimate=cost(3),
        name="step_sum",
    )(ids, *[array for array, _ in parts], forth, back)


def block_sum(parts):
    total = 0.0
    for array, place in parts:
        block = array if array.ndim == 2 else lax.dynamic_index_in_dim(array, place, 0, False)
        total = total + block.astype(f32)
    return total.astype(bf16)


def after(value, earlier):
    return lax.optimization_barrier((value, earlier))[0]


def together(*values):
    return lax.optimization_barrier(values)


class Ring:
    def __init__(self, rows, cols):
        self.rows, self.cols = rows, cols
        self.cores = CORES if cols % CORES == 0 else 1
        self.groups = cols // self.cores
        self.order = [
            (row, group)
            for group in range(self.groups)
            for row in (range(rows) if group % 2 == 0 else range(rows - 1, -1, -1))
        ]
        self.size = len(self.order)
        self.clockwise = self.shift(1)
        self.counter = self.shift(-1)
        self.sibling = [
            (row * cols + col, row * cols + col - col % self.cores + (col + 1) % self.cores)
            for row in range(rows)
            for col in range(cols)
        ]
        row, col = lax.axis_index("row"), lax.axis_index("col")
        group = col // self.cores
        self.core = col % self.cores
        self.place = group * rows + jnp.where(group % 2 == 0, row, rows - 1 - row)

    def shift(self, step):
        pairs = []
        for at, (row, group) in enumerate(self.order):
            to_row, to_group = self.order[(at + step) % self.size]
            for core in range(self.cores):
                pairs.append(
                    (
                        row * self.cols + group * self.cores + core,
                        to_row * self.cols + to_group * self.cores + core,
                    )
                )
        return pairs

    def chip(self, distance):
        at = (self.place + distance + self.size) % self.size
        group = at // self.rows
        along = at % self.rows
        return jnp.where(group % 2 == 0, along, self.rows - 1 - along), group

    def owners(self, distance):
        row, group = self.chip(distance)
        return [(row, group * self.cores + (self.core + k) % self.cores) for k in range(self.cores)]

    def block_ids(self, distance):
        return [col * self.rows + row for row, col in self.owners(distance)]

    def from_siblings(self, block):
        return [block] + [lax.ppermute(block, PLANE, self.sibling)] * (self.cores - 1)

    def gather_steps(self, block):
        forth = back = block
        yield [(block, 0)]
        for step in range(1, (self.size + 1) // 2):
            forth = lax.ppermute(forth, PLANE, self.clockwise)
            back = lax.ppermute(back, PLANE, self.counter)
            sent = yield [(forth, -step), (back, step)]
            if sent is not None:
                forth, back = sent
        if self.size % 2 == 0:
            half = block.shape[0] // 2
            forth = lax.ppermute(forth[:half], PLANE, self.clockwise)
            back = lax.ppermute(back[half:], PLANE, self.counter)
            yield [(jnp.concatenate([forth, back], axis=0), self.size // 2)]

    def with_siblings(self, arrival):
        return [
            pair
            for piece, distance in arrival
            for pair in zip(self.from_siblings(piece), self.block_ids(distance))
        ]

    def place_blocks(self, box, pairs):
        blocks, ids = zip(*pairs)
        count = len(blocks)

        def kernel(ids_ref, *refs):
            step = pl.program_id(0)
            for k in range(count):

                @pl.when(step == k)
                def _():
                    refs[-1][0] = refs[k][...]

        whole = pl.BlockSpec(blocks[0].shape, lambda i, ids: (0,) * blocks[0].ndim)
        return pl.pallas_call(
            kernel,
            grid_spec=pltpu.PrefetchScalarGridSpec(
                num_scalar_prefetch=1,
                grid=(count,),
                in_specs=[whole] * count + [pl.BlockSpec(memory_space=pl.ANY)],
                out_specs=pl.BlockSpec(
                    (1,) + blocks[0].shape, lambda i, ids: (ids[i],) + (0,) * blocks[0].ndim
                ),
            ),
            out_shape=jax.ShapeDtypeStruct(box.shape, box.dtype),
            input_output_aliases={count + 1: 0},
            cost_estimate=cost(count),
            name="place_blocks",
        )(jnp.stack(ids).astype(jnp.int32), *blocks, box)

    def gather_array(self, block):
        box = unwritten((self.rows * self.cols,) + block.shape, block.dtype)
        for arrival in self.gather_steps(block):
            box = self.place_blocks(box, self.with_siblings(arrival))
        return box

    def for_siblings(self, *others):
        return [lax.ppermute(other, PLANE, self.sibling) for other in others]

    def scatter(self, parts):
        return Scatter(self, parts)

    def sum_steps(self, values, kind=f32):
        rows, cols = self.rows, self.cols
        if rows & (rows - 1) or cols & (cols - 1):
            yield lax.psum(values, PLANE)
            return
        swaps = []
        bit = 1
        while bit < cols:
            swaps.append(lambda row, col, bit=bit: (row, col ^ bit))
            bit *= 2
        bit = 1
        while bit < rows:
            swaps.append(lambda row, col, bit=bit: (row ^ bit, col))
            bit *= 2
        for swap in swaps:
            pairs = []
            for row in range(rows):
                for col in range(cols):
                    to_row, to_col = swap(row, col)
                    pairs.append((row * cols + col, to_row * cols + to_col))
            sent = values.astype(kind)
            values = sent.astype(f32) + lax.ppermute(sent, PLANE, pairs).astype(f32)
            yield values

    def small_sum(self, values):
        *_, last = self.sum_steps(values)
        return last


class Scatter:
    def __init__(self, ring, parts):
        self.ring, self.parts = ring, parts
        self.step = ring.size // 2
        self.going = None

    def ready(self):
        ring, step = self.ring, self.step
        if 2 * step == ring.size:
            far = block_sum(self.parts(step))
            half = far.shape[0] // 2
            self.going = far[:half], far[half:]
        elif self.going is None:
            self.going = block_sum(self.parts(step)), block_sum(self.parts(-step))
        else:
            self.going = tuple(step_sum(self.parts(step), self.parts(-step), *self.going))

    def move(self):
        forth, back = self.going
        self.going = (
            lax.ppermute(forth, PLANE, self.ring.clockwise),
            lax.ppermute(back, PLANE, self.ring.counter),
        )
        self.step -= 1

    def tie(self, *values):
        self.going, *values = together(self.going, *values)
        return values

    def total(self):
        own = [
            array if array.ndim == 2 else lax.dynamic_index_in_dim(array, place, 0, False)
            for array, place in self.parts(0)
        ]
        return *own, *self.going


def dp_sum(part):
    count = lax.axis_size("dp")
    rank = lax.axis_index("dp")
    if count == 1:
        return part(rank)
    onward = [(d, (d + 1) % count) for d in range(count)]
    total = part((rank + count - 1) % count)
    for step in range(1, count):
        arrived = lax.ppermute(total.astype(bf16), "dp", onward)
        total = part((rank + 2 * count - 1 - step) % count) + arrived.astype(f32)
    return total


def dp_all_sum(values, kind=f32):
    count = lax.axis_size("dp")
    if count & (count - 1):
        return lax.psum(values, "dp")
    bit = 1
    while bit < count:
        sent = values.astype(kind)
        swapped = lax.ppermute(sent, "dp", [(d, d ^ bit) for d in range(count)])
        values = sent.astype(f32) + swapped.astype(f32)
        bit *= 2
    return values


def exchange_rows(pieces):
    rows = pieces.shape[0]
    row = lax.axis_index("row")
    start = lambda at: (at,) + (0,) * (pieces.ndim - 1)
    taken = unwritten(pieces.shape, pieces.dtype)
    own = lax.dynamic_index_in_dim(pieces, row, 0, True)
    taken = lax.dynamic_update_slice(taken, own, start(row))
    for step in range(1, rows):
        sent = lax.dynamic_index_in_dim(pieces, (row + step) % rows, 0, True)
        sent = lax.ppermute(sent, "row", [(r, (r + step) % rows) for r in range(rows)])
        taken = lax.dynamic_update_slice(taken, sent, start((row + rows - step) % rows))
    return taken


def exchange(pieces, axes):
    return lax.all_to_all(pieces, axes, split_axis=0, concat_axis=0, tiled=True)


def project_kernel(x_ref, gain_ref, weight_ref, out_ref, inverse_ref, squares_ref, low_ref):
    blocks, _, width = x_ref.shape
    total = 0.0
    for block in range(blocks):
        part = x_ref[block].astype(f32)
        total = total + jnp.sum(part * part, axis=1, keepdims=True)
    inverse = lax.rsqrt(total / D + norm_epsilon)
    for block in range(blocks):
        at = pl.ds(block * width, width)
        low_ref[:, at] = (x_ref[block].astype(f32) * inverse * gain_ref[:, at]).astype(bf16)
    out = dot_nn(low_ref[...], weight_ref[...])
    out_ref[...] = out
    inverse_ref[...] = as_row(inverse)
    for j in range(2):
        part = out[:, j * HD : (j + 1) * HD]
        squares_ref[pl.ds(j, 1), :] = as_row(jnp.sum(part * part, axis=1, keepdims=True))


def project(x_blocks, block_rows, gain_row, weight, rows):
    count, _, width = x_blocks.shape
    cols = count // rows
    tile = block_rows
    per = block_rows // tile
    length = cols * block_rows
    return pl.pallas_call(
        project_kernel,
        grid=(cols * per,),
        in_specs=[
            pl.BlockSpec((rows, tile, width), lambda i: (i // per, i % per, 0)),
            pl.BlockSpec((1, D), lambda i: (0, 0)),
            pl.BlockSpec(weight.shape, lambda i: (0, 0)),
        ],
        out_specs=[
            pl.BlockSpec((tile, 3 * HD), lambda i: (i, 0)),
            pl.BlockSpec((1, tile), lambda i: (0, i)),
            pl.BlockSpec((2, tile), lambda i: (0, i)),
        ],
        scratch_shapes=[pltpu.VMEM((tile, D), bf16)],
        out_shape=[
            jax.ShapeDtypeStruct((length, 3 * HD), f32),
            jax.ShapeDtypeStruct((1, length), f32),
            jax.ShapeDtypeStruct((2, length), f32),
        ],
        compiler_params=pltpu.CompilerParams(vmem_limit_bytes=52 * 2**20),
        cost_estimate=cost(14),
        name="norm_and_project",
    )(x_blocks, gain_row, weight)


def project_weight_kernel(x_ref, gain_ref, inverse_ref, grad_ref, weight_ref, out_ref, term_ref, low_ref):
    blocks, _, width = x_ref.shape
    inverse = as_column(inverse_ref[...])

    @pl.when(pl.program_id(0) == 0)
    def _():
        out_ref[...] = jnp.zeros_like(out_ref)

    for block in range(blocks):
        at = pl.ds(block * width, width)
        low_ref[:, at] = (x_ref[block].astype(f32) * inverse * gain_ref[:, at]).astype(bf16)
    for block in range(blocks):
        at = pl.ds(block * width, width)
        total = dot_nn(low_ref[:, at].T, grad_ref[...])
        for j in range(3):
            out_ref[block, j] += total[:, j * HD : (j + 1) * HD]

    @pl.when(pl.program_id(0) == pl.num_programs(0) - 1)
    def _():
        for block in range(blocks):
            at = pl.ds(block * width, width)
            total = 0.0
            for j in range(3):
                total = total + out_ref[block, j] * weight_ref[at, j * HD : (j + 1) * HD].astype(f32)
            total = as_row(jnp.sum(total, axis=1, keepdims=True))
            term_ref[:, at] = total / gain_ref[:, at]


def project_weight(x_blocks, block_rows, gain_row, inverse, grads, weight, rows):
    count, _, width = x_blocks.shape
    cols = count // rows
    tile = block_rows // 3 if block_rows % 384 == 0 else block_rows
    per = block_rows // tile
    return pl.pallas_call(
        project_weight_kernel,
        grid=(cols * per,),
        in_specs=[
            pl.BlockSpec((rows, tile, width), lambda i: (i // per, i % per, 0)),
            pl.BlockSpec((1, D), lambda i: (0, 0)),
            pl.BlockSpec((1, tile), lambda i: (0, i)),
            pl.BlockSpec((tile, 3 * HD), lambda i: (i, 0)),
            pl.BlockSpec(weight.shape, lambda i: (0, 0)),
        ],
        out_specs=[
            pl.BlockSpec((rows, 3, width, HD), lambda i: (0, 0, 0, 0)),
            pl.BlockSpec((1, D), lambda i: (0, 0)),
        ],
        scratch_shapes=[pltpu.VMEM((tile, D), bf16)],
        out_shape=[
            jax.ShapeDtypeStruct((rows, 3, width, HD), f32),
            jax.ShapeDtypeStruct((1, D), f32),
        ],
        compiler_params=pltpu.CompilerParams(vmem_limit_bytes=40 * 2**20),
        cost_estimate=cost(15),
        name="projection_weight_gradient",
    )(x_blocks, gain_row, inverse, grads, weight)


def turn_kernel(raw_ref, squares_ref, gain_ref, cosine_ref, sine_ref, q_ref, k_ref, v_ref, k_flip_ref, v_flip_ref):
    inverse = lax.rsqrt(squares_ref[...] / D + norm_epsilon)
    for j, out_ref in ((0, q_ref), (1, k_ref)):
        normed = raw_ref[:, j * HD : (j + 1) * HD] * as_column(inverse[j : j + 1]) * gain_ref[j : j + 1, :]
        turned = normed * cosine_ref[...] + jnp.roll(normed, HD // 2, axis=1) * sine_ref[...]
        out_ref[...] = turned.astype(bf16)
        if j == 1:
            k_flip_ref[...] = turned.T.astype(bf16)
    v = raw_ref[:, 2 * HD :]
    v_ref[...] = v.astype(bf16)
    v_flip_ref[...] = v.T.astype(bf16)


def turn(raw, squares, gain_pair, cosine, sine_part):
    length = raw.shape[0]
    tile = min(1024, length)
    tall = pl.BlockSpec((tile, HD), lambda i: (i, 0))
    wide = pl.BlockSpec((HD, tile), lambda i: (0, i))
    tall_shape = jax.ShapeDtypeStruct((length, HD), bf16)
    wide_shape = jax.ShapeDtypeStruct((HD, length), bf16)
    return pl.pallas_call(
        turn_kernel,
        grid=(length // tile,),
        in_specs=[
            pl.BlockSpec((tile, 3 * HD), lambda i: (i, 0)),
            pl.BlockSpec((2, tile), lambda i: (0, i)),
            pl.BlockSpec((2, HD), lambda i: (0, 0)),
            tall,
            tall,
        ],
        out_specs=[tall, tall, tall, wide, wide],
        out_shape=[tall_shape, tall_shape, tall_shape, wide_shape, wide_shape],
        cost_estimate=cost(7.4),
        name="query_key_value",
    )(raw, squares, gain_pair, cosine, sine_part)


def branch_kernel(
    groups, sets, at_ref, heads_ref, x_ref, gain_ref, *refs
):
    weights, (residual_ref, low_ref) = refs[: groups * sets], refs[groups * sets :]
    step = pl.program_id(0)
    rows, width = x_ref.shape[0], x_ref.shape[2]
    height = weights[0].shape[1]
    per = height // HD
    branch = x_ref[pl.ds(step, 1)][0].astype(f32)
    for group in range(groups):
        for k in range(sets):
            first = at_ref[2 + group * sets + k]
            heads = jnp.concatenate([heads_ref[first + j] for j in range(per)], axis=1)
            branch = branch + dot_nn(heads, weights[group * sets + k][0])
    residual_ref[:, pl.ds(pl.multiple_of(step * width, width), width)] = branch

    @pl.when(step == rows - 1)
    def _():
        total = residual_ref[...]
        inverse = lax.rsqrt(jnp.sum(total * total, axis=1, keepdims=True) / D + norm_epsilon)
        low_ref[...] = (total * inverse * gain_ref[...]).astype(bf16)


def output_branch(at, table, heads, weight_sets, x_blocks, gain_row, rows, groups):
    tok_rows = heads.shape[1]
    sets = len(weight_sets)
    width = x_blocks.shape[2]
    height = D // (2 * rows)
    fixed = lambda shape: pl.BlockSpec(shape, lambda i, a, t: (0,) * len(shape))
    return pl.pallas_call(
        lambda at_ref, table_ref, *refs: branch_kernel(groups, sets, at_ref, *refs),
        grid_spec=pltpu.PrefetchScalarGridSpec(
            num_scalar_prefetch=2,
            grid=(rows,),
            in_specs=[
                fixed(heads.shape),
                pl.BlockSpec((rows, tok_rows, width), lambda i, a, t: (a[0], a[1], 0)),
                fixed((1, D)),
            ]
            + [
                pl.BlockSpec(
                    (1, height, width),
                    lambda i, a, t, g=g, k=k, half=half: (t[(k * groups + g) * rows + i], half, 0),
                )
                for g in range(groups)
                for k, (_, half) in enumerate(weight_sets)
            ],
            out_specs=[fixed((tok_rows, D)), fixed((tok_rows, D))],
        ),
        out_shape=[
            jax.ShapeDtypeStruct((tok_rows, D), f32),
            jax.ShapeDtypeStruct((tok_rows, D), bf16),
        ],
        compiler_params=pltpu.CompilerParams(vmem_limit_bytes=40 * 2**20),
        cost_estimate=cost(6),
        name="output_projection",
    )(at, table, heads, x_blocks, gain_row, *[w for _ in range(groups) for w, _ in weight_sets])


def resid_kernel(
    at_ref, logit_ref, router_ref, residual_ref, up_ref, gain_ref, *refs,
):
    terms, (grad_low_ref, gain_term_ref) = refs[:-2], refs[-2:]
    rows, width = up_ref.shape[0], up_ref.shape[2]
    grad = sum(ref[...].astype(f32) for ref in terms)
    grad = grad + dot_nn(logit_ref[...], router_ref[...])
    residual = residual_ref[...]
    inverse = lax.rsqrt(jnp.sum(residual * residual, axis=1, keepdims=True) / D + norm_epsilon)
    scaled = grad * gain_ref[...]
    total = jnp.sum(scaled * residual, axis=1, keepdims=True)
    gain_term_ref[...] = jnp.sum(grad * residual * inverse, axis=0, keepdims=True)
    back = inverse * scaled - residual * (inverse * inverse * inverse * total / D)
    for row in range(rows):
        at = pl.ds(row * width, width)
        grad_low_ref[:, at] = (
            up_ref[row].astype(f32) + back[:, row * width : (row + 1) * width]
        ).astype(bf16)


def residual_back(at, terms, grad_logits, router_flip, residual, up_blocks, gain_row, rows):
    tok_rows = residual.shape[0]
    width = up_blocks.shape[2]
    fixed = lambda shape: pl.BlockSpec(shape, lambda i, a: (0,) * len(shape))
    whole, line = fixed((tok_rows, D)), fixed((1, D))
    return pl.pallas_call(
        resid_kernel,
        grid_spec=pltpu.PrefetchScalarGridSpec(
            num_scalar_prefetch=1,
            grid=(1,),
            in_specs=[
                fixed(grad_logits.shape),
                fixed(router_flip.shape),
                whole,
                pl.BlockSpec((rows, tok_rows, width), lambda i, a: (a[0], a[1], 0)),
                line,
            ]
            + [whole] * len(terms),
            out_specs=[whole, line],
        ),
        out_shape=[
            jax.ShapeDtypeStruct((tok_rows, D), bf16),
            jax.ShapeDtypeStruct((1, D), f32),
        ],
        compiler_params=pltpu.CompilerParams(vmem_limit_bytes=40 * 2**20),
        cost_estimate=cost(3),
        name="residual_backward",
    )(at, grad_logits, router_flip, residual, up_blocks, gain_row, *terms)


def dispatch_kernel(hits_ref, x_ref, out_ref):
    experts, _, capacity, _ = out_ref.shape
    width = x_ref.shape[2]
    for block in range(x_ref.shape[0]):
        picked = dot_nn(hits_ref[0], x_ref[block]).astype(bf16)
        for e in range(experts):
            out_ref[e, 0, :, pl.ds(block * width, width)] = picked[e * capacity : (e + 1) * capacity]


def dispatch_blocks(hits, x_blocks, rows, experts):
    group, slot_rows, tok_rows = hits.shape
    width = x_blocks.shape[2]
    capacity = slot_rows // experts
    return pl.pallas_call(
        dispatch_kernel,
        grid=(group,),
        in_specs=[
            pl.BlockSpec((1, slot_rows, tok_rows), lambda b: (b, 0, 0)),
            pl.BlockSpec((rows, tok_rows, width), lambda b: (b // rows, b % rows, 0)),
        ],
        out_specs=pl.BlockSpec((experts, 1, capacity, D), lambda b: (0, b, 0, 0)),
        out_shape=jax.ShapeDtypeStruct((experts, group, capacity, D), bf16),
        cost_estimate=cost(14),
        name="cotangent_to_slots",
    )(hits, x_blocks)


def experts_kernel(count, first, ids_ref, *refs):
    feats = refs[:count]
    raws = refs[count : 2 * count]
    hits_ref, flip_ref, router_ref, gate_w_ref, up_w_ref = refs[2 * count : 2 * count + 5]
    rest = refs[2 * count + 5 :]
    if not first:
        rest = rest[5:]
    slot_ref, hidden_ref, grad_gate_ref, grad_up_ref, scale_ref = rest[:5]
    feat_sums = rest[5 : 5 + count]
    probs_ref, in_acc, in_all = rest[5 + count :]
    e, f = pl.program_id(0), pl.program_id(1)
    last_expert = e == pl.num_programs(0) - 1
    last_tile = f == pl.num_programs(1) - 1
    capacity = raws[0].shape[2]
    chosen = ids_ref[count] + e
    own_slots = pl.ds(pl.multiple_of(e * capacity, 16), capacity)

    @pl.when((e == 0) & (f == 0))
    def _():
        for k in range(count):
            logits = dot_nt(router_ref[...], feats[k][...])
            raised = jnp.exp(logits - jnp.max(logits, axis=0, keepdims=True))
            probs_ref[k] = raised / jnp.sum(raised, axis=0, keepdims=True)

    @pl.when(f == 0)
    def _():
        for k in range(count):
            at = pl.ds(k * capacity, capacity)
            hits = hits_ref[ids_ref[k], own_slots, :]
            slot_ref[0, at, :] = dot_nn(hits, feats[k][...]).astype(bf16)
            probs = probs_ref[k]
            rank = lax.broadcasted_iota(jnp.int32, probs.shape, 0)
            gate = jnp.sum(jnp.where(rank == chosen, probs, 0.0), axis=0, keepdims=True)
            scale_ref[0, at, :] = jnp.sum(hits.astype(f32) * gate, axis=1, keepdims=True)

    slots = slot_ref[0]
    gate_w, up_w = gate_w_ref[0], up_w_ref[0]
    gate_pre = dot_nn(slots, gate_w)
    up_pre = dot_nn(slots, up_w)
    sigmoid = 1.0 / (1.0 + jnp.exp(-gate_pre))
    silu = gate_pre * sigmoid
    hidden_ref[0] = (silu * up_pre).astype(bf16)
    grad_hidden = jnp.concatenate([raw[0, 0] for raw in raws], axis=0) * scale_ref[0]
    grad_gate = (grad_hidden * up_pre * sigmoid * (1.0 + gate_pre * (1.0 - sigmoid))).astype(bf16)
    grad_up = (grad_hidden * silu).astype(bf16)
    grad_gate_ref[0] = grad_gate
    grad_up_ref[0] = grad_up
    in_term = dot_nt(grad_gate, gate_w) + dot_nt(grad_up, up_w)

    @pl.when(f == 0)
    def _():
        in_acc[...] = in_term

    @pl.when(f > 0)
    def _():
        in_acc[...] += in_term

    @pl.when(last_tile)
    def _():
        for k in range(count):
            in_all[k, own_slots, :] = in_acc[pl.ds(k * capacity, capacity), :].astype(bf16)

    @pl.when(last_tile & last_expert)
    def _():
        for k in range(count):
            feat_sums[k][...] = dot_nn(flip_ref[ids_ref[k]], in_all[k]).astype(bf16)


def run_experts(feats, ids, first_expert, grad_raw, hits, flip, router_flip, expand_weight, carried, place):
    count = len(feats)
    experts, group, capacity, _ = grad_raw.shape
    tok_rows = feats[0].shape[0]
    rows = count * capacity
    tile = F // 2
    tiles = F // tile
    first = carried is None
    whole = lambda shape: pl.BlockSpec(shape, lambda e, f, ids: (0,) * len(shape))
    once = lambda shape: pl.BlockSpec(
        shape, lambda e, f, ids: (0,) * len(shape), pipeline_mode=pl.Buffered(1)
    )
    in_specs = [once((tok_rows, D))] * count
    in_specs += [
        pl.BlockSpec((1, 1, capacity, tile), lambda e, f, ids, k=k: (e, ids[k], 0, f))
        for k in range(count)
    ]
    in_specs += [
        once(hits.shape),
        once(flip.shape),
        once(router_flip.shape),
        pl.BlockSpec((1, D, tile), lambda e, f, ids: (e, 0, f)),
        pl.BlockSpec((1, D, tile), lambda e, f, ids: (e, 0, f + tiles)),
    ]
    operands = [*feats, *[grad_raw] * count, hits, flip, router_flip, expand_weight, expand_weight]
    aliases = {}
    if not first:
        in_specs += [pl.BlockSpec(memory_space=pl.ANY)] * 5
        operands += carried
        aliases = {1 + len(operands) - 5 + k: k for k in range(5)}
    wide = pl.BlockSpec((1, rows, D), lambda e, f, ids: (e, place, 0))
    narrow = pl.BlockSpec((1, rows, tile), lambda e, f, ids: (e, place, f))
    thin = pl.BlockSpec((1, rows, 1), lambda e, f, ids: (e, place, 0))
    narrow_shape = jax.ShapeDtypeStruct((experts, group * capacity, F), bf16)
    out = pl.pallas_call(
        functools.partial(experts_kernel, count, first),
        grid_spec=pltpu.PrefetchScalarGridSpec(
            num_scalar_prefetch=1,
            grid=(experts, tiles),
            in_specs=in_specs,
            out_specs=[wide, narrow, narrow, narrow, thin] + [whole((tok_rows, D))] * count,
            scratch_shapes=[
                pltpu.VMEM((count, router_flip.shape[0], tok_rows), f32),
                pltpu.VMEM((rows, D), f32),
                pltpu.VMEM((count, experts * capacity, D), bf16),
            ],
        ),
        out_shape=[jax.ShapeDtypeStruct((experts, group * capacity, D), bf16)]
        + [narrow_shape] * 3
        + [jax.ShapeDtypeStruct((experts, group * capacity, 1), f32)]
        + [jax.ShapeDtypeStruct((tok_rows, D), bf16)] * count,
        input_output_aliases=aliases,
        compiler_params=pltpu.CompilerParams(vmem_limit_bytes=58 * 2**20),
        cost_estimate=cost(13 + 2 * count),
        name="experts",
    )(jnp.stack([*ids, first_expert]).astype(jnp.int32), *operands)
    return out[:5], out[5:]


def combine_kernel(cores, ids_ref, slot_ref, out_ref, up_ref, hits_ref, flip_ref, scale_ref, gates_ref, grad_out_ref, *moe_refs):
    experts, _, capacity, _ = out_ref.shape
    scaled = []
    for e in range(experts):
        expert_out = out_ref[e, 0].astype(f32)
        upstream = up_ref[e, 0].astype(f32)
        scale = scale_ref[e, 0]
        dots = jnp.sum(expert_out * upstream, axis=1, keepdims=True)
        hits = hits_ref[0, e * capacity : (e + 1) * capacity, :].astype(f32)
        gates_ref[0, pl.ds(e, 1), :] = jnp.sum(hits * dots, axis=0, keepdims=True)
        grad_out_ref[e, 0] = (upstream * scale).astype(bf16)
        scaled.append((expert_out * scale).astype(bf16))
    total = dot_nn(flip_ref[0], jnp.concatenate(scaled, axis=0)).astype(bf16)
    for k in range(cores):

        @pl.when(slot_ref[2 * pl.program_id(0)] == k)
        def _():
            moe_refs[k][0] = total


def combine_experts(ids, chips, expert_out, upstream_slots, hits, flip, scale, cores):
    experts, group, capacity, _ = upstream_slots.shape
    tok_rows = hits.shape[2]
    by_place = pl.BlockSpec((experts, 1, capacity, D), lambda j, ids, at: (0, j, 0, 0))
    by_id = lambda shape: pl.BlockSpec((1,) + shape, lambda j, ids, at: (ids[j], 0, 0))
    order = []
    for distance, _ in chips:
        if distance not in order:
            order.append(distance)
    slots = []
    for j, (_, k) in enumerate(chips):
        slots += [k, 0]
    places = []
    for core in range(cores):
        mine = [(j, order.index(distance)) for j, (distance, k) in enumerate(chips) if k == core]
        for j in range(group):
            later = [place for at, place in mine if at >= j]
            places.append(later[0] if later else mine[-1][1])
    table = jnp.array(slots + places, jnp.int32)
    gates, grad_out, *sums = pl.pallas_call(
        functools.partial(combine_kernel, cores),
        grid_spec=pltpu.PrefetchScalarGridSpec(
            num_scalar_prefetch=2,
            grid=(group,),
            in_specs=[
                by_place,
                pl.BlockSpec((experts, 1, capacity, D), lambda j, ids, at: (0, ids[j], 0, 0)),
                by_id(hits.shape[1:]),
                by_id(flip.shape[1:]),
                pl.BlockSpec((experts, 1, capacity, 1), lambda j, ids, at: (0, j, 0, 0)),
            ],
            out_specs=[by_id((experts, tok_rows)), by_place]
            + [
                pl.BlockSpec(
                    (1, tok_rows, D),
                    lambda j, ids, at, k=k: (at[2 * group + k * group + j], 0, 0),
                )
                for k in range(cores)
            ],
        ),
        out_shape=[
            jax.ShapeDtypeStruct((group, experts, tok_rows), f32),
            jax.ShapeDtypeStruct((experts, group, capacity, D), bf16),
        ]
        + [jax.ShapeDtypeStruct((group // cores, tok_rows, D), bf16)] * cores,
        compiler_params=pltpu.CompilerParams(vmem_limit_bytes=40 * 2**20),
        cost_estimate=cost(18),
        name="experts_combine",
    )(
        ids,
        table,
        expert_out.reshape(experts, group, capacity, D),
        upstream_slots,
        hits,
        flip,
        scale.reshape(experts, group, capacity, 1),
    )
    return gates, grad_out, sums, order


def weight_grad_kernel(sides, added, pieces, filled, rank_ref, left_ref, *refs):
    rights, refs = refs[:sides], refs[sides:]
    more, refs = refs[:added], refs[added + filled :]
    outs, flip_ref = refs[:-1], refs[-1]
    e, m, n = pl.program_id(0), pl.program_id(1), pl.program_id(2)

    @pl.when(n == 0)
    def _():
        flip_ref[...] = left_ref[0].T

    for side in range(sides):

        @pl.when(n == side)
        def _():
            total = dot_nn(flip_ref[...], rights[side][0])
            if not added and not pieces:
                outs[0][0] = total
            for k in range(side, max(added, len(outs) if pieces else 0), sides):

                @pl.when(e * pl.num_programs(1) + m == k // sides)
                def _():
                    grown = total + more[k][...].astype(f32) if added else total
                    if pieces:
                        outs[k][...] = grown.astype(bf16)
                    else:
                        outs[0][0] = grown


def weight_grad(left, rights, rank, rows, first=0, experts=None, more=(), pieces=False, into=None):
    experts = left.shape[0] if experts is None else experts
    slots = left.shape[1]
    tile = min(512, rows)
    per = rows // tile
    width = F
    shares = [(right, j) for right in rights for j in range(right.shape[2] // width)]
    sides = len(shares)
    piece = pl.BlockSpec((tile, width), lambda e, m, n, p: (0, 0))
    if pieces:
        out_specs = [piece] * (experts * per * sides)
        out_shape = [jax.ShapeDtypeStruct((tile, width), bf16)] * (experts * per * sides)
    else:
        out_specs = [pl.BlockSpec((1, tile, width), lambda e, m, n, p: (e + first, m, n))]
        out_shape = [jax.ShapeDtypeStruct((left.shape[0], rows, sides * width), f32)]
    out = pl.pallas_call(
        functools.partial(weight_grad_kernel, sides, len(more), pieces, into is not None),
        grid_spec=pltpu.PrefetchScalarGridSpec(
            num_scalar_prefetch=1,
            grid=(experts, per, sides),
            in_specs=[
                pl.BlockSpec((1, slots, tile), lambda e, m, n, p: (e + first, 0, p[0] * per + m))
            ]
            + [
                pl.BlockSpec((1, slots, width), lambda e, m, n, p, j=j: (e + first, 0, j))
                for _, j in shares
            ]
            + [piece] * len(more)
            + [pl.BlockSpec(memory_space=pl.ANY)] * (into is not None),
            out_specs=out_specs,
            scratch_shapes=[pltpu.VMEM((tile, slots), bf16)],
        ),
        out_shape=out_shape,
        input_output_aliases={} if into is None else {2 + sides + len(more): 0},
        compiler_params=pltpu.CompilerParams(vmem_limit_bytes=48 * 2**20),
        cost_estimate=cost(experts * rows * sides / 560 * (2 if more else 1.7)),
        name="weight_gradient",
    )(
        rank.reshape(1).astype(jnp.int32), left, *[right for right, _ in shares], *more,
        *([] if into is None else [into]),
    )
    return out if pieces else out[0]


def weight_grad_sends(left, rights, rows, first, experts):
    count = lax.axis_size("dp")
    rank = lax.axis_index("dp")
    onward = [(d, (d + 1) % count) for d in range(count)]
    sent, arrived = [], []
    for e in range(first, first + experts):
        more = []
        for step in range(1, count):
            parts = weight_grad(left, rights, (rank + count - step) % count, rows, e, 1, more, True)
            more = [lax.ppermute(part, "dp", onward) for part in parts]
        sent += parts if more else []
        arrived += more
    return sent, arrived


def unturn(grad, cosine, sine_part):
    return grad * cosine - jnp.roll(grad, HD // 2, axis=1) * sine_part


def unproject_kernel(
    grad_q_ref, grad_k_ref, grad_v_ref, raw_ref, squares_ref, dots_ref, gain_ref, cosine_ref, sine_ref,
    weight_ref, grad_ref, gain_terms_ref, out_ref,
):
    rows, _, width = out_ref.shape
    inverse = lax.rsqrt(squares_ref[...] / D + norm_epsilon)
    inner = inverse * inverse * dots_ref[:2] / D

    @pl.when(pl.program_id(0) == 0)
    def _():
        gain_terms_ref[...] = jnp.zeros_like(gain_terms_ref)

    for j, part_ref in ((0, grad_q_ref), (1, grad_k_ref)):
        grad = unturn(part_ref[...], cosine_ref[...], sine_ref[...])
        column = as_column(inverse[j : j + 1])
        raw = raw_ref[:, j * HD : (j + 1) * HD]
        gain_terms_ref[pl.ds(j, 1), :] += jnp.sum(grad * raw * column, axis=0, keepdims=True)
        back = column * grad * gain_ref[j : j + 1, :] - raw * as_column(inner[j : j + 1])
        grad_ref[:, pl.ds(j * HD, HD)] = back.astype(bf16)
    grad_ref[:, pl.ds(2 * HD, HD)] = grad_v_ref[...].astype(bf16)
    for row in range(rows):
        at = pl.ds(row * width, width)
        out_ref[row] = dot_nn(grad_ref[...], weight_ref[:, at]).astype(bf16)


def unproject(grads, raw, squares, dots, gain_pair, cosine, sine_part, weight_flip, rows, cols):
    length = raw.shape[0]
    block_rows, width = length // cols, D // rows
    tile = block_rows
    tall = pl.BlockSpec((tile, HD), lambda i: (i, 0))
    three = pl.BlockSpec((tile, 3 * HD), lambda i: (i, 0))
    pair = pl.BlockSpec((2, tile), lambda i: (0, i))
    trio = pl.BlockSpec((3, tile), lambda i: (0, i))
    fixed = pl.BlockSpec((2, HD), lambda i: (0, 0))
    return pl.pallas_call(
        unproject_kernel,
        grid=(length // tile,),
        in_specs=[
            tall, tall, tall, three, pair, trio, fixed, tall, tall,
            pl.BlockSpec(weight_flip.shape, lambda i: (0, 0)),
        ],
        out_specs=[
            three, fixed, pl.BlockSpec((rows, tile, width), lambda i: (i, 0, 0)),
        ],
        out_shape=[
            jax.ShapeDtypeStruct((length, 3 * HD), bf16),
            jax.ShapeDtypeStruct((2, HD), f32),
            jax.ShapeDtypeStruct((rows * cols, block_rows, width), bf16),
        ],
        compiler_params=pltpu.CompilerParams(vmem_limit_bytes=52 * 2**20),
        cost_estimate=cost(15.5),
        name="projection_backward",
    )(*grads, raw, squares, dots, gain_pair, cosine, sine_part, weight_flip)


def norm_back(values, inverse, gain_row, upstream, dot_total):
    scaled = upstream * gain_row
    return inverse[:, None] * scaled - values * (inverse**3 * dot_total / D)[:, None]


def dot(a, b):
    return jnp.dot(a, b, preferred_element_type=f32)


def einsum(spec, a, b):
    return jnp.einsum(spec, a, b, preferred_element_type=f32)


def on_device(
    layer_input,
    gains,
    qkv_weight,
    output_weight,
    router_weight,
    expand_weight,
    reduce_weight,
    routes,
    drop_order,
    prefix_len,
    cotangent,
):
    row_rank, col_rank = lax.axis_index("row"), lax.axis_index("col")
    rows, cols = lax.axis_size("row"), lax.axis_size("col")
    dp_count = lax.axis_size("dp")
    group = rows * cols
    res_rows, row_width = layer_input.shape
    col_width = qkv_weight.shape[2]
    seq_len = res_rows * cols
    tok_rows = res_rows // rows
    block_rank = col_rank * rows + row_rank
    expert_rank = row_rank * cols + col_rank
    expert_count = router_weight.shape[1]
    local_experts = expand_weight.shape[0]
    capacity = tok_rows * TOP // expert_count
    ring = Ring(rows, cols)
    gain_rows = gains.astype(f32)
    router_flip = router_weight.T

    paired = dp_count % 2 == 0
    half_rank = lax.axis_index("dp") % 2 if paired else 0
    partner = [(d, d ^ 1) for d in range(dp_count)]
    halves = 2 if paired else 1
    half_rows = row_width // halves
    head_half = lax.dynamic_slice_in_dim(qkv_weight, half_rank * half_rows, half_rows, 0)
    head_half = head_half.reshape(half_rows, 3, rows, HD).transpose(2, 1, 0, 3)
    head_out = output_weight.reshape(rows, HD, row_width // HD, HD).transpose(0, 2, 1, 3)
    head_half = jnp.concatenate(
        [head_half.reshape(rows, 3 * half_rows, HD), head_out.reshape(rows, row_width, HD)], axis=1
    )
    head_half = exchange(head_half, "row")
    head_out = head_half[:, 3 * half_rows :].reshape(D, HD).reshape(D // HD, HD, HD)
    head_out = head_out.transpose(0, 2, 1).reshape(D, HD)
    head_half = head_half[:, : 3 * half_rows].reshape(rows, 3, half_rows, HD)
    head_half = head_half.transpose(0, 2, 1, 3).reshape(rows, half_rows, 3 * HD)
    half_width = HD // 2
    frequency = rope_base ** (-2.0 * jnp.arange(half_width, dtype=f32) / HD)
    angles = jnp.arange(seq_len).astype(f32)[:, None] * frequency[None, :]
    cosine, sine_part = jnp.cos(angles), jnp.sin(angles)
    cosine = jnp.concatenate([cosine, cosine], axis=1)
    sine_part = jnp.concatenate([-sine_part, sine_part], axis=1)
    own_lines = jnp.concatenate([routes.T, drop_order[None, :]], axis=0)
    lines = jnp.zeros((cols,) + own_lines.shape, jnp.int32)
    lines = lax.dynamic_update_slice(lines, own_lines[None], (col_rank, 0, 0))
    for step in range(1, cols):
        arrived = lax.ppermute(own_lines, "col", [(c, (c + step) % cols) for c in range(cols)])
        lines = lax.dynamic_update_slice(
            lines, arrived[None], ((col_rank + cols - step) % cols, 0, 0)
        )
    first_expert = expert_rank * local_experts
    own_experts = first_expert + jnp.arange(local_experts)
    member = jnp.any(lines[None, :, :TOP] == own_experts[:, None, None, None], axis=2)
    member = member.reshape(local_experts, group, tok_rows).transpose(1, 0, 2)
    drop_rank = lines[:, TOP].reshape(group, tok_rows)
    token_index = jnp.arange(tok_rows)
    earlier = (drop_rank[:, None, :] < drop_rank[:, :, None]) | (
        drop_rank[:, None, :] == drop_rank[:, :, None]
    ) & (token_index[None, None, :] < token_index[None, :, None])
    position = jnp.sum(jnp.where(earlier[:, None] & member[:, :, None, :], 1, 0), axis=-1)
    kept = member & (position < capacity)
    hits = kept[:, :, None, :] & (
        position[:, :, None, :] == jnp.arange(capacity)[None, None, :, None]
    )
    hits = hits.reshape(group, local_experts * capacity, tok_rows)
    dispatch = hits.astype(bf16)
    combine = hits.transpose(0, 2, 1).astype(bf16)

    weight_half = lax.dynamic_slice_in_dim(
        output_weight, half_rank * (col_width // 2), col_width // halves, 0
    )
    at = [col_rank, row_rank]
    for chip_group in range(ring.groups):
        for half in range(2):
            for k in range(ring.cores):
                col = chip_group * ring.cores + (ring.core + k) % ring.cores
                at.append((col * 2 + (half_rank + half) % 2) * (rows // 2))
    at = jnp.stack([jnp.asarray(value, jnp.int32) for value in at])

    x_steps = ring.gather_steps(jnp.concatenate([layer_input, weight_half], axis=0))
    x_blocks = unwritten((group, res_rows + weight_half.shape[0], row_width), bf16)
    x_blocks = ring.place_blocks(x_blocks, ring.with_siblings(next(x_steps)))
    pieces = other_half = None
    for step in range(ring.size // 2):
        arrival = x_steps.send(pieces)
        pieces = [piece for piece, _ in arrival]
        if step == 0:
            pieces, cosine, sine_part = together(pieces, cosine, sine_part)
        elif step == 1:
            pieces, head_half, x_blocks, dispatch, combine = together(
                pieces, head_half, x_blocks, dispatch, combine
            )
            other_half = lax.ppermute(head_half, "dp", partner) if paired else None
        elif step == 2:
            pieces, x_blocks = together(pieces, x_blocks)
        else:
            pieces, x_blocks, other_half = together(pieces, x_blocks, other_half)
        arrival = list(zip(pieces, [distance for _, distance in arrival]))
        x_blocks = ring.place_blocks(x_blocks, ring.with_siblings(arrival))
    if paired:
        head_weight = jnp.where(
            half_rank == 0,
            jnp.stack([head_half, other_half], axis=1),
            jnp.stack([other_half, head_half], axis=1),
        )
    else:
        head_weight = head_half
    head_weight = head_weight.reshape(D, 3 * HD)
    weight_flip = head_weight.T
    half_place = res_rows // (col_width // 2)
    table = []
    for half in range(2):
        for k in range(ring.cores):
            for chip_group in range(ring.groups):
                col = chip_group * ring.cores + (ring.core + k) % ring.cores
                for row in range(rows):
                    whole_plane = half == 0 or not paired
                    table.append(col * rows + row if whole_plane else chip_group * rows + row)
    table = jnp.stack([jnp.asarray(value, jnp.int32) for value in table])
    if paired:
        own_core = x_blocks[:, res_rows:].reshape(
            ring.groups, ring.cores, rows, weight_half.shape[0], row_width
        )
        own_core = lax.dynamic_index_in_dim(own_core, ring.core, 1, False)
        own_core = own_core.reshape(ring.size, weight_half.shape[0], row_width)
        theirs = lax.ppermute(own_core, "dp", partner)
    upstream_blocks = lax.all_gather(after(cotangent, pieces), BLOCKS, axis=0)
    projected, inv_first, square_terms = project(x_blocks, res_rows, gain_rows[0:1], head_weight, rows)
    squares = ring.small_sum(square_terms)

    head_first = block_rank * HD
    gain_pair = lax.dynamic_slice(gain_rows, (1, head_first), (2, HD))
    query_low, key_low, value_low, key_flip, value_flip = turn(
        projected, squares, gain_pair, cosine, sine_part
    )

    query_rows = max(seq_len // 6, 128)
    attn_head, lse = attention(query_low, key_low, value_flip, prefix_len, query_rows)
    attn_tokens = exchange(attn_head.reshape(group, tok_rows, HD), BLOCKS)
    weight_sets = [(x_blocks, half_place)] * ring.cores
    if paired:
        attn_tokens, theirs = together(attn_tokens, theirs)
        weight_sets += [(block, 0) for block in ring.from_siblings(theirs)]
    else:
        weight_sets += [(x_blocks, half_place + 1)] * ring.cores
    upstream_slots = dispatch_blocks(dispatch, upstream_blocks, rows, local_experts)
    residual, second_low = output_branch(
        at, table, attn_tokens, weight_sets, x_blocks, gain_rows[3:4], rows, ring.groups
    )
    feat_steps = ring.gather_steps(second_low)
    grad_raw = einsum(
        "end,efd->enf", upstream_slots.reshape(local_experts, group * capacity, D), reduce_weight
    ).reshape(local_experts, group, capacity, F)

    carried = None
    waiting = [
        (block, ident, 0, k)
        for k, (block, ident) in enumerate(ring.with_siblings(next(feat_steps)))
    ]
    calls = {1: 0, ring.size // 2 - 1: 1}
    feat_sums, taken_by = {}, {}
    pieces = None
    for step in range(ring.size // 2):
        arrival = feat_steps.send(pieces)
        pieces = [piece for piece, _ in arrival]
        if step == 0:
            pieces, upstream_slots = together(pieces, upstream_slots)
        elif step == 1:
            pieces, grad_raw = together(pieces, grad_raw)
        elif step == 2:
            pieces, *carried = together(pieces, *carried)
        direct, later = [], []
        for piece, (_, distance) in zip(pieces, arrival):
            for k, (block, ident) in enumerate(ring.with_siblings([(piece, distance)])):
                (later if k else direct).append((block, ident, distance, k))
        waiting += direct
        if step not in calls:
            waiting += later
            continue
        taken, waiting = (waiting, later) if step == 1 else (waiting + later, [])
        carried, sums = run_experts(
            [block for block, *_ in taken],
            [ident for _, ident, *_ in taken],
            first_expert,
            grad_raw,
            dispatch,
            combine,
            router_flip,
            expand_weight,
            carried,
            calls[step],
        )
        for (_, ident, distance, k), total in zip(taken, sums):
            feat_sums[distance, k] = total
        taken_by[calls[step] * len(taken)] = [item[1:] for item in taken]
    by_slot = [item for start in sorted(taken_by) for item in taken_by[start]]
    places = [ident for ident, _, _ in by_slot]
    chips = [(distance, k) for _, distance, k in by_slot]
    feat_parts = {}

    def feat_part(distance):
        if distance not in feat_parts:
            others = ring.for_siblings(*[feat_sums[distance, k] for k in range(1, ring.cores)])
            feat_parts[distance] = [(block, 0) for block in (feat_sums[distance, 0], *others)]
        return feat_parts[distance]

    slot_rows, hidden, grad_gate_pre, grad_up_pre, slot_gate = carried

    arriving, arrived = [], []

    def taking(count, *values):
        taken, arriving[:count] = arriving[:count], []
        *values, taken = together(*values, taken)
        arrived.extend(taken)
        return values

    def ahead_tie(scatter, parts, *values):
        steps = [scatter.step, -scatter.step] if scatter.step else []
        terms = {step: scatter.parts(step) for step in steps}
        blocks = [[block for block, _ in terms[step] if block.ndim == 2] for step in steps]
        *values, blocks = scatter.tie(*values, blocks)
        for step, given in zip(steps, blocks):
            given = iter(given)
            parts[step] = [
                (next(given), 0) if block.ndim == 2 else (block, place) for block, place in terms[step]
            ]
        return values

    grads = ring.scatter(feat_part)
    grads.ready()
    expand_sides = [grad_gate_pre, grad_up_pre]
    expand_rows, reduce_rows = D // dp_count, F // dp_count
    half = local_experts // 2
    slot_rows, = grads.tie(slot_rows)
    grads.move()
    sent, pieces = weight_grad_sends(slot_rows, expand_sides, expand_rows, 0, half)
    arriving += pieces
    sent, = ahead_tie(grads, feat_parts, sent)
    grads.ready()
    slot_rows, hidden = grads.tie(slot_rows, hidden)
    grads.move()
    expert_out = einsum("enf,efd->end", hidden, reduce_weight).astype(bf16)
    expert_out, = taking(1, *ahead_tie(grads, feat_parts, expert_out))
    grads.ready()
    expert_out, = grads.tie(expert_out)
    grads.move()
    ids = jnp.stack(places).astype(jnp.int32)
    gate_tokens, grad_out_slots, moe_sums, moe_order = combine_experts(
        ids, chips, expert_out, upstream_slots, dispatch, combine, slot_gate, ring.cores
    )
    grad_out_slots = grad_out_slots.reshape(local_experts, group * capacity, D)
    grad_out_slots, moe_sums, gate_tokens = taking(
        1, *ahead_tie(grads, feat_parts, grad_out_slots, moe_sums, gate_tokens)
    )
    grads.ready()
    moe_sums, gate_tokens, slot_rows = grads.tie(moe_sums, gate_tokens, slot_rows)
    grads.move()
    grad_probs = exchange(gate_tokens, BLOCKS)
    sent, pieces = weight_grad_sends(
        slot_rows, expand_sides, expand_rows, half, local_experts - half
    )
    arriving += pieces
    expand_count = len(arrived) + len(arriving)
    moe_others = [lax.ppermute(other, PLANE, ring.sibling) for other in moe_sums[1:]]

    def moe_part(distance):
        place = moe_order.index(distance)
        return [(array, place) for array in (moe_sums[0], *moe_others)]

    grad_probs = grad_probs.reshape(cols, rows, local_experts, tok_rows)
    grad_probs = grad_probs.transpose(1, 0, 2, 3).reshape(expert_count, tok_rows)
    logits = dot_nt(router_flip, second_low)
    probs = jax.nn.softmax(logits, axis=0)
    grad_logits = probs * (grad_probs - jnp.sum(probs * grad_probs, axis=0, keepdims=True))
    grad_logits = grad_logits.T.astype(bf16)
    router_term = einsum("te,td->ed", grad_logits, second_low)
    grad_logits, router_term, moe_others, sent = taking(
        1, *grads.tie(grad_logits, router_term, moe_others, sent)
    )
    moes = ring.scatter(moe_part)
    moes.ready()
    grad_terms = grads.total()

    grad_branch, gain_second_term = residual_back(
        at[:2], grad_terms, grad_logits, router_flip, residual, upstream_blocks, gain_rows[3:4], rows
    )
    branch_steps = ring.gather_steps(grad_branch)
    branch_all = unwritten((group, tok_rows, D), bf16)
    branch_all = ring.place_blocks(branch_all, ring.with_siblings(next(branch_steps)))
    rank = lax.axis_index("dp")
    expand_grad = None
    extra = []
    pieces = None
    for step in range(ring.size // 2):
        arrival = branch_steps.send(pieces)
        if step == ring.size // 2 - 1:
            moes.move()
        pieces, branch_all, extra, moes.going = taking(
            1,
            [piece for piece, _ in arrival],
            branch_all,
            extra,
            moes.going,
        )
        if step == 0:
            left, = together(hidden, pieces)[:1]
            extra, parts = weight_grad_sends(
                left, [grad_out_slots], reduce_rows, 0, local_experts
            )
            arriving += parts
        elif step == 2:
            expand_grad, = extra
        elif step == 1:
            left, = together(slot_rows, pieces)[:1]
            expand_grad = weight_grad(
                left, expand_sides, rank, expand_rows, 0, half, arrived[: expand_count // 2]
            )
            extra = [expand_grad]
        else:
            expand_grad, = extra
        arrival = list(zip(pieces, [distance for _, distance in arrival]))
        branch_all = ring.place_blocks(branch_all, ring.with_siblings(arrival))

    moes.ready()
    branch_all, = moes.tie(branch_all)
    moes.move()
    grad_attn = dot(branch_all.reshape(seq_len, D), head_out).astype(bf16)
    centre = jnp.sum(attn_head.astype(f32) * grad_attn.astype(f32), axis=1)[None]
    grad_query, dot_query, grad_key, grad_value, dot_key, dot_value = attention_back(
        query_low, key_low, key_flip, value_low, grad_attn, lse, centre, prefix_len, query_rows
    )
    head_grads = [grad_query, grad_key, grad_value]
    dots = jnp.concatenate([dot_query, dot_key, dot_value], axis=0)
    dots, = taking(2, *moes.tie(dots))
    moes.ready()
    dots, = moes.tie(dots)
    dots = ring.small_sum(dots)
    dots, = moes.tie(dots)
    moes.move()

    grad_qkv, gain_pair_terms, grad_first_blocks = unproject(
        head_grads, projected, squares, dots, gain_pair, cosine, sine_part, weight_flip, rows, cols
    )

    def first_part(distance):
        if distance not in first_parts:
            mine, *others = ring.block_ids(distance)
            others = ring.for_siblings(
                *[lax.dynamic_index_in_dim(grad_first_blocks, k, 0, False) for k in others]
            )
            first_parts[distance] = [(grad_first_blocks, mine)] + [(block, 0) for block in others]
        return first_parts[distance]

    first_parts = {}
    grad_first_blocks, grad_qkv = taking(1, *moes.tie(grad_first_blocks, grad_qkv))
    first_far = block_sum(first_part(ring.size // 2))
    moes.ready()
    first_far, grad_first_blocks = moes.tie(first_far, grad_first_blocks)
    first_parts = {ring.size // 2: [(first_far, 0)]}
    firsts = ring.scatter(first_part)
    firsts.ready()
    firsts.move()
    moes.move()
    output_term = dot(attn_head.T, branch_all.reshape(seq_len, D))
    output_term = output_term.astype(bf16).reshape(HD, rows, row_width).transpose(1, 0, 2)
    output_term, = taking(1, *moes.tie(*ahead_tie(firsts, first_parts, output_term)))
    moe_terms = moes.total()
    firsts.ready()
    grad_qkv, slot_rows = firsts.tie(grad_qkv, slot_rows)
    firsts.move()
    qkv_term, gain_first_term = project_weight(
        x_blocks, res_rows, gain_rows[0:1], inv_first, grad_qkv, head_weight, rows
    )
    qkv_rows = row_width // dp_count
    qkv_sum = dp_sum(
        lambda rank: lax.dynamic_slice_in_dim(qkv_term, rank * qkv_rows, qkv_rows, 2)
    )
    output_sum = exchange(output_term, "row").reshape(col_width, row_width)
    qkv_term, = taking(1, *ahead_tie(firsts, first_parts, qkv_term))
    firsts.ready()
    slot_rows, = firsts.tie(slot_rows)
    firsts.move()
    expand_grad = weight_grad(
        slot_rows, expand_sides, rank, expand_rows, half, local_experts - half,
        arrived[expand_count // 2 : expand_count], into=expand_grad,
    )
    layer_tokens = residual
    for term in moe_terms:
        layer_tokens = layer_tokens + term.astype(f32)
    layer_tokens = layer_tokens.astype(bf16)
    layer_output = lax.all_to_all(layer_tokens, "row", split_axis=1, concat_axis=0, tiled=True)
    expand_grad, output_sum = taking(
        len(arriving), *ahead_tie(firsts, first_parts, expand_grad, output_sum)
    )
    firsts.ready()
    hidden, qkv_sum = firsts.tie(hidden, qkv_sum)
    firsts.move()
    reduce_grad = weight_grad(
        hidden, [grad_out_slots], rank, reduce_rows, more=arrived[expand_count:]
    )
    reduce_grad, layer_output = firsts.tie(reduce_grad, layer_output)
    grad_first = firsts.total()
    grad_first = sum(term.astype(f32) for term in grad_first)
    grad_block = lax.dynamic_slice(
        branch_all, (col_rank * rows, 0, row_rank * row_width), (rows, tok_rows, row_width)
    ).reshape(res_rows, row_width)
    inverse = lax.rsqrt(squares / D + norm_epsilon)
    dot_first = dots[2] + norm_epsilon * jnp.sum(dots[:2] * inverse, axis=0)
    dot_first = dot_first / inv_first[0]
    own_first = col_rank * res_rows
    dot_first = lax.dynamic_slice_in_dim(dot_first, own_first, res_rows)
    inv_block = lax.dynamic_slice_in_dim(inv_first[0], own_first, res_rows)
    gain_block = lax.dynamic_slice_in_dim(gain_rows[0], row_rank * row_width, row_width)
    input_grad = grad_block.astype(f32) + norm_back(
        layer_input.astype(f32), inv_block, gain_block, grad_first, dot_first
    )

    output_rows = col_width // dp_count
    output_grad = dp_sum(
        lambda rank: lax.dynamic_slice_in_dim(
            output_sum, rank * output_rows, output_rows, 0
        ).astype(f32)
    )
    qkv_grad = exchange(qkv_sum.astype(bf16), "row").transpose(2, 1, 0, 3)
    qkv_grad = qkv_grad.reshape(1, qkv_rows, 3, col_width).astype(f32)

    def placed(term):
        return lax.dynamic_update_slice(jnp.zeros((D,), f32), term, (head_first,))

    gain_terms = jnp.concatenate(
        [
            gain_first_term,
            jnp.stack([placed(gain_pair_terms[0]), placed(gain_pair_terms[1])]),
            gain_second_term,
        ],
        axis=0,
    )
    gain_total = jnp.sum(lax.all_gather(gain_terms, ("dp", "row", "col"), axis=0), axis=0)
    router_all = lax.all_gather(router_term.astype(bf16), ("dp", "row", "col"), axis=0)
    router_total = jnp.sum(router_all.astype(f32), axis=0).T
    return (
        layer_output,
        input_grad.astype(bf16),
        gain_total,
        qkv_grad,
        output_grad[None],
        router_total,
        expand_grad,
        reduce_grad,
    )


def solution(mesh):
    return jax.shard_map(
        on_device,
        mesh=mesh,
        in_specs=(
            P(("dp", "col"), "row"),
            P(),
            P("row", None, "col"),
            P("col", "row"),
            P(),
            P(("row", "col"), None, None),
            P(("row", "col"), None, None),
            P(("dp", "col"), None),
            P(("dp", "col")),
            P("dp"),
            P(("dp", "col"), "row"),
        ),
        out_specs=(
            P(("dp", "col"), "row"),
            P(("dp", "col"), "row"),
            P(),
            P("row", "dp", None, "col"),
            P("col", "dp", "row"),
            P(),
            P(("row", "col"), "dp", None),
            P(("row", "col"), "dp", None),
        ),
        check_vma=False,
    )
```

```python
import functools
import math

import jax
import jax.numpy as jnp
from jax import lax
from jax.experimental import pallas as pl
from jax.experimental.pallas import tpu as pltpu
from jax.sharding import PartitionSpec as P

D = 2048
HD = 128
F = 1024
TOP = 8
CORES = 2
PLANE = ("row", "col")
BLOCKS = ("col", "row")
LOG2E = math.log2(math.e)
MASKED = -1e30
COST_SHARE = 0.1

norm_epsilon = 1e-05
rope_base = 10000.0
bf16 = jnp.bfloat16
f32 = jnp.float32


def dot_nt(a, b):
    return lax.dot_general(a, b, (((1,), (1,)), ((), ())), preferred_element_type=f32)


def dot_nn(a, b):
    return lax.dot_general(a, b, (((1,), (0,)), ((), ())), preferred_element_type=f32)


def cost(microseconds):
    return pl.CostEstimate(
        flops=int(microseconds * 1.1e9 * COST_SHARE), bytes_accessed=0, transcendentals=0
    )


def as_row(column):
    return jnp.broadcast_to(column, (column.shape[0], 128)).T[:1]


def as_column(row):
    return jnp.broadcast_to(row, (8, row.shape[1])).T[:, :1]


def key_limits(first_query, query_rows, key_rows, prefix):
    open_blocks = jnp.maximum((first_query + 1) // key_rows, prefix // key_rows)
    all_blocks = pl.cdiv(jnp.maximum(first_query + query_rows, prefix), key_rows)
    return open_blocks, all_blocks


def mask_scores(scores, first_key, first_query, prefix):
    keys = first_key + lax.broadcasted_iota(jnp.int32, scores.shape, 0)
    queries = first_query + lax.broadcasted_iota(jnp.int32, scores.shape, 1)
    return jnp.where((keys <= queries) | (keys < prefix), scores, MASKED)


def attention_kernel(scale, prefix_ref, q_ref, k_ref, v_flip_ref, out_ref, lse_ref, scores_ref):
    query_rows = q_ref.shape[0]
    key_rows = min(512, k_ref.shape[0])
    first_query = pl.program_id(0) * query_rows
    prefix = prefix_ref[0]
    q = q_ref[...]
    open_blocks, all_blocks = key_limits(first_query, query_rows, key_rows, prefix)

    def score(j, top, masked):
        start = pl.multiple_of(j * key_rows, key_rows)
        scores = dot_nt(k_ref[pl.ds(start, key_rows), :], q) * (scale * LOG2E)
        if masked:
            scores = mask_scores(scores, start, first_query, prefix)
        scores_ref[pl.ds(start, key_rows), :] = scores
        return jnp.maximum(top, jnp.max(scores.reshape(key_rows // 8, 8, query_rows), axis=0))

    top = jnp.full((8, query_rows), MASKED, f32)
    top = lax.fori_loop(0, open_blocks, lambda j, t: score(j, t, False), top)
    top = lax.fori_loop(open_blocks, all_blocks, lambda j, t: score(j, t, True), top)
    peak = jnp.max(top, axis=0, keepdims=True)

    def mix(j, carry):
        total, mixed = carry
        start = pl.multiple_of(j * key_rows, key_rows)
        weights = jnp.exp2(scores_ref[pl.ds(start, key_rows), :] - peak)
        total = total + jnp.sum(weights.reshape(key_rows // 8, 8, query_rows), axis=0)
        mixed = mixed + dot_nn(v_flip_ref[:, pl.ds(start, key_rows)], weights.astype(bf16))
        return total, mixed

    total, mixed = lax.fori_loop(
        0,
        all_blocks,
        mix,
        (jnp.zeros((8, query_rows), f32), jnp.zeros((q.shape[1], query_rows), f32)),
    )
    total = jnp.sum(total, axis=0, keepdims=True)
    out_ref[...] = (mixed / total).T.astype(out_ref.dtype)
    lse_ref[...] = peak + jnp.log2(total)


def attention(q, k, v_flip, prefix_len, query_rows):
    length, width = q.shape
    query_block = pl.BlockSpec((query_rows, width), lambda i, p: (i, 0))
    return pl.pallas_call(
        functools.partial(attention_kernel, width**-0.5),
        grid_spec=pltpu.PrefetchScalarGridSpec(
            num_scalar_prefetch=1,
            grid=(length // query_rows,),
            in_specs=[
                query_block,
                pl.BlockSpec((length, width), lambda i, p: (0, 0)),
                pl.BlockSpec((width, length), lambda i, p: (0, 0)),
            ],
            out_specs=[query_block, pl.BlockSpec((1, query_rows), lambda i, p: (0, i))],
            scratch_shapes=[pltpu.VMEM((length, query_rows), f32)],
        ),
        out_shape=[
            jax.ShapeDtypeStruct((length, width), bf16),
            jax.ShapeDtypeStruct((1, length), f32),
        ],
        compiler_params=pltpu.CompilerParams(vmem_limit_bytes=40 * 2**20),
        cost_estimate=cost(17),
        name="attention_forward",
    )(prefix_len, q, k, v_flip)


def attention_back_kernel(
    scale, prefix_ref, q_ref, grad_ref, lse_ref, centre_ref, k_ref, k_flip_ref, v_ref,
    grad_q_ref, dot_q_ref, grad_k_ref, grad_v_ref, dot_k_ref, dot_v_ref,
):
    query_rows = q_ref.shape[0]
    key_rows = min(512, k_ref.shape[0])
    step = pl.program_id(0)
    first_query = step * query_rows
    prefix = prefix_ref[0]

    @pl.when(step == 0)
    def _():
        grad_k_ref[...] = jnp.zeros_like(grad_k_ref)
        grad_v_ref[...] = jnp.zeros_like(grad_v_ref)

    q = q_ref[...]
    grad = grad_ref[...]
    lse = lse_ref[...]
    centre = centre_ref[...]
    open_blocks, all_blocks = key_limits(first_query, query_rows, key_rows, prefix)

    def block(j, total, masked):
        start = pl.multiple_of(j * key_rows, key_rows)
        rows = pl.ds(start, key_rows)
        scores = dot_nt(k_ref[rows, :], q) * (scale * LOG2E) - lse
        if masked:
            scores = mask_scores(scores, start, first_query, prefix)
        weights = jnp.exp2(scores)
        grad_weights = dot_nt(v_ref[rows, :], grad)
        grad_scores = (weights * (grad_weights - centre)).astype(bf16)
        grad_v_ref[rows, :] += dot_nn(weights.astype(bf16), grad)
        grad_k_ref[rows, :] += dot_nn(grad_scores, q)
        return total + dot_nn(k_flip_ref[:, rows], grad_scores)

    total = jnp.zeros((q.shape[1], query_rows), f32)
    total = lax.fori_loop(0, open_blocks, lambda j, a: block(j, a, False), total)
    total = lax.fori_loop(open_blocks, all_blocks, lambda j, a: block(j, a, True), total)
    grad_q = total.T * scale
    grad_q_ref[...] = grad_q
    dot_q_ref[...] = as_row(jnp.sum(grad_q * q.astype(f32), axis=1, keepdims=True))

    @pl.when(step == pl.num_programs(0) - 1)
    def _():
        for start in range(0, k_ref.shape[0], key_rows):
            rows = pl.ds(start, key_rows)
            grad_k = grad_k_ref[rows, :] * scale
            grad_k_ref[rows, :] = grad_k
            dot_k_ref[:, rows] = as_row(
                jnp.sum(grad_k * k_ref[rows, :].astype(f32), axis=1, keepdims=True)
            )
            dot_v_ref[:, rows] = as_row(
                jnp.sum(grad_v_ref[rows, :] * v_ref[rows, :].astype(f32), axis=1, keepdims=True)
            )


def attention_back(q, k, k_flip, v, grad, lse, centre, prefix_len, query_rows):
    length, width = q.shape
    whole = pl.BlockSpec((length, width), lambda i, p: (0, 0))
    flipped = pl.BlockSpec((width, length), lambda i, p: (0, 0))
    query_block = pl.BlockSpec((query_rows, width), lambda i, p: (i, 0))
    query_row = pl.BlockSpec((1, query_rows), lambda i, p: (0, i))
    key_row = pl.BlockSpec((1, length), lambda i, p: (0, 0))
    result = jax.ShapeDtypeStruct((length, width), f32)
    line = jax.ShapeDtypeStruct((1, length), f32)
    return pl.pallas_call(
        functools.partial(attention_back_kernel, width**-0.5),
        grid_spec=pltpu.PrefetchScalarGridSpec(
            num_scalar_prefetch=1,
            grid=(length // query_rows,),
            in_specs=[query_block, query_block, query_row, query_row, whole, flipped, whole],
            out_specs=[query_block, query_row, whole, whole] + [key_row] * 2,
        ),
        out_shape=[result, line, result, result] + [line] * 2,
        compiler_params=pltpu.CompilerParams(vmem_limit_bytes=40 * 2**20),
        cost_estimate=cost(24),
        name="attention_backward",
    )(prefix_len, q, grad, lse, centre, k, k_flip, v)


def unwritten(shape, dtype):
    return pl.pallas_call(
        lambda out_ref: None,
        out_specs=pl.BlockSpec(memory_space=pl.ANY),
        out_shape=jax.ShapeDtypeStruct(shape, dtype),
        name="buffer",
    )()


def add_low(one, two):
    return (one.astype(f32) + two.astype(f32)).astype(bf16)


def step_sum_kernel(counts, halved, ids_ref, *refs):
    half = pl.program_id(0)
    parts, (forth_ref, back_ref, ahead_ref, behind_ref) = refs[:-4], refs[-4:]
    for start, came_ref, out_ref, at in (
        (0, forth_ref, ahead_ref, 0),
        (counts[0], back_ref, behind_ref, 1),
    ):
        count = counts[at]
        total = sum(ref[0].astype(f32) for ref in parts[start : start + count])
        if not halved:
            out_ref[...] = (total + came_ref[...].astype(f32)).astype(bf16)
            continue

        @pl.when(half == at)
        def _():
            out_ref[...] = (total + came_ref[...].astype(f32)).astype(bf16)

        @pl.when(half != at)
        def _():
            out_ref[...] = total.astype(bf16)


def step_sum(ahead, behind, forth, back):
    parts = [(array if array.ndim == 3 else array[None], place) for array, place in ahead + behind]
    ids = jnp.stack([jnp.asarray(place, jnp.int32) for _, place in parts])
    _, rows, width = parts[0][0].shape
    tile = rows // 2
    halved = forth.shape[0] != rows
    came = pl.BlockSpec((tile, width), (lambda i, ids: (0, 0)) if halved else (lambda i, ids: (i, 0)))
    whole = pl.BlockSpec((tile, width), lambda i, ids: (i, 0))
    return pl.pallas_call(
        functools.partial(step_sum_kernel, (len(ahead), len(behind)), halved),
        grid_spec=pltpu.PrefetchScalarGridSpec(
            num_scalar_prefetch=1,
            grid=(2,),
            in_specs=[
                pl.BlockSpec((1, tile, width), lambda i, ids, k=k: (ids[k], i, 0))
                for k in range(len(parts))
            ]
            + [came, came],
            out_specs=[whole, whole],
        ),
        out_shape=[jax.ShapeDtypeStruct((rows, width), bf16)] * 2,
        cost_estimate=cost(3),
        name="step_sum",
    )(ids, *[array for array, _ in parts], forth, back)


def block_sum(parts):
    total = 0.0
    for array, place in parts:
        block = array if array.ndim == 2 else lax.dynamic_index_in_dim(array, place, 0, False)
        total = total + block.astype(f32)
    return total.astype(bf16)


def after(value, earlier):
    return lax.optimization_barrier((value, earlier))[0]


def together(*values):
    return lax.optimization_barrier(values)


class Ring:
    def __init__(self, rows, cols):
        self.rows, self.cols = rows, cols
        self.cores = CORES if cols % CORES == 0 else 1
        self.groups = cols // self.cores
        self.order = [
            (row, group)
            for group in range(self.groups)
            for row in (range(rows) if group % 2 == 0 else range(rows - 1, -1, -1))
        ]
        self.size = len(self.order)
        self.clockwise = self.shift(1)
        self.counter = self.shift(-1)
        self.sibling = [
            (row * cols + col, row * cols + col - col % self.cores + (col + 1) % self.cores)
            for row in range(rows)
            for col in range(cols)
        ]
        row, col = lax.axis_index("row"), lax.axis_index("col")
        group = col // self.cores
        self.core = col % self.cores
        self.place = group * rows + jnp.where(group % 2 == 0, row, rows - 1 - row)

    def shift(self, step):
        pairs = []
        for at, (row, group) in enumerate(self.order):
            to_row, to_group = self.order[(at + step) % self.size]
            for core in range(self.cores):
                pairs.append(
                    (
                        row * self.cols + group * self.cores + core,
                        to_row * self.cols + to_group * self.cores + core,
                    )
                )
        return pairs

    def chip(self, distance):
        at = (self.place + distance + self.size) % self.size
        group = at // self.rows
        along = at % self.rows
        return jnp.where(group % 2 == 0, along, self.rows - 1 - along), group

    def owners(self, distance):
        row, group = self.chip(distance)
        return [(row, group * self.cores + (self.core + k) % self.cores) for k in range(self.cores)]

    def block_ids(self, distance):
        return [col * self.rows + row for row, col in self.owners(distance)]

    def from_siblings(self, block):
        return [block] + [lax.ppermute(block, PLANE, self.sibling)] * (self.cores - 1)

    def gather_steps(self, block):
        forth = back = block
        yield [(block, 0)]
        for step in range(1, (self.size + 1) // 2):
            forth = lax.ppermute(forth, PLANE, self.clockwise)
            back = lax.ppermute(back, PLANE, self.counter)
            sent = yield [(forth, -step), (back, step)]
            if sent is not None:
                forth, back = sent
        if self.size % 2 == 0:
            half = block.shape[0] // 2
            forth = lax.ppermute(forth[:half], PLANE, self.clockwise)
            back = lax.ppermute(back[half:], PLANE, self.counter)
            yield [(jnp.concatenate([forth, back], axis=0), self.size // 2)]

    def with_siblings(self, arrival):
        return [
            pair
            for piece, distance in arrival
            for pair in zip(self.from_siblings(piece), self.block_ids(distance))
        ]

    def place_blocks(self, box, pairs):
        blocks, ids = zip(*pairs)
        count = len(blocks)

        def kernel(ids_ref, *refs):
            step = pl.program_id(0)
            for k in range(count):

                @pl.when(step == k)
                def _():
                    refs[-1][0] = refs[k][...]

        whole = pl.BlockSpec(blocks[0].shape, lambda i, ids: (0,) * blocks[0].ndim)
        return pl.pallas_call(
            kernel,
            grid_spec=pltpu.PrefetchScalarGridSpec(
                num_scalar_prefetch=1,
                grid=(count,),
                in_specs=[whole] * count + [pl.BlockSpec(memory_space=pl.ANY)],
                out_specs=pl.BlockSpec(
                    (1,) + blocks[0].shape, lambda i, ids: (ids[i],) + (0,) * blocks[0].ndim
                ),
            ),
            out_shape=jax.ShapeDtypeStruct(box.shape, box.dtype),
            input_output_aliases={count + 1: 0},
            cost_estimate=cost(count),
            name="place_blocks",
        )(jnp.stack(ids).astype(jnp.int32), *blocks, box)

    def gather_array(self, block):
        box = unwritten((self.rows * self.cols,) + block.shape, block.dtype)
        for arrival in self.gather_steps(block):
            box = self.place_blocks(box, self.with_siblings(arrival))
        return box

    def for_siblings(self, *others):
        return [lax.ppermute(other, PLANE, self.sibling) for other in others]

    def scatter(self, parts):
        return Scatter(self, parts)

    def sum_steps(self, values, kind=f32):
        rows, cols = self.rows, self.cols
        if rows & (rows - 1) or cols & (cols - 1):
            yield lax.psum(values, PLANE)
            return
        swaps = []
        bit = 1
        while bit < cols:
            swaps.append(lambda row, col, bit=bit: (row, col ^ bit))
            bit *= 2
        bit = 1
        while bit < rows:
            swaps.append(lambda row, col, bit=bit: (row ^ bit, col))
            bit *= 2
        for swap in swaps:
            pairs = []
            for row in range(rows):
                for col in range(cols):
                    to_row, to_col = swap(row, col)
                    pairs.append((row * cols + col, to_row * cols + to_col))
            sent = values.astype(kind)
            values = sent.astype(f32) + lax.ppermute(sent, PLANE, pairs).astype(f32)
            yield values

    def small_sum(self, values):
        *_, last = self.sum_steps(values)
        return last


class Scatter:
    def __init__(self, ring, parts):
        self.ring, self.parts = ring, parts
        self.step = ring.size // 2
        self.going = None

    def ready(self):
        ring, step = self.ring, self.step
        if 2 * step == ring.size:
            far = block_sum(self.parts(step))
            half = far.shape[0] // 2
            self.going = far[:half], far[half:]
        elif self.going is None:
            self.going = block_sum(self.parts(step)), block_sum(self.parts(-step))
        else:
            self.going = tuple(step_sum(self.parts(step), self.parts(-step), *self.going))

    def move(self):
        forth, back = self.going
        self.going = (
            lax.ppermute(forth, PLANE, self.ring.clockwise),
            lax.ppermute(back, PLANE, self.ring.counter),
        )
        self.step -= 1

    def tie(self, *values):
        self.going, *values = together(self.going, *values)
        return values

    def total(self):
        own = [
            array if array.ndim == 2 else lax.dynamic_index_in_dim(array, place, 0, False)
            for array, place in self.parts(0)
        ]
        return *own, *self.going


def dp_sum(part):
    count = lax.axis_size("dp")
    rank = lax.axis_index("dp")
    if count == 1:
        return part(rank)
    onward = [(d, (d + 1) % count) for d in range(count)]
    total = part((rank + count - 1) % count)
    for step in range(1, count):
        arrived = lax.ppermute(total.astype(bf16), "dp", onward)
        total = part((rank + 2 * count - 1 - step) % count) + arrived.astype(f32)
    return total


def dp_all_sum(values, kind=f32):
    count = lax.axis_size("dp")
    if count & (count - 1):
        return lax.psum(values, "dp")
    bit = 1
    while bit < count:
        sent = values.astype(kind)
        swapped = lax.ppermute(sent, "dp", [(d, d ^ bit) for d in range(count)])
        values = sent.astype(f32) + swapped.astype(f32)
        bit *= 2
    return values


def exchange_rows(pieces):
    rows = pieces.shape[0]
    row = lax.axis_index("row")
    start = lambda at: (at,) + (0,) * (pieces.ndim - 1)
    taken = unwritten(pieces.shape, pieces.dtype)
    own = lax.dynamic_index_in_dim(pieces, row, 0, True)
    taken = lax.dynamic_update_slice(taken, own, start(row))
    for step in range(1, rows):
        sent = lax.dynamic_index_in_dim(pieces, (row + step) % rows, 0, True)
        sent = lax.ppermute(sent, "row", [(r, (r + step) % rows) for r in range(rows)])
        taken = lax.dynamic_update_slice(taken, sent, start((row + rows - step) % rows))
    return taken


def exchange(pieces, axes):
    return lax.all_to_all(pieces, axes, split_axis=0, concat_axis=0, tiled=True)


def project_kernel(x_ref, gain_ref, weight_ref, out_ref, inverse_ref, squares_ref, low_ref):
    blocks, _, width = x_ref.shape
    total = 0.0
    for block in range(blocks):
        part = x_ref[block].astype(f32)
        total = total + jnp.sum(part * part, axis=1, keepdims=True)
    inverse = lax.rsqrt(total / D + norm_epsilon)
    for block in range(blocks):
        at = pl.ds(block * width, width)
        low_ref[:, at] = (x_ref[block].astype(f32) * inverse * gain_ref[:, at]).astype(bf16)
    out = dot_nn(low_ref[...], weight_ref[...])
    out_ref[...] = out
    inverse_ref[...] = as_row(inverse)
    for j in range(2):
        part = out[:, j * HD : (j + 1) * HD]
        squares_ref[pl.ds(j, 1), :] = as_row(jnp.sum(part * part, axis=1, keepdims=True))


def project(x_blocks, block_rows, gain_row, weight, rows):
    count, _, width = x_blocks.shape
    cols = count // rows
    tile = block_rows
    per = block_rows // tile
    length = cols * block_rows
    return pl.pallas_call(
        project_kernel,
        grid=(cols * per,),
        in_specs=[
            pl.BlockSpec((rows, tile, width), lambda i: (i // per, i % per, 0)),
            pl.BlockSpec((1, D), lambda i: (0, 0)),
            pl.BlockSpec(weight.shape, lambda i: (0, 0)),
        ],
        out_specs=[
            pl.BlockSpec((tile, 3 * HD), lambda i: (i, 0)),
            pl.BlockSpec((1, tile), lambda i: (0, i)),
            pl.BlockSpec((2, tile), lambda i: (0, i)),
        ],
        scratch_shapes=[pltpu.VMEM((tile, D), bf16)],
        out_shape=[
            jax.ShapeDtypeStruct((length, 3 * HD), f32),
            jax.ShapeDtypeStruct((1, length), f32),
            jax.ShapeDtypeStruct((2, length), f32),
        ],
        compiler_params=pltpu.CompilerParams(vmem_limit_bytes=52 * 2**20),
        cost_estimate=cost(14),
        name="norm_and_project",
    )(x_blocks, gain_row, weight)


def project_weight_kernel(x_ref, gain_ref, inverse_ref, grad_ref, weight_ref, out_ref, term_ref, low_ref):
    blocks, _, width = x_ref.shape
    inverse = as_column(inverse_ref[...])

    @pl.when(pl.program_id(0) == 0)
    def _():
        out_ref[...] = jnp.zeros_like(out_ref)

    for block in range(blocks):
        at = pl.ds(block * width, width)
        low_ref[:, at] = (x_ref[block].astype(f32) * inverse * gain_ref[:, at]).astype(bf16)
    for block in range(blocks):
        at = pl.ds(block * width, width)
        total = dot_nn(low_ref[:, at].T, grad_ref[...])
        for j in range(3):
            out_ref[block, j] += total[:, j * HD : (j + 1) * HD]

    @pl.when(pl.program_id(0) == pl.num_programs(0) - 1)
    def _():
        for block in range(blocks):
            at = pl.ds(block * width, width)
            total = 0.0
            for j in range(3):
                total = total + out_ref[block, j] * weight_ref[at, j * HD : (j + 1) * HD].astype(f32)
            total = as_row(jnp.sum(total, axis=1, keepdims=True))
            term_ref[:, at] = total / gain_ref[:, at]


def project_weight(x_blocks, block_rows, gain_row, inverse, grads, weight, rows):
    count, _, width = x_blocks.shape
    cols = count // rows
    tile = block_rows // 3 if block_rows % 384 == 0 else block_rows
    per = block_rows // tile
    return pl.pallas_call(
        project_weight_kernel,
        grid=(cols * per,),
        in_specs=[
            pl.BlockSpec((rows, tile, width), lambda i: (i // per, i % per, 0)),
            pl.BlockSpec((1, D), lambda i: (0, 0)),
            pl.BlockSpec((1, tile), lambda i: (0, i)),
            pl.BlockSpec((tile, 3 * HD), lambda i: (i, 0)),
            pl.BlockSpec(weight.shape, lambda i: (0, 0)),
        ],
        out_specs=[
            pl.BlockSpec((rows, 3, width, HD), lambda i: (0, 0, 0, 0)),
            pl.BlockSpec((1, D), lambda i: (0, 0)),
        ],
        scratch_shapes=[pltpu.VMEM((tile, D), bf16)],
        out_shape=[
            jax.ShapeDtypeStruct((rows, 3, width, HD), f32),
            jax.ShapeDtypeStruct((1, D), f32),
        ],
        compiler_params=pltpu.CompilerParams(vmem_limit_bytes=40 * 2**20),
        cost_estimate=cost(15),
        name="projection_weight_gradient",
    )(x_blocks, gain_row, inverse, grads, weight)


def turn_kernel(raw_ref, squares_ref, gain_ref, cosine_ref, sine_ref, q_ref, k_ref, v_ref, k_flip_ref, v_flip_ref):
    inverse = lax.rsqrt(squares_ref[...] / D + norm_epsilon)
    for j, out_ref in ((0, q_ref), (1, k_ref)):
        normed = raw_ref[:, j * HD : (j + 1) * HD] * as_column(inverse[j : j + 1]) * gain_ref[j : j + 1, :]
        turned = normed * cosine_ref[...] + jnp.roll(normed, HD // 2, axis=1) * sine_ref[...]
        out_ref[...] = turned.astype(bf16)
        if j == 1:
            k_flip_ref[...] = turned.T.astype(bf16)
    v = raw_ref[:, 2 * HD :]
    v_ref[...] = v.astype(bf16)
    v_flip_ref[...] = v.T.astype(bf16)


def turn(raw, squares, gain_pair, cosine, sine_part):
    length = raw.shape[0]
    tile = min(1024, length)
    tall = pl.BlockSpec((tile, HD), lambda i: (i, 0))
    wide = pl.BlockSpec((HD, tile), lambda i: (0, i))
    tall_shape = jax.ShapeDtypeStruct((length, HD), bf16)
    wide_shape = jax.ShapeDtypeStruct((HD, length), bf16)
    return pl.pallas_call(
        turn_kernel,
        grid=(length // tile,),
        in_specs=[
            pl.BlockSpec((tile, 3 * HD), lambda i: (i, 0)),
            pl.BlockSpec((2, tile), lambda i: (0, i)),
            pl.BlockSpec((2, HD), lambda i: (0, 0)),
            tall,
            tall,
        ],
        out_specs=[tall, tall, tall, wide, wide],
        out_shape=[tall_shape, tall_shape, tall_shape, wide_shape, wide_shape],
        cost_estimate=cost(7.4),
        name="query_key_value",
    )(raw, squares, gain_pair, cosine, sine_part)


def branch_kernel(
    groups, sets, at_ref, heads_ref, x_ref, gain_ref, *refs
):
    weights, (residual_ref, low_ref) = refs[: groups * sets], refs[groups * sets :]
    step = pl.program_id(0)
    rows, width = x_ref.shape[0], x_ref.shape[2]
    height = weights[0].shape[1]
    per = height // HD
    branch = x_ref[pl.ds(step, 1)][0].astype(f32)
    for group in range(groups):
        for k in range(sets):
            first = at_ref[2 + group * sets + k]
            heads = jnp.concatenate([heads_ref[first + j] for j in range(per)], axis=1)
            branch = branch + dot_nn(heads, weights[group * sets + k][0])
    residual_ref[:, pl.ds(pl.multiple_of(step * width, width), width)] = branch

    @pl.when(step == rows - 1)
    def _():
        total = residual_ref[...]
        inverse = lax.rsqrt(jnp.sum(total * total, axis=1, keepdims=True) / D + norm_epsilon)
        low_ref[...] = (total * inverse * gain_ref[...]).astype(bf16)


def output_branch(at, table, heads, weight_sets, x_blocks, gain_row, rows, groups):
    tok_rows = heads.shape[1]
    sets = len(weight_sets)
    width = x_blocks.shape[2]
    height = D // (2 * rows)
    fixed = lambda shape: pl.BlockSpec(shape, lambda i, a, t: (0,) * len(shape))
    return pl.pallas_call(
        lambda at_ref, table_ref, *refs: branch_kernel(groups, sets, at_ref, *refs),
        grid_spec=pltpu.PrefetchScalarGridSpec(
            num_scalar_prefetch=2,
            grid=(rows,),
            in_specs=[
                fixed(heads.shape),
                pl.BlockSpec((rows, tok_rows, width), lambda i, a, t: (a[0], a[1], 0)),
                fixed((1, D)),
            ]
            + [
                pl.BlockSpec(
                    (1, height, width),
                    lambda i, a, t, g=g, k=k, half=half: (t[(k * groups + g) * rows + i], half, 0),
                )
                for g in range(groups)
                for k, (_, half) in enumerate(weight_sets)
            ],
            out_specs=[fixed((tok_rows, D)), fixed((tok_rows, D))],
        ),
        out_shape=[
            jax.ShapeDtypeStruct((tok_rows, D), f32),
            jax.ShapeDtypeStruct((tok_rows, D), bf16),
        ],
        compiler_params=pltpu.CompilerParams(vmem_limit_bytes=40 * 2**20),
        cost_estimate=cost(6),
        name="output_projection",
    )(at, table, heads, x_blocks, gain_row, *[w for _ in range(groups) for w, _ in weight_sets])


def resid_kernel(
    at_ref, logit_ref, router_ref, residual_ref, up_ref, gain_ref, *refs,
):
    terms, (grad_low_ref, gain_term_ref) = refs[:-2], refs[-2:]
    rows, width = up_ref.shape[0], up_ref.shape[2]
    grad = sum(ref[...].astype(f32) for ref in terms)
    grad = grad + dot_nn(logit_ref[...], router_ref[...])
    residual = residual_ref[...]
    inverse = lax.rsqrt(jnp.sum(residual * residual, axis=1, keepdims=True) / D + norm_epsilon)
    scaled = grad * gain_ref[...]
    total = jnp.sum(scaled * residual, axis=1, keepdims=True)
    gain_term_ref[...] = jnp.sum(grad * residual * inverse, axis=0, keepdims=True)
    back = inverse * scaled - residual * (inverse * inverse * inverse * total / D)
    for row in range(rows):
        at = pl.ds(row * width, width)
        grad_low_ref[:, at] = (
            up_ref[row].astype(f32) + back[:, row * width : (row + 1) * width]
        ).astype(bf16)


def residual_back(at, terms, grad_logits, router_flip, residual, up_blocks, gain_row, rows):
    tok_rows = residual.shape[0]
    width = up_blocks.shape[2]
    fixed = lambda shape: pl.BlockSpec(shape, lambda i, a: (0,) * len(shape))
    whole, line = fixed((tok_rows, D)), fixed((1, D))
    return pl.pallas_call(
        resid_kernel,
        grid_spec=pltpu.PrefetchScalarGridSpec(
            num_scalar_prefetch=1,
            grid=(1,),
            in_specs=[
                fixed(grad_logits.shape),
                fixed(router_flip.shape),
                whole,
                pl.BlockSpec((rows, tok_rows, width), lambda i, a: (a[0], a[1], 0)),
                line,
            ]
            + [whole] * len(terms),
            out_specs=[whole, line],
        ),
        out_shape=[
            jax.ShapeDtypeStruct((tok_rows, D), bf16),
            jax.ShapeDtypeStruct((1, D), f32),
        ],
        compiler_params=pltpu.CompilerParams(vmem_limit_bytes=40 * 2**20),
        cost_estimate=cost(3),
        name="residual_backward",
    )(at, grad_logits, router_flip, residual, up_blocks, gain_row, *terms)


def dispatch_kernel(hits_ref, x_ref, out_ref):
    experts, _, capacity, _ = out_ref.shape
    width = x_ref.shape[2]
    for block in range(x_ref.shape[0]):
        picked = dot_nn(hits_ref[0], x_ref[block]).astype(bf16)
        for e in range(experts):
            out_ref[e, 0, :, pl.ds(block * width, width)] = picked[e * capacity : (e + 1) * capacity]


def dispatch_blocks(hits, x_blocks, rows, experts):
    group, slot_rows, tok_rows = hits.shape
    width = x_blocks.shape[2]
    capacity = slot_rows // experts
    return pl.pallas_call(
        dispatch_kernel,
        grid=(group,),
        in_specs=[
            pl.BlockSpec((1, slot_rows, tok_rows), lambda b: (b, 0, 0)),
            pl.BlockSpec((rows, tok_rows, width), lambda b: (b // rows, b % rows, 0)),
        ],
        out_specs=pl.BlockSpec((experts, 1, capacity, D), lambda b: (0, b, 0, 0)),
        out_shape=jax.ShapeDtypeStruct((experts, group, capacity, D), bf16),
        cost_estimate=cost(14),
        name="cotangent_to_slots",
    )(hits, x_blocks)


def experts_kernel(count, first, ids_ref, *refs):
    feats = refs[:count]
    raws = refs[count : 2 * count]
    hits_ref, flip_ref, router_ref, gate_w_ref, up_w_ref = refs[2 * count : 2 * count + 5]
    rest = refs[2 * count + 5 :]
    if not first:
        rest = rest[5:]
    slot_ref, hidden_ref, grad_gate_ref, grad_up_ref, scale_ref = rest[:5]
    feat_sums = rest[5 : 5 + count]
    probs_ref, later_ref, in_acc, in_all = rest[5 + count :]
    rows = slot_ref.shape[1]
    e, f = pl.program_id(0), pl.program_id(1)
    last_expert = e == pl.num_programs(0) - 1
    last_tile = f == pl.num_programs(1) - 1
    capacity = raws[0].shape[2]
    chosen = ids_ref[count] + e
    own_slots = pl.ds(pl.multiple_of(e * capacity, 16), capacity)

    @pl.when((e == 0) & (f == 0))
    def _():
        for k in range(count):
            logits = dot_nt(router_ref[...], feats[k][...])
            raised = jnp.exp(logits - jnp.max(logits, axis=0, keepdims=True))
            probs_ref[k] = raised / jnp.sum(raised, axis=0, keepdims=True)
            picked = dot_nn(hits_ref[ids_ref[k]], feats[k][...]).astype(bf16)
            slot_ref[0, pl.ds(k * capacity, capacity), :] = picked[:capacity]
            for j in range(1, picked.shape[0] // capacity):
                at = pl.ds((j - 1) * rows + k * capacity, capacity)
                later_ref[at, :] = picked[j * capacity : (j + 1) * capacity]

    @pl.when((e > 0) & (f == 0))
    def _():
        slot_ref[0] = later_ref[pl.ds(pl.multiple_of((e - 1) * rows, 16), rows), :]

    @pl.when(f == 0)
    def _():
        for k in range(count):
            at = pl.ds(k * capacity, capacity)
            hits = hits_ref[ids_ref[k], own_slots, :]
            probs = probs_ref[k]
            rank = lax.broadcasted_iota(jnp.int32, probs.shape, 0)
            gate = jnp.sum(jnp.where(rank == chosen, probs, 0.0), axis=0, keepdims=True)
            scale_ref[0, at, :] = jnp.sum(hits.astype(f32) * gate, axis=1, keepdims=True)

    slots = slot_ref[0]
    gate_w, up_w = gate_w_ref[0], up_w_ref[0]
    gate_pre = dot_nn(slots, gate_w)
    up_pre = dot_nn(slots, up_w)
    sigmoid = 1.0 / (1.0 + jnp.exp(-gate_pre))
    silu = gate_pre * sigmoid
    hidden_ref[0] = (silu * up_pre).astype(bf16)
    grad_hidden = jnp.concatenate([raw[0, 0] for raw in raws], axis=0) * scale_ref[0]
    grad_gate = (grad_hidden * up_pre * sigmoid * (1.0 + gate_pre * (1.0 - sigmoid))).astype(bf16)
    grad_up = (grad_hidden * silu).astype(bf16)
    grad_gate_ref[0] = grad_gate
    grad_up_ref[0] = grad_up
    in_term = dot_nt(grad_gate, gate_w) + dot_nt(grad_up, up_w)

    @pl.when(f == 0)
    def _():
        in_acc[...] = in_term

    @pl.when(f > 0)
    def _():
        in_acc[...] += in_term

    @pl.when(last_tile)
    def _():
        for k in range(count):
            in_all[k, own_slots, :] = in_acc[pl.ds(k * capacity, capacity), :].astype(bf16)

    @pl.when(last_tile & last_expert)
    def _():
        for k in range(count):
            feat_sums[k][...] = dot_nn(flip_ref[ids_ref[k]], in_all[k]).astype(bf16)


def run_experts(feats, ids, first_expert, grad_raw, hits, flip, router_flip, expand_weight, carried, place):
    count = len(feats)
    experts, group, capacity, _ = grad_raw.shape
    tok_rows = feats[0].shape[0]
    rows = count * capacity
    tile = F // 2
    tiles = F // tile
    first = carried is None
    whole = lambda shape: pl.BlockSpec(shape, lambda e, f, ids: (0,) * len(shape))
    once = lambda shape: pl.BlockSpec(
        shape, lambda e, f, ids: (0,) * len(shape), pipeline_mode=pl.Buffered(1)
    )
    in_specs = [once((tok_rows, D))] * count
    in_specs += [
        pl.BlockSpec((1, 1, capacity, tile), lambda e, f, ids, k=k: (e, ids[k], 0, f))
        for k in range(count)
    ]
    in_specs += [
        once(hits.shape),
        once(flip.shape),
        once(router_flip.shape),
        pl.BlockSpec((1, D, tile), lambda e, f, ids: (e, 0, f)),
        pl.BlockSpec((1, D, tile), lambda e, f, ids: (e, 0, f + tiles)),
    ]
    operands = [*feats, *[grad_raw] * count, hits, flip, router_flip, expand_weight, expand_weight]
    aliases = {}
    if not first:
        in_specs += [pl.BlockSpec(memory_space=pl.ANY)] * 5
        operands += carried
        aliases = {1 + len(operands) - 5 + k: k for k in range(5)}
    wide = pl.BlockSpec((1, rows, D), lambda e, f, ids: (e, place, 0))
    narrow = pl.BlockSpec((1, rows, tile), lambda e, f, ids: (e, place, f))
    thin = pl.BlockSpec((1, rows, 1), lambda e, f, ids: (e, place, 0))
    narrow_shape = jax.ShapeDtypeStruct((experts, group * capacity, F), bf16)
    out = pl.pallas_call(
        functools.partial(experts_kernel, count, first),
        grid_spec=pltpu.PrefetchScalarGridSpec(
            num_scalar_prefetch=1,
            grid=(experts, tiles),
            in_specs=in_specs,
            out_specs=[wide, narrow, narrow, narrow, thin] + [whole((tok_rows, D))] * count,
            scratch_shapes=[
                pltpu.VMEM((count, router_flip.shape[0], tok_rows), f32),
                pltpu.VMEM((max(experts - 1, 1) * rows, D), bf16),
                pltpu.VMEM((rows, D), f32),
                pltpu.VMEM((count, experts * capacity, D), bf16),
            ],
        ),
        out_shape=[jax.ShapeDtypeStruct((experts, group * capacity, D), bf16)]
        + [narrow_shape] * 3
        + [jax.ShapeDtypeStruct((experts, group * capacity, 1), f32)]
        + [jax.ShapeDtypeStruct((tok_rows, D), bf16)] * count,
        input_output_aliases=aliases,
        compiler_params=pltpu.CompilerParams(vmem_limit_bytes=58 * 2**20),
        cost_estimate=cost(13 + 2 * count),
        name="experts",
    )(jnp.stack([*ids, first_expert]).astype(jnp.int32), *operands)
    return out[:5], out[5:]


def combine_kernel(cores, ids_ref, slot_ref, out_ref, up_ref, hits_ref, flip_ref, scale_ref, gates_ref, grad_out_ref, *moe_refs):
    experts, _, capacity, _ = out_ref.shape
    scaled = []
    for e in range(experts):
        expert_out = out_ref[e, 0].astype(f32)
        upstream = up_ref[e, 0].astype(f32)
        scale = scale_ref[e, 0]
        dots = jnp.sum(expert_out * upstream, axis=1, keepdims=True)
        hits = hits_ref[0, e * capacity : (e + 1) * capacity, :].astype(f32)
        gates_ref[0, pl.ds(e, 1), :] = jnp.sum(hits * dots, axis=0, keepdims=True)
        grad_out_ref[e, 0] = (upstream * scale).astype(bf16)
        scaled.append((expert_out * scale).astype(bf16))
    total = dot_nn(flip_ref[0], jnp.concatenate(scaled, axis=0)).astype(bf16)
    for k in range(cores):

        @pl.when(slot_ref[2 * pl.program_id(0)] == k)
        def _():
            moe_refs[k][0] = total


def combine_experts(ids, chips, expert_out, upstream_slots, hits, flip, scale, cores):
    experts, group, capacity, _ = upstream_slots.shape
    tok_rows = hits.shape[2]
    by_place = pl.BlockSpec((experts, 1, capacity, D), lambda j, ids, at: (0, j, 0, 0))
    by_id = lambda shape: pl.BlockSpec((1,) + shape, lambda j, ids, at: (ids[j], 0, 0))
    order = []
    for distance, _ in chips:
        if distance not in order:
            order.append(distance)
    slots = []
    for j, (_, k) in enumerate(chips):
        slots += [k, 0]
    places = []
    for core in range(cores):
        mine = [(j, order.index(distance)) for j, (distance, k) in enumerate(chips) if k == core]
        for j in range(group):
            later = [place for at, place in mine if at >= j]
            places.append(later[0] if later else mine[-1][1])
    table = jnp.array(slots + places, jnp.int32)
    gates, grad_out, *sums = pl.pallas_call(
        functools.partial(combine_kernel, cores),
        grid_spec=pltpu.PrefetchScalarGridSpec(
            num_scalar_prefetch=2,
            grid=(group,),
            in_specs=[
                by_place,
                pl.BlockSpec((experts, 1, capacity, D), lambda j, ids, at: (0, ids[j], 0, 0)),
                by_id(hits.shape[1:]),
                by_id(flip.shape[1:]),
                pl.BlockSpec((experts, 1, capacity, 1), lambda j, ids, at: (0, j, 0, 0)),
            ],
            out_specs=[by_id((experts, tok_rows)), by_place]
            + [
                pl.BlockSpec(
                    (1, tok_rows, D),
                    lambda j, ids, at, k=k: (at[2 * group + k * group + j], 0, 0),
                )
                for k in range(cores)
            ],
        ),
        out_shape=[
            jax.ShapeDtypeStruct((group, experts, tok_rows), f32),
            jax.ShapeDtypeStruct((experts, group, capacity, D), bf16),
        ]
        + [jax.ShapeDtypeStruct((group // cores, tok_rows, D), bf16)] * cores,
        compiler_params=pltpu.CompilerParams(vmem_limit_bytes=40 * 2**20),
        cost_estimate=cost(18),
        name="experts_combine",
    )(
        ids,
        table,
        expert_out.reshape(experts, group, capacity, D),
        upstream_slots,
        hits,
        flip,
        scale.reshape(experts, group, capacity, 1),
    )
    return gates, grad_out, sums, order


def weight_grad_kernel(sides, added, pieces, filled, rank_ref, left_ref, *refs):
    rights, refs = refs[:sides], refs[sides:]
    more, refs = refs[:added], refs[added + filled :]
    outs, flip_ref = refs[:-1], refs[-1]
    e, m, n = pl.program_id(0), pl.program_id(1), pl.program_id(2)

    @pl.when(n == 0)
    def _():
        flip_ref[...] = left_ref[0].T

    for side in range(sides):

        @pl.when(n == side)
        def _():
            total = dot_nn(flip_ref[...], rights[side][0])
            if not added and not pieces:
                outs[0][0] = total
            for k in range(side, max(added, len(outs) if pieces else 0), sides):

                @pl.when(e * pl.num_programs(1) + m == k // sides)
                def _():
                    grown = total + more[k][...].astype(f32) if added else total
                    if pieces:
                        outs[k][...] = grown.astype(bf16)
                    else:
                        outs[0][0] = grown


def weight_grad(left, rights, rank, rows, first=0, experts=None, more=(), pieces=False, into=None):
    experts = left.shape[0] if experts is None else experts
    slots = left.shape[1]
    tile = min(512, rows)
    per = rows // tile
    width = F
    shares = [(right, j) for right in rights for j in range(right.shape[2] // width)]
    sides = len(shares)
    piece = pl.BlockSpec((tile, width), lambda e, m, n, p: (0, 0))
    if pieces:
        out_specs = [piece] * (experts * per * sides)
        out_shape = [jax.ShapeDtypeStruct((tile, width), bf16)] * (experts * per * sides)
    else:
        out_specs = [pl.BlockSpec((1, tile, width), lambda e, m, n, p: (e + first, m, n))]
        out_shape = [jax.ShapeDtypeStruct((left.shape[0], rows, sides * width), f32)]
    out = pl.pallas_call(
        functools.partial(weight_grad_kernel, sides, len(more), pieces, into is not None),
        grid_spec=pltpu.PrefetchScalarGridSpec(
            num_scalar_prefetch=1,
            grid=(experts, per, sides),
            in_specs=[
                pl.BlockSpec((1, slots, tile), lambda e, m, n, p: (e + first, 0, p[0] * per + m))
            ]
            + [
                pl.BlockSpec((1, slots, width), lambda e, m, n, p, j=j: (e + first, 0, j))
                for _, j in shares
            ]
            + [piece] * len(more)
            + [pl.BlockSpec(memory_space=pl.ANY)] * (into is not None),
            out_specs=out_specs,
            scratch_shapes=[pltpu.VMEM((tile, slots), bf16)],
        ),
        out_shape=out_shape,
        input_output_aliases={} if into is None else {2 + sides + len(more): 0},
        compiler_params=pltpu.CompilerParams(vmem_limit_bytes=48 * 2**20),
        cost_estimate=cost(experts * rows * sides / 560 * (2 if more else 1.7)),
        name="weight_gradient",
    )(
        rank.reshape(1).astype(jnp.int32), left, *[right for right, _ in shares], *more,
        *([] if into is None else [into]),
    )
    return out if pieces else out[0]


def weight_grad_sends(left, rights, rows, first, experts):
    count = lax.axis_size("dp")
    rank = lax.axis_index("dp")
    onward = [(d, (d + 1) % count) for d in range(count)]
    sent, arrived = [], []
    for e in range(first, first + experts):
        more = []
        for step in range(1, count):
            parts = weight_grad(left, rights, (rank + count - step) % count, rows, e, 1, more, True)
            more = [lax.ppermute(part, "dp", onward) for part in parts]
        sent += parts if more else []
        arrived += more
    return sent, arrived


def unturn(grad, cosine, sine_part):
    return grad * cosine - jnp.roll(grad, HD // 2, axis=1) * sine_part


def unproject_kernel(
    grad_q_ref, grad_k_ref, grad_v_ref, raw_ref, squares_ref, dots_ref, gain_ref, cosine_ref, sine_ref,
    weight_ref, grad_ref, gain_terms_ref, out_ref,
):
    rows, _, width = out_ref.shape
    inverse = lax.rsqrt(squares_ref[...] / D + norm_epsilon)
    inner = inverse * inverse * dots_ref[:2] / D

    @pl.when(pl.program_id(0) == 0)
    def _():
        gain_terms_ref[...] = jnp.zeros_like(gain_terms_ref)

    for j, part_ref in ((0, grad_q_ref), (1, grad_k_ref)):
        grad = unturn(part_ref[...], cosine_ref[...], sine_ref[...])
        column = as_column(inverse[j : j + 1])
        raw = raw_ref[:, j * HD : (j + 1) * HD]
        gain_terms_ref[pl.ds(j, 1), :] += jnp.sum(grad * raw * column, axis=0, keepdims=True)
        back = column * grad * gain_ref[j : j + 1, :] - raw * as_column(inner[j : j + 1])
        grad_ref[:, pl.ds(j * HD, HD)] = back.astype(bf16)
    grad_ref[:, pl.ds(2 * HD, HD)] = grad_v_ref[...].astype(bf16)
    for row in range(rows):
        at = pl.ds(row * width, width)
        out_ref[row] = dot_nn(grad_ref[...], weight_ref[:, at]).astype(bf16)


def unproject(grads, raw, squares, dots, gain_pair, cosine, sine_part, weight_flip, rows, cols):
    length = raw.shape[0]
    block_rows, width = length // cols, D // rows
    tile = block_rows
    tall = pl.BlockSpec((tile, HD), lambda i: (i, 0))
    three = pl.BlockSpec((tile, 3 * HD), lambda i: (i, 0))
    pair = pl.BlockSpec((2, tile), lambda i: (0, i))
    trio = pl.BlockSpec((3, tile), lambda i: (0, i))
    fixed = pl.BlockSpec((2, HD), lambda i: (0, 0))
    return pl.pallas_call(
        unproject_kernel,
        grid=(length // tile,),
        in_specs=[
            tall, tall, tall, three, pair, trio, fixed, tall, tall,
            pl.BlockSpec(weight_flip.shape, lambda i: (0, 0)),
        ],
        out_specs=[
            three, fixed, pl.BlockSpec((rows, tile, width), lambda i: (i, 0, 0)),
        ],
        out_shape=[
            jax.ShapeDtypeStruct((length, 3 * HD), bf16),
            jax.ShapeDtypeStruct((2, HD), f32),
            jax.ShapeDtypeStruct((rows * cols, block_rows, width), bf16),
        ],
        compiler_params=pltpu.CompilerParams(vmem_limit_bytes=52 * 2**20),
        cost_estimate=cost(15.5),
        name="projection_backward",
    )(*grads, raw, squares, dots, gain_pair, cosine, sine_part, weight_flip)


def norm_back(values, inverse, gain_row, upstream, dot_total):
    scaled = upstream * gain_row
    return inverse[:, None] * scaled - values * (inverse**3 * dot_total / D)[:, None]


def dot(a, b):
    return jnp.dot(a, b, preferred_element_type=f32)


def einsum(spec, a, b):
    return jnp.einsum(spec, a, b, preferred_element_type=f32)


def on_device(
    layer_input,
    gains,
    qkv_weight,
    output_weight,
    router_weight,
    expand_weight,
    reduce_weight,
    routes,
    drop_order,
    prefix_len,
    cotangent,
):
    row_rank, col_rank = lax.axis_index("row"), lax.axis_index("col")
    rows, cols = lax.axis_size("row"), lax.axis_size("col")
    dp_count = lax.axis_size("dp")
    group = rows * cols
    res_rows, row_width = layer_input.shape
    col_width = qkv_weight.shape[2]
    seq_len = res_rows * cols
    tok_rows = res_rows // rows
    block_rank = col_rank * rows + row_rank
    expert_rank = row_rank * cols + col_rank
    expert_count = router_weight.shape[1]
    local_experts = expand_weight.shape[0]
    capacity = tok_rows * TOP // expert_count
    ring = Ring(rows, cols)
    gain_rows = gains.astype(f32)
    router_flip = router_weight.T

    paired = dp_count % 2 == 0
    half_rank = lax.axis_index("dp") % 2 if paired else 0
    partner = [(d, d ^ 1) for d in range(dp_count)]
    halves = 2 if paired else 1
    half_rows = row_width // halves
    head_half = lax.dynamic_slice_in_dim(qkv_weight, half_rank * half_rows, half_rows, 0)
    head_half = head_half.reshape(half_rows, 3, rows, HD).transpose(2, 1, 0, 3)
    head_out = output_weight.reshape(rows, HD, row_width // HD, HD).transpose(0, 2, 1, 3)
    head_half = jnp.concatenate(
        [head_half.reshape(rows, 3 * half_rows, HD), head_out.reshape(rows, row_width, HD)], axis=1
    )
    head_half = exchange(head_half, "row")
    head_out = head_half[:, 3 * half_rows :].reshape(D, HD).reshape(D // HD, HD, HD)
    head_out = head_out.transpose(0, 2, 1).reshape(D, HD)
    head_half = head_half[:, : 3 * half_rows].reshape(rows, 3, half_rows, HD)
    head_half = head_half.transpose(0, 2, 1, 3).reshape(rows, half_rows, 3 * HD)
    half_width = HD // 2
    frequency = rope_base ** (-2.0 * jnp.arange(half_width, dtype=f32) / HD)
    angles = jnp.arange(seq_len).astype(f32)[:, None] * frequency[None, :]
    cosine, sine_part = jnp.cos(angles), jnp.sin(angles)
    cosine = jnp.concatenate([cosine, cosine], axis=1)
    sine_part = jnp.concatenate([-sine_part, sine_part], axis=1)
    own_lines = jnp.concatenate([routes.T, drop_order[None, :]], axis=0)
    lines = jnp.zeros((cols,) + own_lines.shape, jnp.int32)
    lines = lax.dynamic_update_slice(lines, own_lines[None], (col_rank, 0, 0))
    for step in range(1, cols):
        arrived = lax.ppermute(own_lines, "col", [(c, (c + step) % cols) for c in range(cols)])
        lines = lax.dynamic_update_slice(
            lines, arrived[None], ((col_rank + cols - step) % cols, 0, 0)
        )
    first_expert = expert_rank * local_experts
    own_experts = first_expert + jnp.arange(local_experts)
    member = jnp.any(lines[None, :, :TOP] == own_experts[:, None, None, None], axis=2)
    member = member.reshape(local_experts, group, tok_rows).transpose(1, 0, 2)
    drop_rank = lines[:, TOP].reshape(group, tok_rows)
    token_index = jnp.arange(tok_rows)
    earlier = (drop_rank[:, None, :] < drop_rank[:, :, None]) | (
        drop_rank[:, None, :] == drop_rank[:, :, None]
    ) & (token_index[None, None, :] < token_index[None, :, None])
    position = jnp.sum(jnp.where(earlier[:, None] & member[:, :, None, :], 1, 0), axis=-1)
    kept = member & (position < capacity)
    hits = kept[:, :, None, :] & (
        position[:, :, None, :] == jnp.arange(capacity)[None, None, :, None]
    )
    hits = hits.reshape(group, local_experts * capacity, tok_rows)
    dispatch = hits.astype(bf16)
    combine = hits.transpose(0, 2, 1).astype(bf16)

    weight_half = lax.dynamic_slice_in_dim(
        output_weight, half_rank * (col_width // 2), col_width // halves, 0
    )
    at = [col_rank, row_rank]
    for chip_group in range(ring.groups):
        for half in range(2):
            for k in range(ring.cores):
                col = chip_group * ring.cores + (ring.core + k) % ring.cores
                at.append((col * 2 + (half_rank + half) % 2) * (rows // 2))
    at = jnp.stack([jnp.asarray(value, jnp.int32) for value in at])

    x_steps = ring.gather_steps(jnp.concatenate([layer_input, weight_half], axis=0))
    x_blocks = unwritten((group, res_rows + weight_half.shape[0], row_width), bf16)
    x_blocks = ring.place_blocks(x_blocks, ring.with_siblings(next(x_steps)))
    pieces = other_half = None
    for step in range(ring.size // 2):
        arrival = x_steps.send(pieces)
        pieces = [piece for piece, _ in arrival]
        if step == 0:
            pieces, cosine, sine_part = together(pieces, cosine, sine_part)
        elif step == 1:
            pieces, head_half, x_blocks, dispatch, combine = together(
                pieces, head_half, x_blocks, dispatch, combine
            )
            other_half = lax.ppermute(head_half, "dp", partner) if paired else None
        elif step == 2:
            pieces, x_blocks = together(pieces, x_blocks)
        else:
            pieces, x_blocks, other_half = together(pieces, x_blocks, other_half)
        arrival = list(zip(pieces, [distance for _, distance in arrival]))
        x_blocks = ring.place_blocks(x_blocks, ring.with_siblings(arrival))
    if paired:
        head_weight = jnp.where(
            half_rank == 0,
            jnp.stack([head_half, other_half], axis=1),
            jnp.stack([other_half, head_half], axis=1),
        )
    else:
        head_weight = head_half
    head_weight = head_weight.reshape(D, 3 * HD)
    weight_flip = head_weight.T
    half_place = res_rows // (col_width // 2)
    table = []
    for half in range(2):
        for k in range(ring.cores):
            for chip_group in range(ring.groups):
                col = chip_group * ring.cores + (ring.core + k) % ring.cores
                for row in range(rows):
                    whole_plane = half == 0 or not paired
                    table.append(col * rows + row if whole_plane else chip_group * rows + row)
    table = jnp.stack([jnp.asarray(value, jnp.int32) for value in table])
    if paired:
        own_core = x_blocks[:, res_rows:].reshape(
            ring.groups, ring.cores, rows, weight_half.shape[0], row_width
        )
        own_core = lax.dynamic_index_in_dim(own_core, ring.core, 1, False)
        own_core = own_core.reshape(ring.size, weight_half.shape[0], row_width)
        theirs = lax.ppermute(own_core, "dp", partner)
    upstream_blocks = lax.all_gather(after(cotangent, pieces), BLOCKS, axis=0)
    projected, inv_first, square_terms = project(x_blocks, res_rows, gain_rows[0:1], head_weight, rows)
    squares = ring.small_sum(square_terms)

    head_first = block_rank * HD
    gain_pair = lax.dynamic_slice(gain_rows, (1, head_first), (2, HD))
    query_low, key_low, value_low, key_flip, value_flip = turn(
        projected, squares, gain_pair, cosine, sine_part
    )

    query_rows = max(seq_len // 6, 128)
    attn_head, lse = attention(query_low, key_low, value_flip, prefix_len, 2 * query_rows)
    attn_tokens = exchange(attn_head.reshape(group, tok_rows, HD), BLOCKS)
    weight_sets = [(x_blocks, half_place)] * ring.cores
    if paired:
        attn_tokens, theirs = together(attn_tokens, theirs)
        weight_sets += [(block, 0) for block in ring.from_siblings(theirs)]
    else:
        weight_sets += [(x_blocks, half_place + 1)] * ring.cores
    upstream_slots = dispatch_blocks(dispatch, upstream_blocks, rows, local_experts)
    residual, second_low = output_branch(
        at, table, attn_tokens, weight_sets, x_blocks, gain_rows[3:4], rows, ring.groups
    )
    feat_steps = ring.gather_steps(second_low)
    grad_raw = einsum(
        "end,efd->enf", upstream_slots.reshape(local_experts, group * capacity, D), reduce_weight
    ).reshape(local_experts, group, capacity, F)

    carried = None
    waiting = [
        (block, ident, 0, k)
        for k, (block, ident) in enumerate(ring.with_siblings(next(feat_steps)))
    ]
    calls = {1: 0, ring.size // 2 - 1: 1}
    feat_sums, taken_by = {}, {}
    pieces = None
    for step in range(ring.size // 2):
        arrival = feat_steps.send(pieces)
        pieces = [piece for piece, _ in arrival]
        if step == 0:
            pieces, upstream_slots = together(pieces, upstream_slots)
        elif step == 1:
            pieces, grad_raw = together(pieces, grad_raw)
        elif step == 2:
            pieces, *carried = together(pieces, *carried)
        direct, later = [], []
        for piece, (_, distance) in zip(pieces, arrival):
            for k, (block, ident) in enumerate(ring.with_siblings([(piece, distance)])):
                (later if k else direct).append((block, ident, distance, k))
        waiting += direct
        if step not in calls:
            waiting += later
            continue
        taken, waiting = (waiting, later) if step == 1 else (waiting + later, [])
        carried, sums = run_experts(
            [block for block, *_ in taken],
            [ident for _, ident, *_ in taken],
            first_expert,
            grad_raw,
            dispatch,
            combine,
            router_flip,
            expand_weight,
            carried,
            calls[step],
        )
        for (_, ident, distance, k), total in zip(taken, sums):
            feat_sums[distance, k] = total
        taken_by[calls[step] * len(taken)] = [item[1:] for item in taken]
    by_slot = [item for start in sorted(taken_by) for item in taken_by[start]]
    places = [ident for ident, _, _ in by_slot]
    chips = [(distance, k) for _, distance, k in by_slot]
    feat_parts = {}

    def feat_part(distance):
        if distance not in feat_parts:
            others = ring.for_siblings(*[feat_sums[distance, k] for k in range(1, ring.cores)])
            feat_parts[distance] = [(block, 0) for block in (feat_sums[distance, 0], *others)]
        return feat_parts[distance]

    slot_rows, hidden, grad_gate_pre, grad_up_pre, slot_gate = carried

    arriving, arrived = [], []

    def taking(count, *values):
        taken, arriving[:count] = arriving[:count], []
        *values, taken = together(*values, taken)
        arrived.extend(taken)
        return values

    def ahead_tie(scatter, parts, *values):
        steps = [scatter.step, -scatter.step] if scatter.step else []
        terms = {step: scatter.parts(step) for step in steps}
        blocks = [[block for block, _ in terms[step] if block.ndim == 2] for step in steps]
        *values, blocks = scatter.tie(*values, blocks)
        for step, given in zip(steps, blocks):
            given = iter(given)
            parts[step] = [
                (next(given), 0) if block.ndim == 2 else (block, place) for block, place in terms[step]
            ]
        return values

    grads = ring.scatter(feat_part)
    grads.ready()
    expand_sides = [grad_gate_pre, grad_up_pre]
    expand_rows, reduce_rows = D // dp_count, F // dp_count
    half = local_experts // 2
    slot_rows, = grads.tie(slot_rows)
    grads.move()
    sent, pieces = weight_grad_sends(slot_rows, expand_sides, expand_rows, 0, half)
    arriving += pieces
    sent, = ahead_tie(grads, feat_parts, sent)
    grads.ready()
    slot_rows, hidden = grads.tie(slot_rows, hidden)
    grads.move()
    expert_out = einsum("enf,efd->end", hidden, reduce_weight).astype(bf16)
    expert_out, = taking(1, *ahead_tie(grads, feat_parts, expert_out))
    grads.ready()
    expert_out, = grads.tie(expert_out)
    grads.move()
    ids = jnp.stack(places).astype(jnp.int32)
    gate_tokens, grad_out_slots, moe_sums, moe_order = combine_experts(
        ids, chips, expert_out, upstream_slots, dispatch, combine, slot_gate, ring.cores
    )
    grad_out_slots = grad_out_slots.reshape(local_experts, group * capacity, D)
    grad_out_slots, moe_sums, gate_tokens = taking(
        1, *ahead_tie(grads, feat_parts, grad_out_slots, moe_sums, gate_tokens)
    )
    grads.ready()
    moe_sums, gate_tokens, slot_rows = grads.tie(moe_sums, gate_tokens, slot_rows)
    grads.move()
    grad_probs = exchange(gate_tokens, BLOCKS)
    sent, pieces = weight_grad_sends(
        slot_rows, expand_sides, expand_rows, half, local_experts - half
    )
    arriving += pieces
    expand_count = len(arrived) + len(arriving)
    moe_others = [lax.ppermute(other, PLANE, ring.sibling) for other in moe_sums[1:]]

    def moe_part(distance):
        place = moe_order.index(distance)
        return [(array, place) for array in (moe_sums[0], *moe_others)]

    grad_probs = grad_probs.reshape(cols, rows, local_experts, tok_rows)
    grad_probs = grad_probs.transpose(1, 0, 2, 3).reshape(expert_count, tok_rows)
    logits = dot_nt(router_flip, second_low)
    probs = jax.nn.softmax(logits, axis=0)
    grad_logits = probs * (grad_probs - jnp.sum(probs * grad_probs, axis=0, keepdims=True))
    grad_logits = grad_logits.T.astype(bf16)
    router_term = einsum("te,td->ed", grad_logits, second_low)
    grad_logits, router_term, moe_others, sent = taking(
        1, *grads.tie(grad_logits, router_term, moe_others, sent)
    )
    moes = ring.scatter(moe_part)
    moes.ready()
    grad_terms = grads.total()

    grad_branch, gain_second_term = residual_back(
        at[:2], grad_terms, grad_logits, router_flip, residual, upstream_blocks, gain_rows[3:4], rows
    )
    branch_steps = ring.gather_steps(grad_branch)
    branch_all = unwritten((group, tok_rows, D), bf16)
    branch_all = ring.place_blocks(branch_all, ring.with_siblings(next(branch_steps)))
    rank = lax.axis_index("dp")
    expand_grad = None
    extra = []
    pieces = None
    for step in range(ring.size // 2):
        arrival = branch_steps.send(pieces)
        if step == ring.size // 2 - 1:
            moes.move()
        pieces, branch_all, extra, moes.going = taking(
            1,
            [piece for piece, _ in arrival],
            branch_all,
            extra,
            moes.going,
        )
        if step == 0:
            left, = together(hidden, pieces)[:1]
            extra, parts = weight_grad_sends(
                left, [grad_out_slots], reduce_rows, 0, local_experts
            )
            arriving += parts
        elif step == 2:
            expand_grad, = extra
        elif step == 1:
            left, = together(slot_rows, pieces)[:1]
            expand_grad = weight_grad(
                left, expand_sides, rank, expand_rows, 0, half, arrived[: expand_count // 2]
            )
            extra = [expand_grad]
        else:
            expand_grad, = extra
        arrival = list(zip(pieces, [distance for _, distance in arrival]))
        branch_all = ring.place_blocks(branch_all, ring.with_siblings(arrival))

    moes.ready()
    branch_all, = moes.tie(branch_all)
    moes.move()
    grad_attn = dot(branch_all.reshape(seq_len, D), head_out).astype(bf16)
    centre = jnp.sum(attn_head.astype(f32) * grad_attn.astype(f32), axis=1)[None]
    grad_query, dot_query, grad_key, grad_value, dot_key, dot_value = attention_back(
        query_low, key_low, key_flip, value_low, grad_attn, lse, centre, prefix_len, query_rows
    )
    head_grads = [grad_query, grad_key, grad_value]
    dots = jnp.concatenate([dot_query, dot_key, dot_value], axis=0)
    dots, = taking(1, *moes.tie(dots))
    moes.ready()
    dots, = moes.tie(dots)
    dots = ring.small_sum(dots)
    dots, = moes.tie(dots)
    moes.move()

    grad_qkv, gain_pair_terms, grad_first_blocks = unproject(
        head_grads, projected, squares, dots, gain_pair, cosine, sine_part, weight_flip, rows, cols
    )

    def first_part(distance):
        if distance not in first_parts:
            mine, *others = ring.block_ids(distance)
            others = ring.for_siblings(
                *[lax.dynamic_index_in_dim(grad_first_blocks, k, 0, False) for k in others]
            )
            first_parts[distance] = [(grad_first_blocks, mine)] + [(block, 0) for block in others]
        return first_parts[distance]

    first_parts = {}
    grad_first_blocks, grad_qkv = taking(2, *moes.tie(grad_first_blocks, grad_qkv))
    first_far = block_sum(first_part(ring.size // 2))
    moes.ready()
    first_far, grad_first_blocks = moes.tie(first_far, grad_first_blocks)
    first_parts = {ring.size // 2: [(first_far, 0)]}
    firsts = ring.scatter(first_part)
    firsts.ready()
    firsts.move()
    moes.move()
    output_term = dot(attn_head.T, branch_all.reshape(seq_len, D))
    output_term = output_term.astype(bf16).reshape(HD, rows, row_width).transpose(1, 0, 2)
    output_term, = taking(1, *ahead_tie(firsts, first_parts, output_term))
    firsts.ready()
    grad_qkv, slot_rows = firsts.tie(grad_qkv, slot_rows)
    firsts.move()
    qkv_term, gain_first_term = project_weight(
        x_blocks, res_rows, gain_rows[0:1], inv_first, grad_qkv, head_weight, rows
    )
    qkv_rows = row_width // dp_count
    qkv_sum = dp_sum(
        lambda rank: lax.dynamic_slice_in_dim(qkv_term, rank * qkv_rows, qkv_rows, 2)
    )
    output_sum = exchange(output_term, "row").reshape(col_width, row_width)
    qkv_term, = taking(1, *moes.tie(*ahead_tie(firsts, first_parts, qkv_term)))
    moe_terms = moes.total()
    firsts.ready()
    slot_rows, = firsts.tie(slot_rows)
    firsts.move()
    expand_grad = weight_grad(
        slot_rows, expand_sides, rank, expand_rows, half, local_experts - half,
        arrived[expand_count // 2 : expand_count], into=expand_grad,
    )
    layer_tokens = residual
    for term in moe_terms:
        layer_tokens = layer_tokens + term.astype(f32)
    layer_tokens = layer_tokens.astype(bf16)
    layer_output = lax.all_to_all(layer_tokens, "row", split_axis=1, concat_axis=0, tiled=True)
    expand_grad, output_sum = taking(
        len(arriving), *ahead_tie(firsts, first_parts, expand_grad, output_sum)
    )
    firsts.ready()
    hidden, qkv_sum = firsts.tie(hidden, qkv_sum)
    firsts.move()
    reduce_grad = weight_grad(
        hidden, [grad_out_slots], rank, reduce_rows, more=arrived[expand_count:]
    )
    reduce_grad, layer_output = firsts.tie(reduce_grad, layer_output)
    grad_first = firsts.total()
    grad_first = sum(term.astype(f32) for term in grad_first)
    grad_block = lax.dynamic_slice(
        branch_all, (col_rank * rows, 0, row_rank * row_width), (rows, tok_rows, row_width)
    ).reshape(res_rows, row_width)
    inverse = lax.rsqrt(squares / D + norm_epsilon)
    dot_first = dots[2] + norm_epsilon * jnp.sum(dots[:2] * inverse, axis=0)
    dot_first = dot_first / inv_first[0]
    own_first = col_rank * res_rows
    dot_first = lax.dynamic_slice_in_dim(dot_first, own_first, res_rows)
    inv_block = lax.dynamic_slice_in_dim(inv_first[0], own_first, res_rows)
    gain_block = lax.dynamic_slice_in_dim(gain_rows[0], row_rank * row_width, row_width)
    input_grad = grad_block.astype(f32) + norm_back(
        layer_input.astype(f32), inv_block, gain_block, grad_first, dot_first
    )

    output_rows = col_width // dp_count
    output_grad = dp_sum(
        lambda rank: lax.dynamic_slice_in_dim(
            output_sum, rank * output_rows, output_rows, 0
        ).astype(f32)
    )
    qkv_grad = exchange(qkv_sum.astype(bf16), "row").transpose(2, 1, 0, 3)
    qkv_grad = qkv_grad.reshape(1, qkv_rows, 3, col_width).astype(f32)

    def placed(term):
        return lax.dynamic_update_slice(jnp.zeros((D,), f32), term, (head_first,))

    gain_terms = jnp.concatenate(
        [
            gain_first_term,
            jnp.stack([placed(gain_pair_terms[0]), placed(gain_pair_terms[1])]),
            gain_second_term,
        ],
        axis=0,
    )
    gain_total = jnp.sum(lax.all_gather(gain_terms, ("dp", "row", "col"), axis=0), axis=0)
    router_all = lax.all_gather(router_term.astype(bf16), ("dp", "row", "col"), axis=0)
    router_total = jnp.sum(router_all.astype(f32), axis=0).T
    return (
        layer_output,
        input_grad.astype(bf16),
        gain_total,
        qkv_grad,
        output_grad[None],
        router_total,
        expand_grad,
        reduce_grad,
    )


def solution(mesh):
    return jax.shard_map(
        on_device,
        mesh=mesh,
        in_specs=(
            P(("dp", "col"), "row"),
            P(),
            P("row", None, "col"),
            P("col", "row"),
            P(),
            P(("row", "col"), None, None),
            P(("row", "col"), None, None),
            P(("dp", "col"), None),
            P(("dp", "col")),
            P("dp"),
            P(("dp", "col"), "row"),
        ),
        out_specs=(
            P(("dp", "col"), "row"),
            P(("dp", "col"), "row"),
            P(),
            P("row", "dp", None, "col"),
            P("col", "dp", "row"),
            P(),
            P(("row", "col"), "dp", None),
            P(("row", "col"), "dp", None),
        ),
        check_vma=False,
    )
```

```python
import functools
import math

import jax
import jax.numpy as jnp
from jax import lax
from jax.experimental import pallas as pl
from jax.experimental.pallas import tpu as pltpu
from jax.sharding import PartitionSpec as P

D = 2048
HD = 128
F = 1024
TOP = 8
CORES = 2
PLANE = ("row", "col")
BLOCKS = ("col", "row")
LOG2E = math.log2(math.e)
MASKED = -1e30
COST_SHARE = 0.1

norm_epsilon = 1e-05
rope_base = 10000.0
bf16 = jnp.bfloat16
f32 = jnp.float32


def dot_nt(a, b):
    return lax.dot_general(a, b, (((1,), (1,)), ((), ())), preferred_element_type=f32)


def dot_nn(a, b):
    return lax.dot_general(a, b, (((1,), (0,)), ((), ())), preferred_element_type=f32)


def cost(microseconds):
    return pl.CostEstimate(
        flops=int(microseconds * 1.1e9 * COST_SHARE), bytes_accessed=0, transcendentals=0
    )


def as_row(column):
    return jnp.broadcast_to(column, (column.shape[0], 128)).T[:1]


def as_column(row):
    return jnp.broadcast_to(row, (8, row.shape[1])).T[:, :1]


def key_limits(first_query, query_rows, key_rows, prefix):
    open_blocks = jnp.maximum((first_query + 1) // key_rows, prefix // key_rows)
    all_blocks = pl.cdiv(jnp.maximum(first_query + query_rows, prefix), key_rows)
    return open_blocks, all_blocks


def mask_scores(scores, first_key, first_query, prefix):
    keys = first_key + lax.broadcasted_iota(jnp.int32, scores.shape, 0)
    queries = first_query + lax.broadcasted_iota(jnp.int32, scores.shape, 1)
    return jnp.where((keys <= queries) | (keys < prefix), scores, MASKED)


def attention_kernel(scale, prefix_ref, q_ref, k_ref, v_flip_ref, out_ref, lse_ref, scores_ref):
    query_rows = q_ref.shape[0]
    key_rows = min(512, k_ref.shape[0])
    first_query = pl.program_id(0) * query_rows
    prefix = prefix_ref[0]
    q = q_ref[...]
    open_blocks, all_blocks = key_limits(first_query, query_rows, key_rows, prefix)

    def score(j, top, masked):
        start = pl.multiple_of(j * key_rows, key_rows)
        scores = dot_nt(k_ref[pl.ds(start, key_rows), :], q) * (scale * LOG2E)
        if masked:
            scores = mask_scores(scores, start, first_query, prefix)
        scores_ref[pl.ds(start, key_rows), :] = scores
        return jnp.maximum(top, jnp.max(scores.reshape(key_rows // 8, 8, query_rows), axis=0))

    top = jnp.full((8, query_rows), MASKED, f32)
    top = lax.fori_loop(0, open_blocks, lambda j, t: score(j, t, False), top)
    top = lax.fori_loop(open_blocks, all_blocks, lambda j, t: score(j, t, True), top)
    peak = jnp.max(top, axis=0, keepdims=True)

    def mix(j, carry):
        total, mixed = carry
        start = pl.multiple_of(j * key_rows, key_rows)
        weights = jnp.exp2(scores_ref[pl.ds(start, key_rows), :] - peak)
        total = total + jnp.sum(weights.reshape(key_rows // 8, 8, query_rows), axis=0)
        mixed = mixed + dot_nn(v_flip_ref[:, pl.ds(start, key_rows)], weights.astype(bf16))
        return total, mixed

    total, mixed = lax.fori_loop(
        0,
        all_blocks,
        mix,
        (jnp.zeros((8, query_rows), f32), jnp.zeros((q.shape[1], query_rows), f32)),
    )
    total = jnp.sum(total, axis=0, keepdims=True)
    out_ref[...] = (mixed / total).T.astype(out_ref.dtype)
    lse_ref[...] = peak + jnp.log2(total)


def attention(q, k, v_flip, prefix_len, query_rows):
    length, width = q.shape
    query_block = pl.BlockSpec((query_rows, width), lambda i, p: (i, 0))
    return pl.pallas_call(
        functools.partial(attention_kernel, width**-0.5),
        grid_spec=pltpu.PrefetchScalarGridSpec(
            num_scalar_prefetch=1,
            grid=(length // query_rows,),
            in_specs=[
                query_block,
                pl.BlockSpec((length, width), lambda i, p: (0, 0)),
                pl.BlockSpec((width, length), lambda i, p: (0, 0)),
            ],
            out_specs=[query_block, pl.BlockSpec((1, query_rows), lambda i, p: (0, i))],
            scratch_shapes=[pltpu.VMEM((length, query_rows), f32)],
        ),
        out_shape=[
            jax.ShapeDtypeStruct((length, width), bf16),
            jax.ShapeDtypeStruct((1, length), f32),
        ],
        compiler_params=pltpu.CompilerParams(vmem_limit_bytes=40 * 2**20),
        cost_estimate=cost(17),
        name="attention_forward",
    )(prefix_len, q, k, v_flip)


def attention_back_kernel(
    scale, prefix_ref, q_ref, grad_ref, lse_ref, centre_ref, k_ref, k_flip_ref, v_ref,
    grad_q_ref, dot_q_ref, grad_k_ref, grad_v_ref, dot_k_ref, dot_v_ref,
):
    query_rows = q_ref.shape[0]
    key_rows = min(512, k_ref.shape[0])
    step = pl.program_id(0)
    first_query = step * query_rows
    prefix = prefix_ref[0]

    @pl.when(step == 0)
    def _():
        grad_k_ref[...] = jnp.zeros_like(grad_k_ref)
        grad_v_ref[...] = jnp.zeros_like(grad_v_ref)

    q = q_ref[...]
    grad = grad_ref[...]
    lse = lse_ref[...]
    centre = centre_ref[...]
    open_blocks, all_blocks = key_limits(first_query, query_rows, key_rows, prefix)

    def block(j, total, masked):
        start = pl.multiple_of(j * key_rows, key_rows)
        rows = pl.ds(start, key_rows)
        scores = dot_nt(k_ref[rows, :], q) * (scale * LOG2E) - lse
        if masked:
            scores = mask_scores(scores, start, first_query, prefix)
        weights = jnp.exp2(scores)
        grad_weights = dot_nt(v_ref[rows, :], grad)
        grad_scores = (weights * (grad_weights - centre)).astype(bf16)
        grad_v_ref[rows, :] += dot_nn(weights.astype(bf16), grad)
        grad_k_ref[rows, :] += dot_nn(grad_scores, q)
        return total + dot_nn(k_flip_ref[:, rows], grad_scores)

    total = jnp.zeros((q.shape[1], query_rows), f32)
    total = lax.fori_loop(0, open_blocks, lambda j, a: block(j, a, False), total)
    total = lax.fori_loop(open_blocks, all_blocks, lambda j, a: block(j, a, True), total)
    grad_q = total.T * scale
    grad_q_ref[...] = grad_q
    dot_q_ref[...] = as_row(jnp.sum(grad_q * q.astype(f32), axis=1, keepdims=True))

    @pl.when(step == pl.num_programs(0) - 1)
    def _():
        for start in range(0, k_ref.shape[0], key_rows):
            rows = pl.ds(start, key_rows)
            grad_k = grad_k_ref[rows, :] * scale
            grad_k_ref[rows, :] = grad_k
            dot_k_ref[:, rows] = as_row(
                jnp.sum(grad_k * k_ref[rows, :].astype(f32), axis=1, keepdims=True)
            )
            dot_v_ref[:, rows] = as_row(
                jnp.sum(grad_v_ref[rows, :] * v_ref[rows, :].astype(f32), axis=1, keepdims=True)
            )


def attention_back(q, k, k_flip, v, grad, lse, centre, prefix_len, query_rows):
    length, width = q.shape
    whole = pl.BlockSpec((length, width), lambda i, p: (0, 0))
    flipped = pl.BlockSpec((width, length), lambda i, p: (0, 0))
    query_block = pl.BlockSpec((query_rows, width), lambda i, p: (i, 0))
    query_row = pl.BlockSpec((1, query_rows), lambda i, p: (0, i))
    key_row = pl.BlockSpec((1, length), lambda i, p: (0, 0))
    result = jax.ShapeDtypeStruct((length, width), f32)
    line = jax.ShapeDtypeStruct((1, length), f32)
    return pl.pallas_call(
        functools.partial(attention_back_kernel, width**-0.5),
        grid_spec=pltpu.PrefetchScalarGridSpec(
            num_scalar_prefetch=1,
            grid=(length // query_rows,),
            in_specs=[query_block, query_block, query_row, query_row, whole, flipped, whole],
            out_specs=[query_block, query_row, whole, whole] + [key_row] * 2,
        ),
        out_shape=[result, line, result, result] + [line] * 2,
        compiler_params=pltpu.CompilerParams(vmem_limit_bytes=40 * 2**20),
        cost_estimate=cost(24),
        name="attention_backward",
    )(prefix_len, q, grad, lse, centre, k, k_flip, v)


def unwritten(shape, dtype):
    return pl.pallas_call(
        lambda out_ref: None,
        out_specs=pl.BlockSpec(memory_space=pl.ANY),
        out_shape=jax.ShapeDtypeStruct(shape, dtype),
        name="buffer",
    )()


def add_low(one, two):
    return (one.astype(f32) + two.astype(f32)).astype(bf16)


def step_sum_kernel(counts, halved, ids_ref, *refs):
    half = pl.program_id(0)
    parts, (forth_ref, back_ref, ahead_ref, behind_ref) = refs[:-4], refs[-4:]
    for start, came_ref, out_ref, at in (
        (0, forth_ref, ahead_ref, 0),
        (counts[0], back_ref, behind_ref, 1),
    ):
        count = counts[at]
        total = sum(ref[0].astype(f32) for ref in parts[start : start + count])
        if not halved:
            out_ref[...] = (total + came_ref[...].astype(f32)).astype(bf16)
            continue

        @pl.when(half == at)
        def _():
            out_ref[...] = (total + came_ref[...].astype(f32)).astype(bf16)

        @pl.when(half != at)
        def _():
            out_ref[...] = total.astype(bf16)


def step_sum(ahead, behind, forth, back):
    parts = [(array if array.ndim == 3 else array[None], place) for array, place in ahead + behind]
    ids = jnp.stack([jnp.asarray(place, jnp.int32) for _, place in parts])
    _, rows, width = parts[0][0].shape
    tile = rows // 2
    halved = forth.shape[0] != rows
    came = pl.BlockSpec((tile, width), (lambda i, ids: (0, 0)) if halved else (lambda i, ids: (i, 0)))
    whole = pl.BlockSpec((tile, width), lambda i, ids: (i, 0))
    return pl.pallas_call(
        functools.partial(step_sum_kernel, (len(ahead), len(behind)), halved),
        grid_spec=pltpu.PrefetchScalarGridSpec(
            num_scalar_prefetch=1,
            grid=(2,),
            in_specs=[
                pl.BlockSpec((1, tile, width), lambda i, ids, k=k: (ids[k], i, 0))
                for k in range(len(parts))
            ]
            + [came, came],
            out_specs=[whole, whole],
        ),
        out_shape=[jax.ShapeDtypeStruct((rows, width), bf16)] * 2,
        cost_estimate=cost(3),
        name="step_sum",
    )(ids, *[array for array, _ in parts], forth, back)


def block_sum(parts):
    total = 0.0
    for array, place in parts:
        block = array if array.ndim == 2 else lax.dynamic_index_in_dim(array, place, 0, False)
        total = total + block.astype(f32)
    return total.astype(bf16)


def after(value, earlier):
    return lax.optimization_barrier((value, earlier))[0]


def together(*values):
    return lax.optimization_barrier(values)


class Ring:
    def __init__(self, rows, cols):
        self.rows, self.cols = rows, cols
        self.cores = CORES if cols % CORES == 0 else 1
        self.groups = cols // self.cores
        self.order = [
            (row, group)
            for group in range(self.groups)
            for row in (range(rows) if group % 2 == 0 else range(rows - 1, -1, -1))
        ]
        self.size = len(self.order)
        self.clockwise = self.shift(1)
        self.counter = self.shift(-1)
        self.sibling = [
            (row * cols + col, row * cols + col - col % self.cores + (col + 1) % self.cores)
            for row in range(rows)
            for col in range(cols)
        ]
        row, col = lax.axis_index("row"), lax.axis_index("col")
        group = col // self.cores
        self.core = col % self.cores
        self.place = group * rows + jnp.where(group % 2 == 0, row, rows - 1 - row)

    def shift(self, step):
        pairs = []
        for at, (row, group) in enumerate(self.order):
            to_row, to_group = self.order[(at + step) % self.size]
            for core in range(self.cores):
                pairs.append(
                    (
                        row * self.cols + group * self.cores + core,
                        to_row * self.cols + to_group * self.cores + core,
                    )
                )
        return pairs

    def chip(self, distance):
        at = (self.place + distance + self.size) % self.size
        group = at // self.rows
        along = at % self.rows
        return jnp.where(group % 2 == 0, along, self.rows - 1 - along), group

    def owners(self, distance):
        row, group = self.chip(distance)
        return [(row, group * self.cores + (self.core + k) % self.cores) for k in range(self.cores)]

    def block_ids(self, distance):
        return [col * self.rows + row for row, col in self.owners(distance)]

    def from_siblings(self, block):
        return [block] + [lax.ppermute(block, PLANE, self.sibling)] * (self.cores - 1)

    def gather_steps(self, block):
        forth = back = block
        yield [(block, 0)]
        for step in range(1, (self.size + 1) // 2):
            forth = lax.ppermute(forth, PLANE, self.clockwise)
            back = lax.ppermute(back, PLANE, self.counter)
            sent = yield [(forth, -step), (back, step)]
            if sent is not None:
                forth, back = sent
        if self.size % 2 == 0:
            half = block.shape[0] // 2
            forth = lax.ppermute(forth[:half], PLANE, self.clockwise)
            back = lax.ppermute(back[half:], PLANE, self.counter)
            yield [(jnp.concatenate([forth, back], axis=0), self.size // 2)]

    def with_siblings(self, arrival):
        return [
            pair
            for piece, distance in arrival
            for pair in zip(self.from_siblings(piece), self.block_ids(distance))
        ]

    def place_blocks(self, box, pairs):
        blocks, ids = zip(*pairs)
        count = len(blocks)

        def kernel(ids_ref, *refs):
            step = pl.program_id(0)
            for k in range(count):

                @pl.when(step == k)
                def _():
                    refs[-1][0] = refs[k][...]

        whole = pl.BlockSpec(blocks[0].shape, lambda i, ids: (0,) * blocks[0].ndim)
        return pl.pallas_call(
            kernel,
            grid_spec=pltpu.PrefetchScalarGridSpec(
                num_scalar_prefetch=1,
                grid=(count,),
                in_specs=[whole] * count + [pl.BlockSpec(memory_space=pl.ANY)],
                out_specs=pl.BlockSpec(
                    (1,) + blocks[0].shape, lambda i, ids: (ids[i],) + (0,) * blocks[0].ndim
                ),
            ),
            out_shape=jax.ShapeDtypeStruct(box.shape, box.dtype),
            input_output_aliases={count + 1: 0},
            cost_estimate=cost(count),
            name="place_blocks",
        )(jnp.stack(ids).astype(jnp.int32), *blocks, box)

    def gather_array(self, block):
        box = unwritten((self.rows * self.cols,) + block.shape, block.dtype)
        for arrival in self.gather_steps(block):
            box = self.place_blocks(box, self.with_siblings(arrival))
        return box

    def for_siblings(self, *others):
        return [lax.ppermute(other, PLANE, self.sibling) for other in others]

    def scatter(self, parts):
        return Scatter(self, parts)

    def sum_steps(self, values, kind=f32):
        rows, cols = self.rows, self.cols
        if rows & (rows - 1) or cols & (cols - 1):
            yield lax.psum(values, PLANE)
            return
        swaps = []
        bit = 1
        while bit < cols:
            swaps.append(lambda row, col, bit=bit: (row, col ^ bit))
            bit *= 2
        bit = 1
        while bit < rows:
            swaps.append(lambda row, col, bit=bit: (row ^ bit, col))
            bit *= 2
        for swap in swaps:
            pairs = []
            for row in range(rows):
                for col in range(cols):
                    to_row, to_col = swap(row, col)
                    pairs.append((row * cols + col, to_row * cols + to_col))
            sent = values.astype(kind)
            values = sent.astype(f32) + lax.ppermute(sent, PLANE, pairs).astype(f32)
            yield values

    def small_sum(self, values):
        *_, last = self.sum_steps(values)
        return last


class Scatter:
    def __init__(self, ring, parts):
        self.ring, self.parts = ring, parts
        self.step = ring.size // 2
        self.going = None

    def ready(self):
        ring, step = self.ring, self.step
        if 2 * step == ring.size:
            far = block_sum(self.parts(step))
            half = far.shape[0] // 2
            self.going = far[:half], far[half:]
        elif self.going is None:
            self.going = block_sum(self.parts(step)), block_sum(self.parts(-step))
        else:
            self.going = tuple(step_sum(self.parts(step), self.parts(-step), *self.going))

    def move(self):
        forth, back = self.going
        self.going = (
            lax.ppermute(forth, PLANE, self.ring.clockwise),
            lax.ppermute(back, PLANE, self.ring.counter),
        )
        self.step -= 1

    def tie(self, *values):
        self.going, *values = together(self.going, *values)
        return values

    def total(self):
        own = [
            array if array.ndim == 2 else lax.dynamic_index_in_dim(array, place, 0, False)
            for array, place in self.parts(0)
        ]
        return *own, *self.going


def dp_sum(part):
    count = lax.axis_size("dp")
    rank = lax.axis_index("dp")
    if count == 1:
        return part(rank)
    onward = [(d, (d + 1) % count) for d in range(count)]
    total = part((rank + count - 1) % count)
    for step in range(1, count):
        arrived = lax.ppermute(total.astype(bf16), "dp", onward)
        total = part((rank + 2 * count - 1 - step) % count) + arrived.astype(f32)
    return total


def dp_all_sum(values, kind=f32):
    count = lax.axis_size("dp")
    if count & (count - 1):
        return lax.psum(values, "dp")
    bit = 1
    while bit < count:
        sent = values.astype(kind)
        swapped = lax.ppermute(sent, "dp", [(d, d ^ bit) for d in range(count)])
        values = sent.astype(f32) + swapped.astype(f32)
        bit *= 2
    return values


def exchange_rows(pieces):
    rows = pieces.shape[0]
    row = lax.axis_index("row")
    start = lambda at: (at,) + (0,) * (pieces.ndim - 1)
    taken = unwritten(pieces.shape, pieces.dtype)
    own = lax.dynamic_index_in_dim(pieces, row, 0, True)
    taken = lax.dynamic_update_slice(taken, own, start(row))
    for step in range(1, rows):
        sent = lax.dynamic_index_in_dim(pieces, (row + step) % rows, 0, True)
        sent = lax.ppermute(sent, "row", [(r, (r + step) % rows) for r in range(rows)])
        taken = lax.dynamic_update_slice(taken, sent, start((row + rows - step) % rows))
    return taken


def exchange(pieces, axes):
    return lax.all_to_all(pieces, axes, split_axis=0, concat_axis=0, tiled=True)


def project_kernel(x_ref, gain_ref, weight_ref, out_ref, inverse_ref, squares_ref, low_ref):
    blocks, _, width = x_ref.shape
    total = 0.0
    for block in range(blocks):
        part = x_ref[block].astype(f32)
        total = total + jnp.sum(part * part, axis=1, keepdims=True)
    inverse = lax.rsqrt(total / D + norm_epsilon)
    for block in range(blocks):
        at = pl.ds(block * width, width)
        low_ref[:, at] = (x_ref[block].astype(f32) * inverse * gain_ref[:, at]).astype(bf16)
    out = dot_nn(low_ref[...], weight_ref[...])
    out_ref[...] = out
    inverse_ref[...] = as_row(inverse)
    for j in range(2):
        part = out[:, j * HD : (j + 1) * HD]
        squares_ref[pl.ds(j, 1), :] = as_row(jnp.sum(part * part, axis=1, keepdims=True))


def project(x_blocks, block_rows, gain_row, weight, rows):
    count, _, width = x_blocks.shape
    cols = count // rows
    tile = block_rows
    per = block_rows // tile
    length = cols * block_rows
    return pl.pallas_call(
        project_kernel,
        grid=(cols * per,),
        in_specs=[
            pl.BlockSpec((rows, tile, width), lambda i: (i // per, i % per, 0)),
            pl.BlockSpec((1, D), lambda i: (0, 0)),
            pl.BlockSpec(weight.shape, lambda i: (0, 0)),
        ],
        out_specs=[
            pl.BlockSpec((tile, 3 * HD), lambda i: (i, 0)),
            pl.BlockSpec((1, tile), lambda i: (0, i)),
            pl.BlockSpec((2, tile), lambda i: (0, i)),
        ],
        scratch_shapes=[pltpu.VMEM((tile, D), bf16)],
        out_shape=[
            jax.ShapeDtypeStruct((length, 3 * HD), f32),
            jax.ShapeDtypeStruct((1, length), f32),
            jax.ShapeDtypeStruct((2, length), f32),
        ],
        compiler_params=pltpu.CompilerParams(vmem_limit_bytes=52 * 2**20),
        cost_estimate=cost(14),
        name="norm_and_project",
    )(x_blocks, gain_row, weight)


def project_weight_kernel(x_ref, gain_ref, inverse_ref, grad_ref, weight_ref, out_ref, term_ref, low_ref):
    blocks, _, width = x_ref.shape
    inverse = as_column(inverse_ref[...])

    @pl.when(pl.program_id(0) == 0)
    def _():
        out_ref[...] = jnp.zeros_like(out_ref)

    for block in range(blocks):
        at = pl.ds(block * width, width)
        low_ref[:, at] = (x_ref[block].astype(f32) * inverse * gain_ref[:, at]).astype(bf16)
    for block in range(blocks):
        at = pl.ds(block * width, width)
        total = dot_nn(low_ref[:, at].T, grad_ref[...])
        for j in range(3):
            out_ref[block, j] += total[:, j * HD : (j + 1) * HD]

    @pl.when(pl.program_id(0) == pl.num_programs(0) - 1)
    def _():
        for block in range(blocks):
            at = pl.ds(block * width, width)
            total = 0.0
            for j in range(3):
                total = total + out_ref[block, j] * weight_ref[at, j * HD : (j + 1) * HD].astype(f32)
            total = as_row(jnp.sum(total, axis=1, keepdims=True))
            term_ref[:, at] = total / gain_ref[:, at]


def project_weight(x_blocks, block_rows, gain_row, inverse, grads, weight, rows):
    count, _, width = x_blocks.shape
    cols = count // rows
    tile = block_rows // 3 if block_rows % 384 == 0 else block_rows
    per = block_rows // tile
    return pl.pallas_call(
        project_weight_kernel,
        grid=(cols * per,),
        in_specs=[
            pl.BlockSpec((rows, tile, width), lambda i: (i // per, i % per, 0)),
            pl.BlockSpec((1, D), lambda i: (0, 0)),
            pl.BlockSpec((1, tile), lambda i: (0, i)),
            pl.BlockSpec((tile, 3 * HD), lambda i: (i, 0)),
            pl.BlockSpec(weight.shape, lambda i: (0, 0)),
        ],
        out_specs=[
            pl.BlockSpec((rows, 3, width, HD), lambda i: (0, 0, 0, 0)),
            pl.BlockSpec((1, D), lambda i: (0, 0)),
        ],
        scratch_shapes=[pltpu.VMEM((tile, D), bf16)],
        out_shape=[
            jax.ShapeDtypeStruct((rows, 3, width, HD), f32),
            jax.ShapeDtypeStruct((1, D), f32),
        ],
        compiler_params=pltpu.CompilerParams(vmem_limit_bytes=40 * 2**20),
        cost_estimate=cost(15),
        name="projection_weight_gradient",
    )(x_blocks, gain_row, inverse, grads, weight)


def turn_kernel(raw_ref, squares_ref, gain_ref, cosine_ref, sine_ref, q_ref, k_ref, v_ref, k_flip_ref, v_flip_ref):
    inverse = lax.rsqrt(squares_ref[...] / D + norm_epsilon)
    for j, out_ref in ((0, q_ref), (1, k_ref)):
        normed = raw_ref[:, j * HD : (j + 1) * HD] * as_column(inverse[j : j + 1]) * gain_ref[j : j + 1, :]
        turned = normed * cosine_ref[...] + jnp.roll(normed, HD // 2, axis=1) * sine_ref[...]
        out_ref[...] = turned.astype(bf16)
        if j == 1:
            k_flip_ref[...] = turned.T.astype(bf16)
    v = raw_ref[:, 2 * HD :]
    v_ref[...] = v.astype(bf16)
    v_flip_ref[...] = v.T.astype(bf16)


def turn(raw, squares, gain_pair, cosine, sine_part):
    length = raw.shape[0]
    tile = min(1024, length)
    tall = pl.BlockSpec((tile, HD), lambda i: (i, 0))
    wide = pl.BlockSpec((HD, tile), lambda i: (0, i))
    tall_shape = jax.ShapeDtypeStruct((length, HD), bf16)
    wide_shape = jax.ShapeDtypeStruct((HD, length), bf16)
    return pl.pallas_call(
        turn_kernel,
        grid=(length // tile,),
        in_specs=[
            pl.BlockSpec((tile, 3 * HD), lambda i: (i, 0)),
            pl.BlockSpec((2, tile), lambda i: (0, i)),
            pl.BlockSpec((2, HD), lambda i: (0, 0)),
            tall,
            tall,
        ],
        out_specs=[tall, tall, tall, wide, wide],
        out_shape=[tall_shape, tall_shape, tall_shape, wide_shape, wide_shape],
        cost_estimate=cost(7.4),
        name="query_key_value",
    )(raw, squares, gain_pair, cosine, sine_part)


def branch_kernel(
    groups, sets, at_ref, heads_ref, x_ref, gain_ref, *refs
):
    weights, (residual_ref, low_ref) = refs[: groups * sets], refs[groups * sets :]
    step = pl.program_id(0)
    rows, width = x_ref.shape[0], x_ref.shape[2]
    height = weights[0].shape[1]
    per = height // HD
    branch = x_ref[pl.ds(step, 1)][0].astype(f32)
    for group in range(groups):
        for k in range(sets):
            first = at_ref[2 + group * sets + k]
            heads = jnp.concatenate([heads_ref[first + j] for j in range(per)], axis=1)
            branch = branch + dot_nn(heads, weights[group * sets + k][0])
    residual_ref[:, pl.ds(pl.multiple_of(step * width, width), width)] = branch

    @pl.when(step == rows - 1)
    def _():
        total = residual_ref[...]
        inverse = lax.rsqrt(jnp.sum(total * total, axis=1, keepdims=True) / D + norm_epsilon)
        low_ref[...] = (total * inverse * gain_ref[...]).astype(bf16)


def output_branch(at, table, heads, weight_sets, x_blocks, gain_row, rows, groups):
    tok_rows = heads.shape[1]
    sets = len(weight_sets)
    width = x_blocks.shape[2]
    height = D // (2 * rows)
    fixed = lambda shape: pl.BlockSpec(shape, lambda i, a, t: (0,) * len(shape))
    return pl.pallas_call(
        lambda at_ref, table_ref, *refs: branch_kernel(groups, sets, at_ref, *refs),
        grid_spec=pltpu.PrefetchScalarGridSpec(
            num_scalar_prefetch=2,
            grid=(rows,),
            in_specs=[
                fixed(heads.shape),
                pl.BlockSpec((rows, tok_rows, width), lambda i, a, t: (a[0], a[1], 0)),
                fixed((1, D)),
            ]
            + [
                pl.BlockSpec(
                    (1, height, width),
                    lambda i, a, t, g=g, k=k, half=half: (t[(k * groups + g) * rows + i], half, 0),
                )
                for g in range(groups)
                for k, (_, half) in enumerate(weight_sets)
            ],
            out_specs=[fixed((tok_rows, D)), fixed((tok_rows, D))],
        ),
        out_shape=[
            jax.ShapeDtypeStruct((tok_rows, D), f32),
            jax.ShapeDtypeStruct((tok_rows, D), bf16),
        ],
        compiler_params=pltpu.CompilerParams(vmem_limit_bytes=40 * 2**20),
        cost_estimate=cost(6),
        name="output_projection",
    )(at, table, heads, x_blocks, gain_row, *[w for _ in range(groups) for w, _ in weight_sets])


def resid_kernel(
    at_ref, logit_ref, router_ref, residual_ref, up_ref, gain_ref, *refs,
):
    terms, (grad_low_ref, gain_term_ref) = refs[:-2], refs[-2:]
    rows, width = up_ref.shape[0], up_ref.shape[2]
    grad = sum(ref[...].astype(f32) for ref in terms)
    grad = grad + dot_nn(logit_ref[...], router_ref[...])
    residual = residual_ref[...]
    inverse = lax.rsqrt(jnp.sum(residual * residual, axis=1, keepdims=True) / D + norm_epsilon)
    scaled = grad * gain_ref[...]
    total = jnp.sum(scaled * residual, axis=1, keepdims=True)
    gain_term_ref[...] = jnp.sum(grad * residual * inverse, axis=0, keepdims=True)
    back = inverse * scaled - residual * (inverse * inverse * inverse * total / D)
    for row in range(rows):
        at = pl.ds(row * width, width)
        grad_low_ref[:, at] = (
            up_ref[row].astype(f32) + back[:, row * width : (row + 1) * width]
        ).astype(bf16)


def residual_back(at, terms, grad_logits, router_flip, residual, up_blocks, gain_row, rows):
    tok_rows = residual.shape[0]
    width = up_blocks.shape[2]
    fixed = lambda shape: pl.BlockSpec(shape, lambda i, a: (0,) * len(shape))
    whole, line = fixed((tok_rows, D)), fixed((1, D))
    return pl.pallas_call(
        resid_kernel,
        grid_spec=pltpu.PrefetchScalarGridSpec(
            num_scalar_prefetch=1,
            grid=(1,),
            in_specs=[
                fixed(grad_logits.shape),
                fixed(router_flip.shape),
                whole,
                pl.BlockSpec((rows, tok_rows, width), lambda i, a: (a[0], a[1], 0)),
                line,
            ]
            + [whole] * len(terms),
            out_specs=[whole, line],
        ),
        out_shape=[
            jax.ShapeDtypeStruct((tok_rows, D), bf16),
            jax.ShapeDtypeStruct((1, D), f32),
        ],
        compiler_params=pltpu.CompilerParams(vmem_limit_bytes=40 * 2**20),
        cost_estimate=cost(3),
        name="residual_backward",
    )(at, grad_logits, router_flip, residual, up_blocks, gain_row, *terms)


def dispatch_kernel(hits_ref, x_ref, out_ref):
    experts, _, capacity, _ = out_ref.shape
    width = x_ref.shape[2]
    for block in range(x_ref.shape[0]):
        picked = dot_nn(hits_ref[0], x_ref[block]).astype(bf16)
        for e in range(experts):
            out_ref[e, 0, :, pl.ds(block * width, width)] = picked[e * capacity : (e + 1) * capacity]


def dispatch_blocks(hits, x_blocks, rows, experts):
    group, slot_rows, tok_rows = hits.shape
    width = x_blocks.shape[2]
    capacity = slot_rows // experts
    return pl.pallas_call(
        dispatch_kernel,
        grid=(group,),
        in_specs=[
            pl.BlockSpec((1, slot_rows, tok_rows), lambda b: (b, 0, 0)),
            pl.BlockSpec((rows, tok_rows, width), lambda b: (b // rows, b % rows, 0)),
        ],
        out_specs=pl.BlockSpec((experts, 1, capacity, D), lambda b: (0, b, 0, 0)),
        out_shape=jax.ShapeDtypeStruct((experts, group, capacity, D), bf16),
        cost_estimate=cost(14),
        name="cotangent_to_slots",
    )(hits, x_blocks)


def experts_kernel(count, first, ids_ref, *refs):
    feats = refs[:count]
    raws = refs[count : 2 * count]
    hits_ref, flip_ref, router_ref, gate_w_ref, up_w_ref = refs[2 * count : 2 * count + 5]
    rest = refs[2 * count + 5 :]
    if not first:
        rest = rest[5:]
    slot_ref, hidden_ref, grad_gate_ref, grad_up_ref, scale_ref = rest[:5]
    feat_sums = rest[5 : 5 + count]
    probs_ref, later_ref, in_acc, in_all = rest[5 + count :]
    rows = slot_ref.shape[1]
    e, f = pl.program_id(0), pl.program_id(1)
    last_expert = e == pl.num_programs(0) - 1
    last_tile = f == pl.num_programs(1) - 1
    capacity = raws[0].shape[2]
    chosen = ids_ref[count] + e
    own_slots = pl.ds(pl.multiple_of(e * capacity, 16), capacity)

    @pl.when((e == 0) & (f == 0))
    def _():
        for k in range(count):
            logits = dot_nt(router_ref[...], feats[k][...])
            raised = jnp.exp(logits - jnp.max(logits, axis=0, keepdims=True))
            probs_ref[k] = raised / jnp.sum(raised, axis=0, keepdims=True)
            picked = dot_nn(hits_ref[ids_ref[k]], feats[k][...]).astype(bf16)
            slot_ref[0, pl.ds(k * capacity, capacity), :] = picked[:capacity]
            for j in range(1, picked.shape[0] // capacity):
                at = pl.ds((j - 1) * rows + k * capacity, capacity)
                later_ref[at, :] = picked[j * capacity : (j + 1) * capacity]

    @pl.when((e > 0) & (f == 0))
    def _():
        slot_ref[0] = later_ref[pl.ds(pl.multiple_of((e - 1) * rows, 16), rows), :]

    @pl.when(f == 0)
    def _():
        for k in range(count):
            at = pl.ds(k * capacity, capacity)
            hits = hits_ref[ids_ref[k], own_slots, :]
            probs = probs_ref[k]
            rank = lax.broadcasted_iota(jnp.int32, probs.shape, 0)
            gate = jnp.sum(jnp.where(rank == chosen, probs, 0.0), axis=0, keepdims=True)
            scale_ref[0, at, :] = jnp.sum(hits.astype(f32) * gate, axis=1, keepdims=True)

    slots = slot_ref[0]
    gate_w, up_w = gate_w_ref[0], up_w_ref[0]
    gate_pre = dot_nn(slots, gate_w)
    up_pre = dot_nn(slots, up_w)
    sigmoid = 1.0 / (1.0 + jnp.exp(-gate_pre))
    silu = gate_pre * sigmoid
    hidden_ref[0] = (silu * up_pre).astype(bf16)
    grad_hidden = jnp.concatenate([raw[0, 0] for raw in raws], axis=0) * scale_ref[0]
    grad_gate = (grad_hidden * up_pre * sigmoid * (1.0 + gate_pre * (1.0 - sigmoid))).astype(bf16)
    grad_up = (grad_hidden * silu).astype(bf16)
    grad_gate_ref[0] = grad_gate
    grad_up_ref[0] = grad_up
    in_term = dot_nt(grad_gate, gate_w) + dot_nt(grad_up, up_w)

    @pl.when(f == 0)
    def _():
        in_acc[...] = in_term

    @pl.when(f > 0)
    def _():
        in_acc[...] += in_term

    @pl.when(last_tile)
    def _():
        for k in range(count):
            in_all[k, own_slots, :] = in_acc[pl.ds(k * capacity, capacity), :].astype(bf16)

    @pl.when(last_tile & last_expert)
    def _():
        for k in range(count):
            feat_sums[k][...] = dot_nn(flip_ref[ids_ref[k]], in_all[k]).astype(bf16)


def run_experts(feats, ids, first_expert, grad_raw, hits, flip, router_flip, expand_weight, carried, place):
    count = len(feats)
    experts, group, capacity, _ = grad_raw.shape
    tok_rows = feats[0].shape[0]
    rows = count * capacity
    tile = F // 2
    tiles = F // tile
    first = carried is None
    whole = lambda shape: pl.BlockSpec(shape, lambda e, f, ids: (0,) * len(shape))
    once = lambda shape: pl.BlockSpec(
        shape, lambda e, f, ids: (0,) * len(shape), pipeline_mode=pl.Buffered(1)
    )
    in_specs = [once((tok_rows, D))] * count
    in_specs += [
        pl.BlockSpec((1, 1, capacity, tile), lambda e, f, ids, k=k: (e, ids[k], 0, f))
        for k in range(count)
    ]
    in_specs += [
        once(hits.shape),
        once(flip.shape),
        once(router_flip.shape),
        pl.BlockSpec((1, D, tile), lambda e, f, ids: (e, 0, f)),
        pl.BlockSpec((1, D, tile), lambda e, f, ids: (e, 0, f + tiles)),
    ]
    operands = [*feats, *[grad_raw] * count, hits, flip, router_flip, expand_weight, expand_weight]
    aliases = {}
    if not first:
        in_specs += [pl.BlockSpec(memory_space=pl.ANY)] * 5
        operands += carried
        aliases = {1 + len(operands) - 5 + k: k for k in range(5)}
    wide = pl.BlockSpec((1, rows, D), lambda e, f, ids: (e, place, 0))
    narrow = pl.BlockSpec((1, rows, tile), lambda e, f, ids: (e, place, f))
    thin = pl.BlockSpec((1, rows, 1), lambda e, f, ids: (e, place, 0))
    narrow_shape = jax.ShapeDtypeStruct((experts, group * capacity, F), bf16)
    out = pl.pallas_call(
        functools.partial(experts_kernel, count, first),
        grid_spec=pltpu.PrefetchScalarGridSpec(
            num_scalar_prefetch=1,
            grid=(experts, tiles),
            in_specs=in_specs,
            out_specs=[wide, narrow, narrow, narrow, thin] + [whole((tok_rows, D))] * count,
            scratch_shapes=[
                pltpu.VMEM((count, router_flip.shape[0], tok_rows), f32),
                pltpu.VMEM((max(experts - 1, 1) * rows, D), bf16),
                pltpu.VMEM((rows, D), f32),
                pltpu.VMEM((count, experts * capacity, D), bf16),
            ],
        ),
        out_shape=[jax.ShapeDtypeStruct((experts, group * capacity, D), bf16)]
        + [narrow_shape] * 3
        + [jax.ShapeDtypeStruct((experts, group * capacity, 1), f32)]
        + [jax.ShapeDtypeStruct((tok_rows, D), bf16)] * count,
        input_output_aliases=aliases,
        compiler_params=pltpu.CompilerParams(vmem_limit_bytes=58 * 2**20),
        cost_estimate=cost(13 + 2 * count),
        name="experts",
    )(jnp.stack([*ids, first_expert]).astype(jnp.int32), *operands)
    return out[:5], out[5:]


def combine_kernel(cores, ids_ref, slot_ref, out_ref, up_ref, hits_ref, flip_ref, scale_ref, gates_ref, grad_out_ref, *moe_refs):
    experts, _, capacity, _ = out_ref.shape
    scaled = []
    for e in range(experts):
        expert_out = out_ref[e, 0].astype(f32)
        upstream = up_ref[e, 0].astype(f32)
        scale = scale_ref[e, 0]
        dots = jnp.sum(expert_out * upstream, axis=1, keepdims=True)
        hits = hits_ref[0, e * capacity : (e + 1) * capacity, :].astype(f32)
        gates_ref[0, pl.ds(e, 1), :] = jnp.sum(hits * dots, axis=0, keepdims=True)
        grad_out_ref[e, 0] = (upstream * scale).astype(bf16)
        scaled.append((expert_out * scale).astype(bf16))
    total = dot_nn(flip_ref[0], jnp.concatenate(scaled, axis=0)).astype(bf16)
    for k in range(cores):

        @pl.when(slot_ref[2 * pl.program_id(0)] == k)
        def _():
            moe_refs[k][0] = total


def combine_experts(ids, chips, expert_out, upstream_slots, hits, flip, scale, cores):
    experts, group, capacity, _ = upstream_slots.shape
    tok_rows = hits.shape[2]
    by_place = pl.BlockSpec((experts, 1, capacity, D), lambda j, ids, at: (0, j, 0, 0))
    by_id = lambda shape: pl.BlockSpec((1,) + shape, lambda j, ids, at: (ids[j], 0, 0))
    order = []
    for distance, _ in chips:
        if distance not in order:
            order.append(distance)
    slots = []
    for j, (_, k) in enumerate(chips):
        slots += [k, 0]
    places = []
    for core in range(cores):
        mine = [(j, order.index(distance)) for j, (distance, k) in enumerate(chips) if k == core]
        for j in range(group):
            later = [place for at, place in mine if at >= j]
            places.append(later[0] if later else mine[-1][1])
    table = jnp.array(slots + places, jnp.int32)
    gates, grad_out, *sums = pl.pallas_call(
        functools.partial(combine_kernel, cores),
        grid_spec=pltpu.PrefetchScalarGridSpec(
            num_scalar_prefetch=2,
            grid=(group,),
            in_specs=[
                by_place,
                pl.BlockSpec((experts, 1, capacity, D), lambda j, ids, at: (0, ids[j], 0, 0)),
                by_id(hits.shape[1:]),
                by_id(flip.shape[1:]),
                pl.BlockSpec((experts, 1, capacity, 1), lambda j, ids, at: (0, j, 0, 0)),
            ],
            out_specs=[by_id((experts, tok_rows)), by_place]
            + [
                pl.BlockSpec(
                    (1, tok_rows, D),
                    lambda j, ids, at, k=k: (at[2 * group + k * group + j], 0, 0),
                )
                for k in range(cores)
            ],
        ),
        out_shape=[
            jax.ShapeDtypeStruct((group, experts, tok_rows), f32),
            jax.ShapeDtypeStruct((experts, group, capacity, D), bf16),
        ]
        + [jax.ShapeDtypeStruct((group // cores, tok_rows, D), bf16)] * cores,
        compiler_params=pltpu.CompilerParams(vmem_limit_bytes=40 * 2**20),
        cost_estimate=cost(18),
        name="experts_combine",
    )(
        ids,
        table,
        expert_out.reshape(experts, group, capacity, D),
        upstream_slots,
        hits,
        flip,
        scale.reshape(experts, group, capacity, 1),
    )
    return gates, grad_out, sums, order


def weight_grad_kernel(sides, added, pieces, filled, rank_ref, left_ref, *refs):
    rights, refs = refs[:sides], refs[sides:]
    more, refs = refs[:added], refs[added + filled :]
    outs, flip_ref = refs[:-1], refs[-1]
    e, m, n = pl.program_id(0), pl.program_id(1), pl.program_id(2)

    @pl.when(n == 0)
    def _():
        flip_ref[...] = left_ref[0].T

    for side in range(sides):

        @pl.when(n == side)
        def _():
            total = dot_nn(flip_ref[...], rights[side][0])
            if not added and not pieces:
                outs[0][0] = total
            for k in range(side, max(added, len(outs) if pieces else 0), sides):

                @pl.when(e * pl.num_programs(1) + m == k // sides)
                def _():
                    grown = total + more[k][...].astype(f32) if added else total
                    if pieces:
                        outs[k][...] = grown.astype(bf16)
                    else:
                        outs[0][0] = grown


def weight_grad(left, rights, rank, rows, first=0, experts=None, more=(), pieces=False, into=None):
    experts = left.shape[0] if experts is None else experts
    slots = left.shape[1]
    tile = min(512, rows)
    per = rows // tile
    width = F
    shares = [(right, j) for right in rights for j in range(right.shape[2] // width)]
    sides = len(shares)
    piece = pl.BlockSpec((tile, width), lambda e, m, n, p: (0, 0))
    if pieces:
        out_specs = [piece] * (experts * per * sides)
        out_shape = [jax.ShapeDtypeStruct((tile, width), bf16)] * (experts * per * sides)
    else:
        out_specs = [pl.BlockSpec((1, tile, width), lambda e, m, n, p: (e + first, m, n))]
        out_shape = [jax.ShapeDtypeStruct((left.shape[0], rows, sides * width), f32)]
    out = pl.pallas_call(
        functools.partial(weight_grad_kernel, sides, len(more), pieces, into is not None),
        grid_spec=pltpu.PrefetchScalarGridSpec(
            num_scalar_prefetch=1,
            grid=(experts, per, sides),
            in_specs=[
                pl.BlockSpec((1, slots, tile), lambda e, m, n, p: (e + first, 0, p[0] * per + m))
            ]
            + [
                pl.BlockSpec((1, slots, width), lambda e, m, n, p, j=j: (e + first, 0, j))
                for _, j in shares
            ]
            + [piece] * len(more)
            + [pl.BlockSpec(memory_space=pl.ANY)] * (into is not None),
            out_specs=out_specs,
            scratch_shapes=[pltpu.VMEM((tile, slots), bf16)],
        ),
        out_shape=out_shape,
        input_output_aliases={} if into is None else {2 + sides + len(more): 0},
        compiler_params=pltpu.CompilerParams(vmem_limit_bytes=48 * 2**20),
        cost_estimate=cost(experts * rows * sides / 560 * (2 if more else 1.7)),
        name="weight_gradient",
    )(
        rank.reshape(1).astype(jnp.int32), left, *[right for right, _ in shares], *more,
        *([] if into is None else [into]),
    )
    return out if pieces else out[0]


def weight_grad_sends(left, rights, rows, first, experts):
    count = lax.axis_size("dp")
    rank = lax.axis_index("dp")
    onward = [(d, (d + 1) % count) for d in range(count)]
    sent, arrived = [], []
    for e in range(first, first + experts):
        more = []
        for step in range(1, count):
            parts = weight_grad(left, rights, (rank + count - step) % count, rows, e, 1, more, True)
            more = [lax.ppermute(part, "dp", onward) for part in parts]
        sent += parts if more else []
        arrived += more
    return sent, arrived


def unturn(grad, cosine, sine_part):
    return grad * cosine - jnp.roll(grad, HD // 2, axis=1) * sine_part


def unproject_kernel(
    grad_q_ref, grad_k_ref, grad_v_ref, raw_ref, squares_ref, dots_ref, gain_ref, cosine_ref, sine_ref,
    weight_ref, grad_ref, gain_terms_ref, out_ref,
):
    rows, _, width = out_ref.shape
    inverse = lax.rsqrt(squares_ref[...] / D + norm_epsilon)
    inner = inverse * inverse * dots_ref[:2] / D

    @pl.when(pl.program_id(0) == 0)
    def _():
        gain_terms_ref[...] = jnp.zeros_like(gain_terms_ref)

    for j, part_ref in ((0, grad_q_ref), (1, grad_k_ref)):
        grad = unturn(part_ref[...], cosine_ref[...], sine_ref[...])
        column = as_column(inverse[j : j + 1])
        raw = raw_ref[:, j * HD : (j + 1) * HD]
        gain_terms_ref[pl.ds(j, 1), :] += jnp.sum(grad * raw * column, axis=0, keepdims=True)
        back = column * grad * gain_ref[j : j + 1, :] - raw * as_column(inner[j : j + 1])
        grad_ref[:, pl.ds(j * HD, HD)] = back.astype(bf16)
    grad_ref[:, pl.ds(2 * HD, HD)] = grad_v_ref[...].astype(bf16)
    for row in range(rows):
        at = pl.ds(row * width, width)
        out_ref[row] = dot_nn(grad_ref[...], weight_ref[:, at]).astype(bf16)


def unproject(grads, raw, squares, dots, gain_pair, cosine, sine_part, weight_flip, rows, cols):
    length = raw.shape[0]
    block_rows, width = length // cols, D // rows
    tile = block_rows
    tall = pl.BlockSpec((tile, HD), lambda i: (i, 0))
    three = pl.BlockSpec((tile, 3 * HD), lambda i: (i, 0))
    pair = pl.BlockSpec((2, tile), lambda i: (0, i))
    trio = pl.BlockSpec((3, tile), lambda i: (0, i))
    fixed = pl.BlockSpec((2, HD), lambda i: (0, 0))
    return pl.pallas_call(
        unproject_kernel,
        grid=(length // tile,),
        in_specs=[
            tall, tall, tall, three, pair, trio, fixed, tall, tall,
            pl.BlockSpec(weight_flip.shape, lambda i: (0, 0)),
        ],
        out_specs=[
            three, fixed, pl.BlockSpec((rows, tile, width), lambda i: (i, 0, 0)),
        ],
        out_shape=[
            jax.ShapeDtypeStruct((length, 3 * HD), bf16),
            jax.ShapeDtypeStruct((2, HD), f32),
            jax.ShapeDtypeStruct((rows * cols, block_rows, width), bf16),
        ],
        compiler_params=pltpu.CompilerParams(vmem_limit_bytes=52 * 2**20),
        cost_estimate=cost(15.5),
        name="projection_backward",
    )(*grads, raw, squares, dots, gain_pair, cosine, sine_part, weight_flip)


def norm_back(values, inverse, gain_row, upstream, dot_total):
    scaled = upstream * gain_row
    return inverse[:, None] * scaled - values * (inverse**3 * dot_total / D)[:, None]


def dot(a, b):
    return jnp.dot(a, b, preferred_element_type=f32)


def einsum(spec, a, b):
    return jnp.einsum(spec, a, b, preferred_element_type=f32)


def on_device(
    layer_input,
    gains,
    qkv_weight,
    output_weight,
    router_weight,
    expand_weight,
    reduce_weight,
    routes,
    drop_order,
    prefix_len,
    cotangent,
):
    row_rank, col_rank = lax.axis_index("row"), lax.axis_index("col")
    rows, cols = lax.axis_size("row"), lax.axis_size("col")
    dp_count = lax.axis_size("dp")
    group = rows * cols
    res_rows, row_width = layer_input.shape
    col_width = qkv_weight.shape[2]
    seq_len = res_rows * cols
    tok_rows = res_rows // rows
    block_rank = col_rank * rows + row_rank
    expert_rank = row_rank * cols + col_rank
    expert_count = router_weight.shape[1]
    local_experts = expand_weight.shape[0]
    capacity = tok_rows * TOP // expert_count
    ring = Ring(rows, cols)
    gain_rows = gains.astype(f32)
    router_flip = router_weight.T

    paired = dp_count % 2 == 0
    half_rank = lax.axis_index("dp") % 2 if paired else 0
    partner = [(d, d ^ 1) for d in range(dp_count)]
    halves = 2 if paired else 1
    half_rows = row_width // halves
    head_half = lax.dynamic_slice_in_dim(qkv_weight, half_rank * half_rows, half_rows, 0)
    head_half = head_half.reshape(half_rows, 3, rows, HD).transpose(2, 1, 0, 3)
    head_out = output_weight.reshape(rows, HD, row_width // HD, HD).transpose(0, 2, 1, 3)
    head_half = jnp.concatenate(
        [head_half.reshape(rows, 3 * half_rows, HD), head_out.reshape(rows, row_width, HD)], axis=1
    )
    head_half = exchange(head_half, "row")
    head_out = head_half[:, 3 * half_rows :].reshape(D, HD).reshape(D // HD, HD, HD)
    head_out = head_out.transpose(0, 2, 1).reshape(D, HD)
    head_half = head_half[:, : 3 * half_rows].reshape(rows, 3, half_rows, HD)
    head_half = head_half.transpose(0, 2, 1, 3).reshape(rows, half_rows, 3 * HD)
    half_width = HD // 2
    frequency = rope_base ** (-2.0 * jnp.arange(half_width, dtype=f32) / HD)
    angles = jnp.arange(seq_len).astype(f32)[:, None] * frequency[None, :]
    cosine, sine_part = jnp.cos(angles), jnp.sin(angles)
    cosine = jnp.concatenate([cosine, cosine], axis=1)
    sine_part = jnp.concatenate([-sine_part, sine_part], axis=1)
    own_lines = jnp.concatenate([routes.T, drop_order[None, :]], axis=0)
    lines = jnp.zeros((cols,) + own_lines.shape, jnp.int32)
    lines = lax.dynamic_update_slice(lines, own_lines[None], (col_rank, 0, 0))
    for step in range(1, cols):
        arrived = lax.ppermute(own_lines, "col", [(c, (c + step) % cols) for c in range(cols)])
        lines = lax.dynamic_update_slice(
            lines, arrived[None], ((col_rank + cols - step) % cols, 0, 0)
        )
    first_expert = expert_rank * local_experts
    own_experts = first_expert + jnp.arange(local_experts)
    member = jnp.any(lines[None, :, :TOP] == own_experts[:, None, None, None], axis=2)
    member = member.reshape(local_experts, group, tok_rows).transpose(1, 0, 2)
    drop_rank = lines[:, TOP].reshape(group, tok_rows)
    token_index = jnp.arange(tok_rows)
    earlier = (drop_rank[:, None, :] < drop_rank[:, :, None]) | (
        drop_rank[:, None, :] == drop_rank[:, :, None]
    ) & (token_index[None, None, :] < token_index[None, :, None])
    position = jnp.sum(jnp.where(earlier[:, None] & member[:, :, None, :], 1, 0), axis=-1)
    kept = member & (position < capacity)
    hits = kept[:, :, None, :] & (
        position[:, :, None, :] == jnp.arange(capacity)[None, None, :, None]
    )
    hits = hits.reshape(group, local_experts * capacity, tok_rows)
    dispatch = hits.astype(bf16)
    combine = hits.transpose(0, 2, 1).astype(bf16)

    weight_half = lax.dynamic_slice_in_dim(
        output_weight, half_rank * (col_width // 2), col_width // halves, 0
    )
    at = [col_rank, row_rank]
    for chip_group in range(ring.groups):
        for half in range(2):
            for k in range(ring.cores):
                col = chip_group * ring.cores + (ring.core + k) % ring.cores
                at.append((col * 2 + (half_rank + half) % 2) * (rows // 2))
    at = jnp.stack([jnp.asarray(value, jnp.int32) for value in at])

    x_steps = ring.gather_steps(jnp.concatenate([layer_input, weight_half], axis=0))
    x_blocks = unwritten((group, res_rows + weight_half.shape[0], row_width), bf16)
    x_blocks = ring.place_blocks(x_blocks, ring.with_siblings(next(x_steps)))
    pieces = other_half = None
    for step in range(ring.size // 2):
        arrival = x_steps.send(pieces)
        pieces = [piece for piece, _ in arrival]
        if step == 0:
            pieces, cosine, sine_part = together(pieces, cosine, sine_part)
        elif step == 1:
            pieces, head_half, x_blocks, dispatch, combine = together(
                pieces, head_half, x_blocks, dispatch, combine
            )
            other_half = lax.ppermute(head_half, "dp", partner) if paired else None
        elif step == 2:
            pieces, x_blocks = together(pieces, x_blocks)
        else:
            pieces, x_blocks, other_half = together(pieces, x_blocks, other_half)
        arrival = list(zip(pieces, [distance for _, distance in arrival]))
        x_blocks = ring.place_blocks(x_blocks, ring.with_siblings(arrival))
    if paired:
        head_weight = jnp.where(
            half_rank == 0,
            jnp.stack([head_half, other_half], axis=1),
            jnp.stack([other_half, head_half], axis=1),
        )
    else:
        head_weight = head_half
    head_weight = head_weight.reshape(D, 3 * HD)
    weight_flip = head_weight.T
    half_place = res_rows // (col_width // 2)
    table = []
    for half in range(2):
        for k in range(ring.cores):
            for chip_group in range(ring.groups):
                col = chip_group * ring.cores + (ring.core + k) % ring.cores
                for row in range(rows):
                    whole_plane = half == 0 or not paired
                    table.append(col * rows + row if whole_plane else chip_group * rows + row)
    table = jnp.stack([jnp.asarray(value, jnp.int32) for value in table])
    if paired:
        own_core = x_blocks[:, res_rows:].reshape(
            ring.groups, ring.cores, rows, weight_half.shape[0], row_width
        )
        own_core = lax.dynamic_index_in_dim(own_core, ring.core, 1, False)
        own_core = own_core.reshape(ring.size, weight_half.shape[0], row_width)
        theirs = lax.ppermute(own_core, "dp", partner)
    upstream_blocks = lax.all_gather(after(cotangent, pieces), BLOCKS, axis=0)
    projected, inv_first, square_terms = project(x_blocks, res_rows, gain_rows[0:1], head_weight, rows)
    squares = ring.small_sum(square_terms)

    head_first = block_rank * HD
    gain_pair = lax.dynamic_slice(gain_rows, (1, head_first), (2, HD))
    query_low, key_low, value_low, key_flip, value_flip = turn(
        projected, squares, gain_pair, cosine, sine_part
    )

    query_rows = max(seq_len // 6, 128)
    attn_head, lse = attention(query_low, key_low, value_flip, prefix_len, 2 * query_rows)
    attn_tokens = exchange(attn_head.reshape(group, tok_rows, HD), BLOCKS)
    weight_sets = [(x_blocks, half_place)] * ring.cores
    if paired:
        attn_tokens, theirs = together(attn_tokens, theirs)
        weight_sets += [(block, 0) for block in ring.from_siblings(theirs)]
    else:
        weight_sets += [(x_blocks, half_place + 1)] * ring.cores
    upstream_slots = dispatch_blocks(dispatch, upstream_blocks, rows, local_experts)
    residual, second_low = output_branch(
        at, table, attn_tokens, weight_sets, x_blocks, gain_rows[3:4], rows, ring.groups
    )
    feat_steps = ring.gather_steps(second_low)
    grad_raw = einsum(
        "end,efd->enf", upstream_slots.reshape(local_experts, group * capacity, D), reduce_weight
    ).reshape(local_experts, group, capacity, F)

    carried = None
    waiting = [
        (block, ident, 0, k)
        for k, (block, ident) in enumerate(ring.with_siblings(next(feat_steps)))
    ]
    calls = {1: 0, ring.size // 2 - 1: 1}
    feat_sums, taken_by = {}, {}
    pieces = None
    for step in range(ring.size // 2):
        arrival = feat_steps.send(pieces)
        pieces = [piece for piece, _ in arrival]
        if step == 0:
            pieces, upstream_slots = together(pieces, upstream_slots)
        elif step == 1:
            pieces, grad_raw = together(pieces, grad_raw)
        elif step == 2:
            pieces, *carried = together(pieces, *carried)
        direct, later = [], []
        for piece, (_, distance) in zip(pieces, arrival):
            for k, (block, ident) in enumerate(ring.with_siblings([(piece, distance)])):
                (later if k else direct).append((block, ident, distance, k))
        waiting += direct
        if step not in calls:
            waiting += later
            continue
        taken, waiting = (waiting, later) if step == 1 else (waiting + later, [])
        carried, sums = run_experts(
            [block for block, *_ in taken],
            [ident for _, ident, *_ in taken],
            first_expert,
            grad_raw,
            dispatch,
            combine,
            router_flip,
            expand_weight,
            carried,
            calls[step],
        )
        for (_, ident, distance, k), total in zip(taken, sums):
            feat_sums[distance, k] = total
        taken_by[calls[step] * len(taken)] = [item[1:] for item in taken]
    by_slot = [item for start in sorted(taken_by) for item in taken_by[start]]
    places = [ident for ident, _, _ in by_slot]
    chips = [(distance, k) for _, distance, k in by_slot]
    feat_parts = {}

    def feat_part(distance):
        if distance not in feat_parts:
            others = ring.for_siblings(*[feat_sums[distance, k] for k in range(1, ring.cores)])
            feat_parts[distance] = [(block, 0) for block in (feat_sums[distance, 0], *others)]
        return feat_parts[distance]

    slot_rows, hidden, grad_gate_pre, grad_up_pre, slot_gate = carried

    arriving, arrived = [], []

    def taking(count, *values):
        taken, arriving[:count] = arriving[:count], []
        *values, taken = together(*values, taken)
        arrived.extend(taken)
        return values

    def ahead_tie(scatter, parts, *values):
        steps = [scatter.step, -scatter.step] if scatter.step else []
        terms = {step: scatter.parts(step) for step in steps}
        blocks = [[block for block, _ in terms[step] if block.ndim == 2] for step in steps]
        *values, blocks = scatter.tie(*values, blocks)
        for step, given in zip(steps, blocks):
            given = iter(given)
            parts[step] = [
                (next(given), 0) if block.ndim == 2 else (block, place) for block, place in terms[step]
            ]
        return values

    grads = ring.scatter(feat_part)
    grads.ready()
    expand_sides = [grad_gate_pre, grad_up_pre]
    expand_rows, reduce_rows = D // dp_count, F // dp_count
    half = local_experts // 2
    slot_rows, = grads.tie(slot_rows)
    grads.move()
    sent, pieces = weight_grad_sends(slot_rows, expand_sides, expand_rows, 0, half)
    arriving += pieces
    sent, = ahead_tie(grads, feat_parts, sent)
    grads.ready()
    slot_rows, hidden = grads.tie(slot_rows, hidden)
    grads.move()
    expert_out = einsum("enf,efd->end", hidden, reduce_weight).astype(bf16)
    expert_out, = taking(1, *ahead_tie(grads, feat_parts, expert_out))
    grads.ready()
    expert_out, = grads.tie(expert_out)
    grads.move()
    ids = jnp.stack(places).astype(jnp.int32)
    gate_tokens, grad_out_slots, moe_sums, moe_order = combine_experts(
        ids, chips, expert_out, upstream_slots, dispatch, combine, slot_gate, ring.cores
    )
    grad_out_slots = grad_out_slots.reshape(local_experts, group * capacity, D)
    grad_out_slots, moe_sums, gate_tokens = taking(
        1, *ahead_tie(grads, feat_parts, grad_out_slots, moe_sums, gate_tokens)
    )
    grads.ready()
    moe_sums, gate_tokens, slot_rows = grads.tie(moe_sums, gate_tokens, slot_rows)
    grads.move()
    grad_probs = exchange(gate_tokens, BLOCKS)
    sent, pieces = weight_grad_sends(
        slot_rows, expand_sides, expand_rows, half, local_experts - half
    )
    arriving += pieces
    expand_count = len(arrived) + len(arriving)
    moe_others = [lax.ppermute(other, PLANE, ring.sibling) for other in moe_sums[1:]]

    def moe_part(distance):
        place = moe_order.index(distance)
        return [(array, place) for array in (moe_sums[0], *moe_others)]

    grad_probs = grad_probs.reshape(cols, rows, local_experts, tok_rows)
    grad_probs = grad_probs.transpose(1, 0, 2, 3).reshape(expert_count, tok_rows)
    logits = dot_nt(router_flip, second_low)
    probs = jax.nn.softmax(logits, axis=0)
    grad_logits = probs * (grad_probs - jnp.sum(probs * grad_probs, axis=0, keepdims=True))
    grad_logits = grad_logits.T.astype(bf16)
    router_term = einsum("te,td->ed", grad_logits, second_low)
    grad_logits, router_term, moe_others, sent = taking(
        1, *grads.tie(grad_logits, router_term, moe_others, sent)
    )
    moes = ring.scatter(moe_part)
    moes.ready()
    grad_terms = grads.total()

    grad_branch, gain_second_term = residual_back(
        at[:2], grad_terms, grad_logits, router_flip, residual, upstream_blocks, gain_rows[3:4], rows
    )
    branch_steps = ring.gather_steps(grad_branch)
    branch_all = unwritten((group, tok_rows, D), bf16)
    branch_all = ring.place_blocks(branch_all, ring.with_siblings(next(branch_steps)))
    rank = lax.axis_index("dp")
    expand_grad = None
    extra = []
    pieces = None
    for step in range(ring.size // 2):
        arrival = branch_steps.send(pieces)
        if step == ring.size // 2 - 1:
            moes.move()
        pieces, branch_all, extra, moes.going = taking(
            1,
            [piece for piece, _ in arrival],
            branch_all,
            extra,
            moes.going,
        )
        if step == 0:
            left, = together(hidden, pieces)[:1]
            extra, parts = weight_grad_sends(
                left, [grad_out_slots], reduce_rows, 0, local_experts
            )
            arriving += parts
        elif step == 2:
            expand_grad, = extra
        elif step == 1:
            left, = together(slot_rows, pieces)[:1]
            expand_grad = weight_grad(
                left, expand_sides, rank, expand_rows, 0, half, arrived[: expand_count // 2]
            )
            extra = [expand_grad]
        else:
            expand_grad, = extra
        arrival = list(zip(pieces, [distance for _, distance in arrival]))
        branch_all = ring.place_blocks(branch_all, ring.with_siblings(arrival))

    moes.ready()
    branch_all, = moes.tie(branch_all)
    moes.move()
    grad_attn = dot(branch_all.reshape(seq_len, D), head_out).astype(bf16)
    centre = jnp.sum(attn_head.astype(f32) * grad_attn.astype(f32), axis=1)[None]
    grad_query, dot_query, grad_key, grad_value, dot_key, dot_value = attention_back(
        query_low, key_low, key_flip, value_low, grad_attn, lse, centre, prefix_len, query_rows
    )
    head_grads = [grad_query, grad_key, grad_value]
    dots = jnp.concatenate([dot_query, dot_key, dot_value], axis=0)
    dots, = taking(1, *moes.tie(dots))
    moes.ready()
    dots, = moes.tie(dots)
    dots = ring.small_sum(dots)
    dots, = moes.tie(dots)
    moes.move()

    grad_qkv, gain_pair_terms, grad_first_blocks = unproject(
        head_grads, projected, squares, dots, gain_pair, cosine, sine_part, weight_flip, rows, cols
    )

    def first_part(distance):
        if distance not in first_parts:
            mine, *others = ring.block_ids(distance)
            others = ring.for_siblings(
                *[lax.dynamic_index_in_dim(grad_first_blocks, k, 0, False) for k in others]
            )
            first_parts[distance] = [(grad_first_blocks, mine)] + [(block, 0) for block in others]
        return first_parts[distance]

    first_parts = {}
    grad_first_blocks, grad_qkv = taking(2, *moes.tie(grad_first_blocks, grad_qkv))
    first_far = block_sum(first_part(ring.size // 2))
    moes.ready()
    first_far, grad_first_blocks = moes.tie(first_far, grad_first_blocks)
    first_parts = {ring.size // 2: [(first_far, 0)]}
    firsts = ring.scatter(first_part)
    firsts.ready()
    firsts.move()
    moes.move()
    output_term = dot(attn_head.T, branch_all.reshape(seq_len, D))
    output_term = output_term.astype(bf16).reshape(HD, rows, row_width).transpose(1, 0, 2)
    output_term, = taking(1, *ahead_tie(firsts, first_parts, output_term))
    firsts.ready()
    grad_qkv, slot_rows = firsts.tie(grad_qkv, slot_rows)
    firsts.move()
    qkv_term, gain_first_term = project_weight(
        x_blocks, res_rows, gain_rows[0:1], inv_first, grad_qkv, head_weight, rows
    )
    qkv_rows = row_width // dp_count
    qkv_sum = dp_sum(
        lambda rank: lax.dynamic_slice_in_dim(qkv_term, rank * qkv_rows, qkv_rows, 2)
    )
    output_sum = exchange(output_term, "row").reshape(col_width, row_width)
    qkv_term, = taking(1, *moes.tie(*ahead_tie(firsts, first_parts, qkv_term)))
    moe_terms = moes.total()
    firsts.ready()
    slot_rows, = firsts.tie(slot_rows)
    firsts.move()
    expand_grad = weight_grad(
        slot_rows, expand_sides, rank, expand_rows, half, local_experts - half,
        arrived[expand_count // 2 : expand_count], into=expand_grad,
    )
    layer_tokens = residual
    for term in moe_terms:
        layer_tokens = layer_tokens + term.astype(f32)
    layer_tokens = layer_tokens.astype(bf16)
    layer_output = lax.all_to_all(layer_tokens, "row", split_axis=1, concat_axis=0, tiled=True)
    expand_grad, output_sum = taking(
        len(arriving), *ahead_tie(firsts, first_parts, expand_grad, output_sum)
    )
    firsts.ready()
    hidden, = firsts.tie(hidden)
    firsts.move()
    reduce_grad = weight_grad(
        hidden, [grad_out_slots], rank, reduce_rows, more=arrived[expand_count:]
    )
    qkv_grad = exchange(qkv_sum.astype(bf16), "row")
    reduce_grad, layer_output, qkv_grad = firsts.tie(reduce_grad, layer_output, qkv_grad)
    grad_first = firsts.total()
    grad_first = sum(term.astype(f32) for term in grad_first)
    grad_block = lax.dynamic_slice(
        branch_all, (col_rank * rows, 0, row_rank * row_width), (rows, tok_rows, row_width)
    ).reshape(res_rows, row_width)
    inverse = lax.rsqrt(squares / D + norm_epsilon)
    dot_first = dots[2] + norm_epsilon * jnp.sum(dots[:2] * inverse, axis=0)
    dot_first = dot_first / inv_first[0]
    own_first = col_rank * res_rows
    dot_first = lax.dynamic_slice_in_dim(dot_first, own_first, res_rows)
    inv_block = lax.dynamic_slice_in_dim(inv_first[0], own_first, res_rows)
    gain_block = lax.dynamic_slice_in_dim(gain_rows[0], row_rank * row_width, row_width)
    input_grad = grad_block.astype(f32) + norm_back(
        layer_input.astype(f32), inv_block, gain_block, grad_first, dot_first
    )

    output_rows = col_width // dp_count
    output_grad = dp_sum(
        lambda rank: lax.dynamic_slice_in_dim(
            output_sum, rank * output_rows, output_rows, 0
        ).astype(f32)
    )
    qkv_grad = qkv_grad.transpose(2, 1, 0, 3).reshape(1, qkv_rows, 3, col_width).astype(f32)

    def placed(term):
        return lax.dynamic_update_slice(jnp.zeros((D,), f32), term, (head_first,))

    gain_terms = jnp.concatenate(
        [
            gain_first_term,
            jnp.stack([placed(gain_pair_terms[0]), placed(gain_pair_terms[1])]),
            gain_second_term,
        ],
        axis=0,
    )
    gain_total = jnp.sum(lax.all_gather(gain_terms, ("dp", "row", "col"), axis=0), axis=0)
    router_all = lax.all_gather(router_term.astype(bf16), ("dp", "row", "col"), axis=0)
    router_total = jnp.sum(router_all.astype(f32), axis=0).T
    return (
        layer_output,
        input_grad.astype(bf16),
        gain_total,
        qkv_grad,
        output_grad[None],
        router_total,
        expand_grad,
        reduce_grad,
    )


def solution(mesh):
    return jax.shard_map(
        on_device,
        mesh=mesh,
        in_specs=(
            P(("dp", "col"), "row"),
            P(),
            P("row", None, "col"),
            P("col", "row"),
            P(),
            P(("row", "col"), None, None),
            P(("row", "col"), None, None),
            P(("dp", "col"), None),
            P(("dp", "col")),
            P("dp"),
            P(("dp", "col"), "row"),
        ),
        out_specs=(
            P(("dp", "col"), "row"),
            P(("dp", "col"), "row"),
            P(),
            P("row", "dp", None, "col"),
            P("col", "dp", "row"),
            P(),
            P(("row", "col"), "dp", None),
            P(("row", "col"), "dp", None),
        ),
        check_vma=False,
    )
```
